32 devices in a mesh: gx: 4 (over z), gy: 2 (over x), gz: 4 (over y, core).
Axes of the slice: x: 2, y: 2, z: 4, core: 2. Of those that a mesh axis runs over, the one named last changes fastest.
Arguments:
- eigvecs: bfloat16 [8, 8, 16, 2, 3, 256], P('gx', 'gy', 'gz'), may hold values from -6 to 6
- links: float32 [8, 8, 16, 3, 2, 3, 3], P('gx', 'gy', 'gz'), may hold values from -6 to 6
- directions: int32 [4], replicated, may hold values from 0 to 2
- spin_mats: float32 [4, 4, 4], replicated, may hold values from -6 to 6
- forward_peram: bfloat16 [2, 1024, 1024], P(None, 'gx', 'gy'), may hold values from -0.1875 to 0.1875
- backward_peram: bfloat16 [2, 1024, 1024], P(None, 'gx', 'gy'), may hold values from -0.1875 to 0.1875
- chain_order: int32 [16, 2], P('gz'), may hold values from 0 to 3
Outputs:
- operators: bfloat16 [16, 2, 1024, 1024], P('gz', None, 'gx', 'gy')
The draws below stay inside these ranges and needn't reach their ends.
All inputs are finite; a program needn't handle non-finite values.
Results may differ from the reference program's by a relative error of at most 0.012.
Values may be sent and summed in bfloat16 or wider, within the bound.
No kernel may reach another device: no remote copies, remote signals or barrier semaphores. Data moves between devices by JAX's collectives and lax.ppermute only.
A program may use at most 192 MiB of HBM per device.

```python
import math
import jax
import jax.numpy as jnp
from jax import lax

NV = 256
NB = 1024
OPS = 16
NX = 8
NY = 8
NZ = 16


def touch_ends(drawn, key, low, high):
    longest = drawn.shape.index(max(drawn.shape))
    spots = []
    for shift in (0, 1):
        where = [jax.random.randint(jax.random.fold_in(key, axis), (), 0, length) for axis, length in enumerate(drawn.shape)]
        where[longest] = (where[longest] + shift) % drawn.shape[longest]
        spots.append(tuple(where))
    return drawn.at[spots[0]].set(low).at[spots[1]].set(high)


def block_scale(own_key, extent, cuts, smallest, top_value):
    def one(axis_at, shards_of):
        draws = jax.random.uniform(jax.random.fold_in(jax.random.fold_in(own_key, 6), axis_at), (shards_of,), jnp.float32, smallest / len(cuts), top_value / len(cuts))
        return jnp.repeat(jnp.exp(draws), extent[axis_at] // shards_of).reshape((-1,) + (1,) * (len(extent) - axis_at - 1))

    level = one(*cuts[0])
    for cut in cuts[1:]:
        level = level * one(*cut)
    return level


def bell_draw(key, extent, scale, reach, cuts=(), held_as=jnp.bfloat16):
    entries = jax.random.normal(key, extent, jnp.float32) * scale
    if len(cuts) > 0:
        entries = block_scale(key, extent, cuts, -0.22, 0.18) * entries
    return jnp.clip(entries, min=-reach, max=reach).astype(held_as)


def setup_inputs(seed: int = 0) -> dict:
    key_of = jax.random.split(jax.random.key(seed), 8)
    return {
        "eigvecs": bell_draw(key_of[0], (NX, NY, NZ, 2, 3, NV), 1.0, 6.0, ((0, 4), (1, 2), (2, 4))),
        "links": bell_draw(key_of[1], (NX, NY, NZ, 3, 2, 3, 3), 0.408, 6.0, ((0, 4), (1, 2), (2, 4)), jnp.float32),
        "directions": touch_ends(jax.random.randint(key_of[2], (4,), 0, 3), jax.random.fold_in(key_of[2], 1), 0, 2).astype(jnp.int32),
        "spin_mats": bell_draw(key_of[3], (4, 4, 4), 0.5, 6.0, (), jnp.float32),
        "forward_peram": bell_draw(key_of[4], (2, NB, NB), NB ** -0.5, 0.1875, ((1, 4), (2, 2))),
        "backward_peram": bell_draw(key_of[5], (2, NB, NB), NB ** -0.5, 0.1875, ((1, 4), (2, 2))),
        "chain_order": touch_ends(jax.random.randint(key_of[6], (OPS, 2), 0, 4), jax.random.fold_in(key_of[6], 1), 0, 3).astype(jnp.int32),
    }


def transport(link_dir, shifted):
    highest = lax.Precision.HIGHEST
    real_v = shifted[..., 0, :, :].astype(jnp.float32)
    imag_v = shifted[..., 1, :, :].astype(jnp.float32)
    real_u = link_dir[..., 0, :, :]
    imag_u = link_dir[..., 1, :, :]

    def apply_link(matrix, vector):
        return jnp.einsum('...ab,...bn->...an', matrix, vector, precision=highest)
    moved_re = apply_link(real_u, real_v) - apply_link(imag_u, imag_v)
    moved_im = apply_link(real_u, imag_v) + apply_link(imag_u, real_v)
    moved = jnp.stack([moved_re, moved_im], axis=-3).astype(jnp.bfloat16)
    turned = jnp.stack([moved_im, -moved_re], axis=-3).astype(jnp.bfloat16)
    return (moved, turned)

def correlation(vec_part, moved, turned):
    width = vec_part.shape[-1]
    left_side = vec_part.reshape(-1, width)
    right_side = jnp.concatenate([moved.reshape(-1, width), turned.reshape(-1, width)], axis=1)
    product = lax.dot_general(left_side, right_side, (((0,), (0,)), ((), ())), preferred_element_type=jnp.float32)
    return jnp.stack([product[:, :width], product[:, width:]])

def complex_product(left_mat, right_mat):
    row_count = left_mat.shape[1]
    stacked = left_mat.reshape(2 * row_count, left_mat.shape[2])
    first_half = jnp.dot(stacked, right_mat[0], preferred_element_type=jnp.float32)
    second_half = jnp.dot(stacked, right_mat[1], preferred_element_type=jnp.float32)
    return jnp.stack([first_half[:row_count] - second_half[row_count:], second_half[:row_count] + first_half[row_count:]])

def reference(eigvecs, links, directions, spin_mats, forward_peram, backward_peram, chain_order):
    highest = lax.Precision.HIGHEST

    def plane_terms(plane_index, total):
        plane = lax.dynamic_index_in_dim(eigvecs, plane_index, 0, keepdims=False)
        after = lax.dynamic_index_in_dim(eigvecs, (plane_index + 1) % NX, 0, keepdims=False)
        link_plane = lax.dynamic_index_in_dim(links, plane_index, 0, keepdims=False)
        shifted = [after, jnp.roll(plane, -1, axis=0), jnp.roll(plane, -1, axis=1)]
        terms = []
        for direction in range(3):
            moved, turned = transport(link_plane[:, :, direction], shifted[direction])
            terms.append(correlation(plane, moved, turned))
        return total + jnp.stack(terms)
    elem_dir = lax.fori_loop(0, NX, plane_terms, jnp.zeros((3, 2, NV, NV), jnp.float32))
    elem_dir = elem_dir * (1.0 / math.sqrt(12.0 * NX * NY * NZ))
    chooser = (directions[:, None] == jnp.arange(3, dtype=jnp.int32)[None, :]).astype(jnp.float32)
    elementals = jnp.einsum('ke,ecij->kcij', chooser, elem_dir, precision=highest)
    spin_elem = jnp.einsum('kcij,kst->kcisjt', elementals, spin_mats, precision=highest)
    spin_elem = spin_elem.reshape(4, 2, NB, NB).astype(jnp.bfloat16)
    inverse = 1.0 / math.sqrt(NB)

    def one_operator(pair):
        left_elem = lax.dynamic_index_in_dim(spin_elem, pair[0], 0, keepdims=False)
        right_elem = lax.dynamic_index_in_dim(spin_elem, pair[1], 0, keepdims=False)
        first = complex_product(forward_peram, right_elem).astype(jnp.bfloat16)
        second = (complex_product(left_elem, first) * inverse).astype(jnp.bfloat16)
        return complex_product(second, backward_peram).astype(jnp.bfloat16)
    return lax.map(one_operator, chain_order)
```

```python
import functools
import math

import jax
import jax.numpy as jnp
import numpy as np
from jax import lax
from jax.experimental import pallas as pl
from jax.experimental.pallas import tpu as pltpu
from jax.sharding import PartitionSpec as P

VMEM = pl.BlockSpec(memory_space=pltpu.VMEM)
SMEM = pl.BlockSpec(memory_space=pltpu.SMEM)
BF16 = jnp.bfloat16
F32 = jnp.float32


def passed_along(value, axis, steps):
    count = lax.axis_size(axis)
    pairs = [(source, (source + steps) % count) for source in range(count)]
    return lax.ppermute(value, axis, pairs)


def mm(left, right):
    return jnp.dot(left, right, preferred_element_type=F32)


def site_tables(extent):
    sites = [(a, b, c) for a in range(extent[0]) for b in range(extent[1]) for c in range(extent[2])]
    count = len(sites)
    where = {site: n for n, site in enumerate(sites)}
    rows = [(c, n, a) for c in range(2) for n in range(count) for a in range(3)]
    spread = np.zeros((len(rows), count), np.float32)
    for r, (c, n, a) in enumerate(rows):
        spread[r, n] = 1
    tables = []
    for e in range(3):
        face = [s for s in sites if s[e] == 0]
        inner = sites if e else [s for s in sites if s[0] > 0]
        columns = [(c, s, b) for c in range(2) for s in inner for b in range(3)]
        beyond = [tuple(v + extent[e] * (d == e) for d, v in enumerate(s)) for s in face]
        columns += [(c, s, b) for c in range(2) for s in beyond for b in range(3)]
        mask = np.zeros((len(rows), len(columns)), np.float32)
        keep = np.zeros((len(rows), 108), np.float32)
        place = np.zeros((108, len(columns)), np.float32)
        by_site = {}
        for q, (cc, s, b) in enumerate(columns):
            by_site.setdefault(s, []).append(q)
            place[cc * 9 + b, q] = -1 if cc else 1
            place[54 + (1 - cc) * 9 + b, q] = 1
        full = np.zeros((108, len(columns)), np.float32)
        for c in range(2):
            for cc in range(2):
                for a in range(3):
                    for b in range(3):
                        full[c * 54 + e * 18 + cc * 9 + a * 3 + b] = place[c * 54 + cc * 9 + b]
        for r, (c, n, a) in enumerate(rows):
            s = sites[n]
            mask[r, by_site[tuple(v + (d == e) for d, v in enumerate(s))]] = 1
            for cc in range(2):
                for b in range(3):
                    keep[r, c * 54 + e * 18 + cc * 9 + a * 3 + b] = 1
        tables.append((mask, keep, full))
    return spread, tables


def prepare_kernel(z_ref, link_ref, fwd_ref, bwd_ref, perm_ref, spread_ref, *refs):
    masks, keeps, places = refs[0:3], refs[3:6], refs[6:9]
    fwd_out, bwd_out = refs[9:11]
    link_outs = refs[11:14]
    z = z_ref[0]
    rows = fwd_ref.shape[1]
    piece = fwd_out.shape[1]
    per_spin = rows // 4
    flat = lax.broadcasted_iota(jnp.int32, (piece, rows), 0) + z * piece
    spin = jnp.zeros_like(flat)
    for t in range(1, 4):
        spin += jnp.where(flat >= t * per_spin, 1, 0)
    source = 4 * (flat - spin * per_spin) + spin
    select = jnp.where(lax.broadcasted_iota(jnp.int32, (piece, rows), 1) == source, 1.0, 0.0)
    select = select.astype(BF16)
    for c in range(2):
        picked = mm(select, fwd_ref[c]).astype(BF16)
        fwd_out[c] = mm(picked, perm_ref[...]).astype(BF16)
        bwd_out[c] = mm(select, bwd_ref[c]).astype(BF16)
    link = link_ref[...]
    high = link.astype(BF16)
    rest = link - high.astype(F32)
    mid = rest.astype(BF16)
    low = (rest - mid.astype(F32)).astype(BF16)
    spread = spread_ref[...]
    by_row = [mm(spread, part) for part in (high, mid, low)]
    for e in range(3):
        keep = keeps[e][...].astype(F32)
        picked = jnp.concatenate(
            [jnp.concatenate([part, part], axis=1) * keep for part in by_row], axis=0
        ).astype(BF16)
        placed = mm(picked, places[e][...])
        mask = masks[e][...].astype(F32)
        mask = jnp.concatenate([mask, mask, mask], axis=0)
        link_outs[e][...] = (placed * mask).astype(BF16)


def correlate_kernel(scale, vec_ref, face0, face1, face2, mat0, mat1, mat2, out_ref):
    vec = vec_ref[...]
    rows = vec.shape[0]
    half = rows // 2
    width = vec.shape[1]
    lower = half - face0.shape[0] // 2
    sources = [
        jnp.concatenate([vec[half - lower : half], vec[rows - lower :], face0[...]], axis=0),
        jnp.concatenate([vec, face1[...]], axis=0),
        jnp.concatenate([vec, face2[...]], axis=0),
    ]
    for e, mat in enumerate((mat0, mat1, mat2)):
        terms = mm(mat[...], sources[e])
        moved = terms[:rows] + terms[rows : 2 * rows] + terms[2 * rows :]
        moved = moved.astype(BF16)
        turned = jnp.concatenate([moved[half:], -moved[:half]], axis=0)
        right = jnp.concatenate([moved, turned], axis=1)
        product = lax.dot_general(
            vec, right, (((0,), (0,)), ((), ())), preferred_element_type=F32
        )
        product = (product * scale).astype(BF16)
        out_ref[2 * e] = product[:, :width]
        out_ref[2 * e + 1] = product[:, width:]


def chain_kernel(
    inverse, gx_ref, dirs_ref, spin_ref, chain_ref, elem_ref, fwd_ref, bwd_ref, out_ref, x_ref, p_ref, q_ref, b_ref
):
    num_vecs = elem_ref.shape[2]
    gx_n, gy_n, gz_n, _, _, width = fwd_ref.shape
    op_count = out_ref.shape[0]
    row_count = out_ref.shape[2]
    vec_rows = row_count // 4
    spin_pieces = gz_n // 4
    lane = width // 4
    first_row = pl.multiple_of(gx_ref[0] * vec_rows, vec_rows)

    def own(d, c):
        return elem_ref[d, c, pl.ds(first_row, vec_rows), :]

    real_rows = [jnp.concatenate([own(d, 0), -own(d, 1)], axis=1) for d in range(3)]
    imag_rows = [jnp.concatenate([own(d, 1), own(d, 0)], axis=1) for d in range(3)]
    left = jnp.concatenate([part for d in range(3) for part in (real_rows[d], imag_rows[d])], axis=0)
    for t in range(4):
        planes = slice(t * spin_pieces, (t + 1) * spin_pieces)
        for block in range(gy_n):
            right = jnp.concatenate(
                [fwd_ref[:, block, planes, c].reshape(num_vecs, width) for c in range(2)], axis=0
            )
            result = mm(left, right).astype(BF16)
            for d in range(3):
                for c in range(2):
                    at = (d * 2 + c) * vec_rows
                    x_ref[d, c, t, :, block * width : (block + 1) * width] = result[at : at + vec_rows]
        for c in range(2):
            at = (t * 2 + c) * num_vecs
            b_ref[at : at + num_vecs, :] = bwd_ref[:, planes, c].reshape(num_vecs, width)

    row = lax.broadcasted_iota(jnp.int32, (row_count, row_count), 0)
    column = lax.broadcasted_iota(jnp.int32, (row_count, row_count), 1)
    row_spin = lax.rem(row, 4)
    diagonal = lax.div(row, 4) == lax.rem(column, vec_rows)
    column_spin = lax.div(column, vec_rows)

    def one_operator(op, carry):
        a = chain_ref[op, 0]
        b = chain_ref[op, 1]
        dir_a = dirs_ref[a]
        dir_b = dirs_ref[b]
        mix = jnp.zeros((row_count, row_count), F32)
        for t in range(4):
            in_t = column_spin == t
            for s in range(4):
                mix = jnp.where(in_t & (row_spin == s), spin_ref[a, s, t], mix)
        mix = jnp.where(diagonal, mix, 0.0)
        high = mix.astype(BF16)
        low = (mix - high.astype(F32)).astype(BF16)
        mix = jnp.concatenate([high, low], axis=1)
        for c in range(2):
            source = x_ref[dir_a, c].reshape(row_count, 4 * num_vecs)
            result = mm(mix, jnp.concatenate([source, source], axis=0)).astype(BF16)
            for s in range(4):
                for block in range(gy_n):
                    at = block * width + s * lane
                    to = c * num_vecs + block * lane
                    p_ref[s, :, to : to + lane] = result[:, at : at + lane]
        real_b, imag_b = elem_ref[dir_b, 0], elem_ref[dir_b, 1]
        right = jnp.concatenate(
            [
                jnp.concatenate([real_b, imag_b], axis=1),
                jnp.concatenate([-imag_b, real_b], axis=1),
            ],
            axis=0,
        )
        parts = [mm(p_ref[s], right) for s in range(4)]
        for t in range(4):
            total = parts[0] * (spin_ref[b, 0, t] * inverse)
            for s in range(1, 4):
                total += parts[s] * (spin_ref[b, s, t] * inverse)
            total = total.astype(BF16)
            real, imag = total[:, :num_vecs], total[:, num_vecs:]
            at = 2 * t * num_vecs
            q_ref[:row_count, at : at + num_vecs] = real
            q_ref[:row_count, at + num_vecs : at + 2 * num_vecs] = -imag
            q_ref[row_count:, at : at + num_vecs] = imag
            q_ref[row_count:, at + num_vecs : at + 2 * num_vecs] = real
        final = mm(q_ref[...], b_ref[...]).astype(BF16)
        out_ref[op, 0] = final[:row_count]
        out_ref[op, 1] = final[row_count:]
        return carry

    lax.fori_loop(0, op_count, one_operator, 0)


def summed_over(value, axis):
    total = value.astype(F32)
    for step in range(1, lax.axis_size(axis)):
        total += passed_along(value, axis, step).astype(F32)
    return total


def scattered_over(value, axis):
    count = lax.axis_size(axis)
    me = lax.axis_index(axis)
    total = lax.dynamic_index_in_dim(value, me, 0, keepdims=False).astype(F32)
    for step in range(1, count):
        part = lax.dynamic_index_in_dim(value, lax.rem(me + step, count), 0, keepdims=False)
        total += passed_along(part, axis, step).astype(F32)
    return total


def gathered_over(value, axis):
    count = lax.axis_size(axis)
    me = lax.axis_index(axis)
    result = jnp.zeros((count,) + value.shape, value.dtype)
    for step in range(count):
        part = passed_along(value, axis, step) if step else value
        result = lax.dynamic_update_index_in_dim(result, part, lax.rem(me - step + count, count), 0)
    return result


def on_device(eigvecs, links, directions, spin_mats, forward_peram, backward_peram, chain_order):
    extent = eigvecs.shape[:3]
    num_vecs = eigvecs.shape[-1]
    gx_n, gy_n, gz_n = (lax.axis_size(name) for name in ("gx", "gy", "gz"))
    gx, gz = lax.axis_index("gx"), lax.axis_index("gz")

    ordered = eigvecs.transpose(3, 0, 1, 2, 4, 5)
    faces = []
    for e, axis in enumerate(("gx", "gy", "gz")):
        face = lax.slice_in_dim(ordered, 0, 1, axis=1 + e).reshape(-1, num_vecs)
        faces.append(passed_along(face, axis, -1))
    vec = ordered.reshape(-1, num_vecs)

    rows, cols = forward_peram.shape[1:]
    piece = rows // gz_n
    spread, tables = site_tables(extent)
    lane = cols // 4
    perm = np.zeros((cols, cols), np.float32)
    for s in range(4):
        perm[4 * np.arange(lane) + s, s * lane + np.arange(lane)] = 1
    constants = [perm, spread] + [tables[e][k] for k in range(3) for e in range(3)]
    constants = [jnp.asarray(c, BF16) for c in constants]
    piece_shape = jax.ShapeDtypeStruct((2, piece, cols), BF16)
    fwd_piece, bwd_piece, *link_mats = pl.pallas_call(
        prepare_kernel,
        out_shape=[piece_shape, piece_shape]
        + [jax.ShapeDtypeStruct((3 * t[0].shape[0], t[0].shape[1]), BF16) for t in tables],
        in_specs=[SMEM] + [VMEM] * (3 + len(constants)),
        out_specs=[VMEM] * 5,
        compiler_params=pltpu.CompilerParams(vmem_limit_bytes=24 * 2**20),
        name="prepare",
    )(gz.reshape(1), links.reshape(-1, 54), forward_peram, backward_peram, *constants)

    fwd_all = lax.all_gather(fwd_piece, ("gx", "gy", "gz"), axis=0, tiled=False)
    fwd_all = fwd_all.reshape(gx_n, gy_n, gz_n, 2, piece, cols)
    bwd_all = lax.all_gather(bwd_piece, ("gx", "gz"), axis=0, tiled=False)
    bwd_all = bwd_all.reshape(gx_n, gz_n, 2, piece, cols)

    volume = math.prod(extent) * gx_n * gy_n * gz_n
    partial = pl.pallas_call(
        functools.partial(correlate_kernel, 1.0 / math.sqrt(12.0 * volume)),
        out_shape=jax.ShapeDtypeStruct((6, num_vecs, num_vecs), BF16),
        in_specs=[VMEM] * 7,
        out_specs=VMEM,
        compiler_params=pltpu.CompilerParams(vmem_limit_bytes=24 * 2**20),
        name="correlate",
    )(vec, *faces, *link_mats)

    own_rows = num_vecs // (gz_n * gx_n)
    parts = partial.reshape(6, gz_n, gx_n, own_rows, num_vecs).transpose(1, 2, 0, 3, 4)
    summed = scattered_over(parts, "gz").astype(BF16)
    summed = summed_over(summed, "gy").astype(BF16)
    summed = scattered_over(summed, "gx").astype(BF16)
    elem = gathered_over(gathered_over(summed, "gx"), "gz")
    elem = elem.transpose(2, 0, 1, 3, 4).reshape(3, 2, num_vecs, num_vecs)

    op_count = chain_order.shape[0]
    row_count = rows
    return pl.pallas_call(
        functools.partial(chain_kernel, 1.0 / math.sqrt(4 * num_vecs)),
        out_shape=jax.ShapeDtypeStruct((op_count, 2, row_count, cols), BF16),
        in_specs=[SMEM] * 4 + [VMEM] * 3,
        out_specs=VMEM,
        scratch_shapes=[
            pltpu.VMEM((3, 2, 4, row_count // 4, 4 * num_vecs), BF16),
            pltpu.VMEM((4, row_count, 2 * num_vecs), BF16),
            pltpu.VMEM((2 * row_count, 8 * num_vecs), BF16),
            pltpu.VMEM((8 * num_vecs, cols), BF16),
        ],
        compiler_params=pltpu.CompilerParams(vmem_limit_bytes=48 * 2**20),
        name="chain",
    )(gx.reshape(1), directions, spin_mats, chain_order, elem, fwd_all, bwd_all)


def solution(mesh):
    in_specs = (
        P("gx", "gy", "gz", None, None, None),
        P("gx", "gy", "gz", None, None, None, None),
        P(),
        P(),
        P(None, "gx", "gy"),
        P(None, "gx", "gy"),
        P("gz", None),
    )
    out_specs = P("gz", None, "gx", "gy")
    return jax.shard_map(
        on_device, mesh=mesh, in_specs=in_specs, out_specs=out_specs, check_vma=False
    )
```

```python
import functools
import math

import jax
import jax.numpy as jnp
from jax import lax
from jax.experimental import pallas as pl
from jax.experimental.pallas import tpu as pltpu
from jax.sharding import PartitionSpec as P

VMEM = pl.BlockSpec(memory_space=pltpu.VMEM)
SMEM = pl.BlockSpec(memory_space=pltpu.SMEM)
BF16 = jnp.bfloat16
F32 = jnp.float32


def passed_along(value, axis, steps):
    count = lax.axis_size(axis)
    pairs = [(source, (source + steps) % count) for source in range(count)]
    return lax.ppermute(value, axis, pairs)


def mm(left, right):
    return jnp.dot(left, right, preferred_element_type=F32)


def parts_of(value, divisor):
    quotient = jnp.floor((value + 0.5) * (1.0 / divisor))
    return quotient, value - quotient * divisor


def whole_numbers(shape, axis):
    return lax.broadcasted_iota(jnp.int32, shape, axis).astype(F32)


def chosen(condition):
    return jnp.where(condition, 1.0, 0.0)


def coordinates(index, extent):
    rest, third = parts_of(index, extent[2])
    first, second = parts_of(rest, extent[1])
    return [first, second, third]


def source_columns(extent, e):
    count = math.prod(extent)
    face = count // extent[e]
    inner = count - face if e == 0 else count
    total = 6 * (inner + face)
    column = whole_numbers((1, total), 1)
    beyond = chosen(column >= 6 * inner)
    place = column - beyond * (6 * inner)
    block = 3 * inner + beyond * (3 * (face - inner))
    part = chosen(place >= block)
    site, colour = parts_of(place - part * block, 3)
    within = coordinates(site, extent)
    if e == 0:
        within[0] = within[0] + 1
    flat = [n for d, n in enumerate(extent) if d != e]
    outer, last = parts_of(site, flat[1])
    edge = [outer, last]
    edge.insert(e, jnp.full_like(site, extent[e]))
    where = [w + beyond * (o - w) for w, o in zip(within, edge)]
    return total, part, where, colour


def pieces_kernel(z_ref, fwd_ref, bwd_ref, fwd_out, bwd_out):
    rows, cols = fwd_ref.shape[1:]
    piece = fwd_out.shape[1]
    per_spin = rows // 4
    lane = cols // 4
    flat = lax.broadcasted_iota(jnp.int32, (piece, 1), 0) + z_ref[0] * piece
    spin = jnp.zeros_like(flat)
    for t in range(1, 4):
        spin += jnp.where(flat >= t * per_spin, 1, 0)
    source = 4 * (flat - spin * per_spin) + spin
    select = chosen(lax.broadcasted_iota(jnp.int32, (piece, rows), 1) == source).astype(BF16)
    column = lax.broadcasted_iota(jnp.int32, (1, cols), 1)
    spin = jnp.zeros_like(column)
    for t in range(1, 4):
        spin += jnp.where(column >= t * lane, 1, 0)
    source = 4 * (column - spin * lane) + spin
    perm = chosen(lax.broadcasted_iota(jnp.int32, (cols, cols), 0) == source).astype(BF16)
    for c in range(2):
        picked = mm(select, fwd_ref[c]).astype(BF16)
        fwd_out[c] = mm(picked, perm).astype(BF16)
        bwd_out[c] = mm(select, bwd_ref[c]).astype(BF16)


def links_kernel(extent, link_ref, *outs):
    count = math.prod(extent)
    rows = 6 * count
    row = whole_numbers((rows, 1), 0)
    row_part = chosen(row >= 3 * count)
    row_site, row_colour = parts_of(row - row_part * (3 * count), 3)
    row_where = coordinates(row_site, extent)
    link = link_ref[...]
    high = link.astype(BF16)
    rest = link - high.astype(F32)
    mid = rest.astype(BF16)
    low = (rest - mid.astype(F32)).astype(BF16)
    spread = chosen(row_site == whole_numbers((rows, count), 1)).astype(BF16)
    by_row = [mm(spread, part) for part in (high, mid, low)]
    by_row = [jnp.concatenate([part, part], axis=1) for part in by_row]

    def entry_of(entry):
        half = chosen(entry >= 54)
        direction, left = parts_of(entry - 54 * half, 18)
        part, left = parts_of(left, 9)
        into, out_of = parts_of(left, 3)
        return half, direction, part, into, out_of

    half, direction, _, into, _ = entry_of(whole_numbers((1, 108), 1))
    own_part = (half == row_part) & (into == row_colour)
    place_half, _, place_part, _, place_colour = entry_of(whole_numbers((108, 1), 0))
    for e, out in enumerate(outs):
        keep = chosen(own_part & (direction == e))
        picked = jnp.concatenate([part * keep for part in by_row], axis=0).astype(BF16)
        total, part, where, colour = source_columns(extent, e)
        sign = 1.0 - 2.0 * part * (1.0 - place_half)
        match = (place_colour == colour) & (jnp.abs(place_part - part) == place_half)
        placed = mm(picked, jnp.where(match, sign, 0.0).astype(BF16))
        same = None
        for d in range(3):
            hit = row_where[d] + (1.0 if d == e else 0.0) == where[d]
            same = hit if same is None else same & hit
        mask = chosen(same)
        for n in range(3):
            at = slice(n * rows, (n + 1) * rows)
            out[at, :] = (placed[at] * mask).astype(BF16)


def correlate_kernel(scale, vec_ref, face0, face1, face2, mat0, mat1, mat2, out_ref):
    vec = vec_ref[...]
    rows = vec.shape[0]
    half = rows // 2
    width = vec.shape[1]
    lower = half - face0.shape[0] // 2
    sources = [
        jnp.concatenate([vec[half - lower : half], vec[rows - lower :], face0[...]], axis=0),
        jnp.concatenate([vec, face1[...]], axis=0),
        jnp.concatenate([vec, face2[...]], axis=0),
    ]
    for e, mat in enumerate((mat0, mat1, mat2)):
        terms = mm(mat[...], sources[e])
        moved = terms[:rows] + terms[rows : 2 * rows] + terms[2 * rows :]
        moved = moved.astype(BF16)
        turned = jnp.concatenate([moved[half:], -moved[:half]], axis=0)
        right = jnp.concatenate([moved, turned], axis=1)
        product = lax.dot_general(
            vec, right, (((0,), (0,)), ((), ())), preferred_element_type=F32
        )
        product = (product * scale).astype(BF16)
        out_ref[2 * e] = product[:, :width]
        out_ref[2 * e + 1] = product[:, width:]


def chain_kernel(
    inverse, plan, me_ref, dirs_ref, spin_ref, chain_ref, *refs
):
    elem_count, fwd_keys, bwd_keys = plan
    elem_in, refs = refs[:elem_count], refs[elem_count:]
    fwd_in, refs = refs[: len(fwd_keys)], refs[len(fwd_keys) :]
    bwd_in, refs = refs[: len(bwd_keys)], refs[len(bwd_keys) :]
    out_ref, elem_all, fwd_ref, bwd_ref, x_ref, p_ref, q_ref, b_ref, sems = refs
    _, gx_n, gz_n, own_rows, num_vecs = elem_all.shape
    gy_n = fwd_ref.shape[1]
    width = fwd_ref.shape[-1]
    op_count = out_ref.shape[0]
    row_count = out_ref.shape[2]
    vec_rows = row_count // 4
    spin_pieces = gz_n // 4
    lane = width // 4
    gx, gy, gz = me_ref[0], me_ref[1], me_ref[2]

    def back(at, step, count):
        return lax.rem(at - step + count, count)

    def gz_from(dy, dc):
        return back(gz // 2, dy, gz_n // 2) * 2 + back(lax.rem(gz, 2), dc, 2)

    copies = []

    def place(source, target):
        copy = pltpu.make_async_copy(source, target, sems.at[len(copies)])
        copy.start()
        copies.append(copy)

    for n, ref in enumerate(elem_in):
        for step in range(gx_n):
            place(ref.at[step], elem_all.at[:, back(gx, step, gx_n), back(gz, n, gz_n)])
    for (dx, dy, dc), ref in zip(fwd_keys, fwd_in):
        for step in range(gx_n):
            place(ref.at[step], fwd_ref.at[back(gx, step, gx_n), back(gy, dx, gy_n), gz_from(dy, dc)])
    for (dy, dc), ref in zip(bwd_keys, bwd_in):
        for step in range(gx_n):
            place(ref.at[step], bwd_ref.at[back(gx, step, gx_n), gz_from(dy, dc)])
    for copy in copies:
        copy.wait()

    def elem(d, c):
        return elem_all[2 * d + c].reshape(num_vecs, num_vecs)

    def own(d, c):
        return elem_all[2 * d + c, gx].reshape(vec_rows, num_vecs)

    real_rows = [jnp.concatenate([own(d, 0), -own(d, 1)], axis=1) for d in range(3)]
    imag_rows = [jnp.concatenate([own(d, 1), own(d, 0)], axis=1) for d in range(3)]
    left = jnp.concatenate([part for d in range(3) for part in (real_rows[d], imag_rows[d])], axis=0)
    for t in range(4):
        planes = slice(t * spin_pieces, (t + 1) * spin_pieces)
        for block in range(gy_n):
            right = jnp.concatenate(
                [fwd_ref[:, block, planes, c].reshape(num_vecs, width) for c in range(2)], axis=0
            )
            result = mm(left, right).astype(BF16)
            for d in range(3):
                for c in range(2):
                    at = (d * 2 + c) * vec_rows
                    x_ref[d, c, t, :, block * width : (block + 1) * width] = result[at : at + vec_rows]
        for c in range(2):
            at = (t * 2 + c) * num_vecs
            b_ref[at : at + num_vecs, :] = bwd_ref[:, planes, c].reshape(num_vecs, width)

    row = lax.broadcasted_iota(jnp.int32, (row_count, row_count), 0)
    column = lax.broadcasted_iota(jnp.int32, (row_count, row_count), 1)
    row_spin = lax.rem(row, 4)
    diagonal = lax.div(row, 4) == lax.rem(column, vec_rows)
    column_spin = lax.div(column, vec_rows)

    def one_operator(op, carry):
        a = chain_ref[op, 0]
        b = chain_ref[op, 1]
        dir_a = dirs_ref[a]
        dir_b = dirs_ref[b]
        mix = jnp.zeros((row_count, row_count), F32)
        for t in range(4):
            in_t = column_spin == t
            for s in range(4):
                mix = jnp.where(in_t & (row_spin == s), spin_ref[a, s, t], mix)
        mix = jnp.where(diagonal, mix, 0.0)
        high = mix.astype(BF16)
        low = (mix - high.astype(F32)).astype(BF16)
        mix = jnp.concatenate([high, low], axis=1)
        for c in range(2):
            source = x_ref[dir_a, c].reshape(row_count, 4 * num_vecs)
            result = mm(mix, jnp.concatenate([source, source], axis=0)).astype(BF16)
            for s in range(4):
                for block in range(gy_n):
                    at = block * width + s * lane
                    to = c * num_vecs + block * lane
                    p_ref[s, :, to : to + lane] = result[:, at : at + lane]
        real_b, imag_b = elem(dir_b, 0), elem(dir_b, 1)
        right = jnp.concatenate(
            [
                jnp.concatenate([real_b, imag_b], axis=1),
                jnp.concatenate([-imag_b, real_b], axis=1),
            ],
            axis=0,
        )
        parts = [mm(p_ref[s], right) for s in range(4)]
        for t in range(4):
            total = parts[0] * (spin_ref[b, 0, t] * inverse)
            for s in range(1, 4):
                total += parts[s] * (spin_ref[b, s, t] * inverse)
            total = total.astype(BF16)
            real, imag = total[:, :num_vecs], total[:, num_vecs:]
            at = 2 * t * num_vecs
            q_ref[:row_count, at : at + num_vecs] = real
            q_ref[:row_count, at + num_vecs : at + 2 * num_vecs] = -imag
            q_ref[row_count:, at : at + num_vecs] = imag
            q_ref[row_count:, at + num_vecs : at + 2 * num_vecs] = real
        final = mm(q_ref[...], b_ref[...]).astype(BF16)
        out_ref[op, 0] = final[:row_count]
        out_ref[op, 1] = final[row_count:]
        return carry

    lax.fori_loop(0, op_count, one_operator, 0)


def summed_over(value, axis):
    total = value.astype(F32)
    for step in range(1, lax.axis_size(axis)):
        total += passed_along(value, axis, step).astype(F32)
    return total


def scattered_over(value, axis):
    count = lax.axis_size(axis)
    me = lax.axis_index(axis)
    total = lax.dynamic_index_in_dim(value, me, 0, keepdims=False).astype(F32)
    for step in range(1, count):
        part = lax.dynamic_index_in_dim(value, lax.rem(me + step, count), 0, keepdims=False)
        total += passed_along(part, axis, step).astype(F32)
    return total


def gathered_over(value, axis):
    count = lax.axis_size(axis)
    return jnp.stack([value] + [passed_along(value, axis, step) for step in range(1, count)])


def passed_in_gz(value, dy, dc):
    count = lax.axis_size("gz")
    chips = count // 2
    pairs = [(n, ((n // 2 + dy) % chips) * 2 + (n + dc) % 2) for n in range(count)]
    return lax.ppermute(value, "gz", pairs)


def on_device(eigvecs, links, directions, spin_mats, forward_peram, backward_peram, chain_order):
    extent = eigvecs.shape[:3]
    num_vecs = eigvecs.shape[-1]
    gx_n, gy_n, gz_n = (lax.axis_size(name) for name in ("gx", "gy", "gz"))
    chips = gz_n // 2
    me = jnp.stack([lax.axis_index(name) for name in ("gx", "gy", "gz")]).astype(jnp.int32)

    ordered = eigvecs.transpose(3, 0, 1, 2, 4, 5)
    faces = []
    for e, axis in enumerate(("gx", "gy", "gz")):
        face = lax.slice_in_dim(ordered, 0, 1, axis=1 + e).reshape(-1, num_vecs)
        faces.append(passed_along(face, axis, -1))
    vec = ordered.reshape(-1, num_vecs)

    rows, cols = forward_peram.shape[1:]
    piece = rows // gz_n
    piece_shape = jax.ShapeDtypeStruct((2, piece, cols), BF16)
    fwd_piece, bwd_piece = pl.pallas_call(
        pieces_kernel,
        out_shape=[piece_shape, piece_shape],
        in_specs=[SMEM, VMEM, VMEM],
        out_specs=[VMEM, VMEM],
        compiler_params=pltpu.CompilerParams(vmem_limit_bytes=24 * 2**20),
        name="pieces",
    )(me[2:], forward_peram, backward_peram)

    fwd_line = gathered_over(fwd_piece, "gx")
    bwd_line = gathered_over(bwd_piece, "gx")
    fwd_parts, bwd_parts = {}, {}
    for dy in range(chips):
        mine = passed_in_gz(fwd_line, dy, 0) if dy else fwd_line
        for dx in range(gy_n):
            fwd_parts[dx, dy, 0] = passed_along(mine, "gy", dx) if dx else mine
        bwd_parts[dy, 0] = passed_in_gz(bwd_line, dy, 0) if dy else bwd_line
    for dx, dy, _ in list(fwd_parts):
        fwd_parts[dx, dy, 1] = passed_in_gz(fwd_parts[dx, dy, 0], 0, 1)
    for dy, _ in list(bwd_parts):
        bwd_parts[dy, 1] = passed_in_gz(bwd_parts[dy, 0], 0, 1)

    site_rows = 6 * math.prod(extent)
    link_mats = pl.pallas_call(
        functools.partial(links_kernel, extent),
        out_shape=[
            jax.ShapeDtypeStruct((3 * site_rows, site_rows - (0 if e else site_rows // extent[0]) + site_rows // extent[e]), BF16)
            for e in range(3)
        ],
        in_specs=[VMEM],
        out_specs=[VMEM] * 3,
        compiler_params=pltpu.CompilerParams(vmem_limit_bytes=24 * 2**20),
        name="link_matrices",
    )(links.reshape(-1, 54))

    volume = math.prod(extent) * gx_n * gy_n * gz_n
    partial = pl.pallas_call(
        functools.partial(correlate_kernel, 1.0 / math.sqrt(12.0 * volume)),
        out_shape=jax.ShapeDtypeStruct((6, num_vecs, num_vecs), BF16),
        in_specs=[VMEM] * 7,
        out_specs=VMEM,
        compiler_params=pltpu.CompilerParams(vmem_limit_bytes=24 * 2**20),
        name="correlate",
    )(vec, *faces, *link_mats)

    own_rows = num_vecs // (gz_n * gx_n)
    parts = partial.reshape(6, gx_n, gz_n, own_rows, num_vecs).transpose(2, 1, 0, 3, 4)
    summed = scattered_over(parts, "gz").astype(BF16)
    summed = summed_over(summed, "gy").astype(BF16)
    summed = scattered_over(summed, "gx").astype(BF16)
    elem_line = gathered_over(summed, "gx")
    elem_parts = [elem_line] + [passed_along(elem_line, "gz", step) for step in range(1, gz_n)]

    op_count = chain_order.shape[0]
    plan = (len(elem_parts), tuple(fwd_parts), tuple(bwd_parts))
    operands = [*elem_parts, *fwd_parts.values(), *bwd_parts.values()]
    return pl.pallas_call(
        functools.partial(chain_kernel, 1.0 / math.sqrt(4 * num_vecs), plan),
        out_shape=jax.ShapeDtypeStruct((op_count, 2, rows, cols), BF16),
        in_specs=[SMEM] * 4 + [pl.BlockSpec(memory_space=pl.ANY)] * len(operands),
        out_specs=VMEM,
        scratch_shapes=[
            pltpu.VMEM((6, gx_n, gz_n, own_rows, num_vecs), BF16),
            pltpu.VMEM((gx_n, gy_n, gz_n, 2, piece, cols), BF16),
            pltpu.VMEM((gx_n, gz_n, 2, piece, cols), BF16),
            pltpu.VMEM((3, 2, 4, rows // 4, 4 * num_vecs), BF16),
            pltpu.VMEM((4, rows, 2 * num_vecs), BF16),
            pltpu.VMEM((2 * rows, 8 * num_vecs), BF16),
            pltpu.VMEM((8 * num_vecs, cols), BF16),
            pltpu.SemaphoreType.DMA((gx_n * len(operands),)),
        ],
        compiler_params=pltpu.CompilerParams(vmem_limit_bytes=40 * 2**20),
        name="chain",
    )(me, directions, spin_mats, chain_order, *operands)


def solution(mesh):
    in_specs = (
        P("gx", "gy", "gz", None, None, None),
        P("gx", "gy", "gz", None, None, None, None),
        P(),
        P(),
        P(None, "gx", "gy"),
        P(None, "gx", "gy"),
        P("gz", None),
    )
    out_specs = P("gz", None, "gx", "gy")
    return jax.shard_map(
        on_device, mesh=mesh, in_specs=in_specs, out_specs=out_specs, check_vma=False
    )
```

```python
import functools
import math

import jax
import jax.numpy as jnp
from jax import lax
from jax.experimental import pallas as pl
from jax.experimental.pallas import tpu as pltpu
from jax.sharding import PartitionSpec as P

VMEM = pl.BlockSpec(memory_space=pltpu.VMEM)
SMEM = pl.BlockSpec(memory_space=pltpu.SMEM)
BF16 = jnp.bfloat16
F32 = jnp.float32


def passed_along(value, axis, steps):
    count = lax.axis_size(axis)
    pairs = [(source, (source + steps) % count) for source in range(count)]
    return lax.ppermute(value, axis, pairs)


def mm(left, right):
    return jnp.dot(left, right, preferred_element_type=F32)


def parts_of(value, divisor):
    quotient = jnp.floor((value + 0.5) * (1.0 / divisor))
    return quotient, value - quotient * divisor


def whole_numbers(shape, axis):
    return lax.broadcasted_iota(jnp.int32, shape, axis).astype(F32)


def chosen(condition):
    return jnp.where(condition, 1.0, 0.0)


def coordinates(index, extent):
    rest, third = parts_of(index, extent[2])
    first, second = parts_of(rest, extent[1])
    return [first, second, third]


def source_columns(extent, e):
    count = math.prod(extent)
    face = count // extent[e]
    inner = count - face if e == 0 else count
    total = 6 * (inner + face)
    column = whole_numbers((1, total), 1)
    beyond = chosen(column >= 6 * inner)
    place = column - beyond * (6 * inner)
    block = 3 * inner + beyond * (3 * (face - inner))
    part = chosen(place >= block)
    site, colour = parts_of(place - part * block, 3)
    within = coordinates(site, extent)
    if e == 0:
        within[0] = within[0] + 1
    flat = [n for d, n in enumerate(extent) if d != e]
    outer, last = parts_of(site, flat[1])
    edge = [outer, last]
    edge.insert(e, jnp.full_like(site, extent[e]))
    where = [w + beyond * (o - w) for w, o in zip(within, edge)]
    return total, part, where, colour


def pieces_kernel(z_ref, fwd_ref, bwd_ref, fwd_out, bwd_out):
    rows, cols = fwd_ref.shape[1:]
    piece = fwd_out.shape[1]
    per_spin = rows // 4
    lane = cols // 4
    flat = lax.broadcasted_iota(jnp.int32, (piece, 1), 0) + z_ref[0] * piece
    spin = jnp.zeros_like(flat)
    for t in range(1, 4):
        spin += jnp.where(flat >= t * per_spin, 1, 0)
    source = 4 * (flat - spin * per_spin) + spin
    select = chosen(lax.broadcasted_iota(jnp.int32, (piece, rows), 1) == source).astype(BF16)
    column = lax.broadcasted_iota(jnp.int32, (1, cols), 1)
    spin = jnp.zeros_like(column)
    for t in range(1, 4):
        spin += jnp.where(column >= t * lane, 1, 0)
    source = 4 * (column - spin * lane) + spin
    perm = chosen(lax.broadcasted_iota(jnp.int32, (cols, cols), 0) == source).astype(BF16)
    for c in range(2):
        picked = mm(select, fwd_ref[c]).astype(BF16)
        fwd_out[c] = mm(picked, perm).astype(BF16)
        bwd_out[c] = mm(select, bwd_ref[c]).astype(BF16)


def links_kernel(extent, link_ref, *outs):
    count = math.prod(extent)
    rows = 6 * count
    row = whole_numbers((rows, 1), 0)
    row_part = chosen(row >= 3 * count)
    row_site, row_colour = parts_of(row - row_part * (3 * count), 3)
    row_where = coordinates(row_site, extent)
    link = link_ref[...]
    high = link.astype(BF16)
    rest = link - high.astype(F32)
    mid = rest.astype(BF16)
    low = (rest - mid.astype(F32)).astype(BF16)
    spread = chosen(row_site == whole_numbers((rows, count), 1)).astype(BF16)
    by_row = [mm(spread, part) for part in (high, mid, low)]
    by_row = [jnp.concatenate([part, part], axis=1) for part in by_row]

    def entry_of(entry):
        half = chosen(entry >= 54)
        direction, left = parts_of(entry - 54 * half, 18)
        part, left = parts_of(left, 9)
        into, out_of = parts_of(left, 3)
        return half, direction, part, into, out_of

    half, direction, _, into, _ = entry_of(whole_numbers((1, 108), 1))
    own_part = (half == row_part) & (into == row_colour)
    place_half, _, place_part, _, place_colour = entry_of(whole_numbers((108, 1), 0))
    for e, out in enumerate(outs):
        keep = chosen(own_part & (direction == e))
        picked = jnp.concatenate([part * keep for part in by_row], axis=0).astype(BF16)
        total, part, where, colour = source_columns(extent, e)
        sign = 1.0 - 2.0 * part * (1.0 - place_half)
        match = (place_colour == colour) & (jnp.abs(place_part - part) == place_half)
        placed = mm(picked, jnp.where(match, sign, 0.0).astype(BF16))
        same = None
        for d in range(3):
            hit = row_where[d] + (1.0 if d == e else 0.0) == where[d]
            same = hit if same is None else same & hit
        mask = chosen(same)
        for n in range(3):
            at = slice(n * rows, (n + 1) * rows)
            out[at, :] = (placed[at] * mask).astype(BF16)


def correlate_kernel(scale, vec_ref, face0, face1, face2, mat0, mat1, mat2, out_ref):
    gz_n, gx_n, _, own_rows, _ = out_ref.shape
    vec = vec_ref[...]
    rows = vec.shape[0]
    half = rows // 2
    width = vec.shape[1]
    lower = half - face0.shape[0] // 2
    sources = [
        jnp.concatenate([vec[half - lower : half], vec[rows - lower :], face0[...]], axis=0),
        jnp.concatenate([vec, face1[...]], axis=0),
        jnp.concatenate([vec, face2[...]], axis=0),
    ]
    for e, mat in enumerate((mat0, mat1, mat2)):
        terms = mm(mat[...], sources[e])
        moved = terms[:rows] + terms[rows : 2 * rows] + terms[2 * rows :]
        moved = moved.astype(BF16)
        turned = jnp.concatenate([moved[half:], -moved[:half]], axis=0)
        right = jnp.concatenate([moved, turned], axis=1)
        product = lax.dot_general(
            vec, right, (((0,), (0,)), ((), ())), preferred_element_type=F32
        )
        product = (product * scale).astype(BF16)
        for g in range(gx_n):
            for z in range(gz_n):
                at = (g * gz_n + z) * own_rows
                out_ref[z, g, 2 * e] = product[at : at + own_rows, :width]
                out_ref[z, g, 2 * e + 1] = product[at : at + own_rows, width:]


def chain_kernel(inverse, plan, me_ref, dirs_ref, spin_ref, chain_ref, *refs):
    line, elem_keys, fwd_keys, bwd_keys = plan
    elem_in, refs = refs[: len(elem_keys)], refs[len(elem_keys) :]
    fwd_in, refs = refs[: len(fwd_keys)], refs[len(fwd_keys) :]
    bwd_in, refs = refs[: len(bwd_keys)], refs[len(bwd_keys) :]
    out_ref, elem_all, elem_ref, x_ref, p_ref, q_ref, b_ref = refs
    _, gx_n, gz_n, own_rows, num_vecs = elem_all.shape
    width = out_ref.shape[3]
    op_count = out_ref.shape[0]
    row_count = out_ref.shape[2]
    vec_rows = row_count // 4
    gy_n = 4 * num_vecs // width
    lane = width // 4
    halves = gz_n // 4
    gx, gy, gz = me_ref[0], me_ref[1], me_ref[2]

    def back(at, step, count):
        return lax.rem(at - step + count, count)

    def gz_from(dy, dc):
        return back(lax.div(gz, 2), dy, gz_n // 2) * 2 + back(lax.rem(gz, 2), dc, 2)

    for (dy, dc), ref in zip(elem_keys, elem_in):
        for step in range(gx_n):
            elem_all[:, back(gx, step, gx_n), gz_from(dy, dc)] = ref[step]
    column = lax.broadcasted_iota(jnp.int32, (1, num_vecs), 1)
    source = jnp.zeros_like(column)
    half_rows = vec_rows // halves
    for place, offset in enumerate(line):
        for half in range(halves):
            at = place * vec_rows + half * half_rows
            from_half = lax.bitwise_xor(lax.rem(gz, 2), half) if halves == 2 else half
            begin = lax.bitwise_xor(gx, offset) * vec_rows + from_half * half_rows
            inside = (column >= at) & (column < at + half_rows)
            source = jnp.where(inside, column + (begin - at), source)
    perm = chosen(lax.broadcasted_iota(jnp.int32, (num_vecs, num_vecs), 0) == source).astype(BF16)
    for n in range(6):
        elem_ref[n] = mm(elem_all[n].reshape(num_vecs, num_vecs), perm).astype(BF16)

    if halves == 1:
        groups = [[key] for key in bwd_keys]
    else:
        groups = [[(dy, dc) for dc in range(2)] for dy in range(gz_n // 2)]
    spins = [lax.div(gz_from(*group[0]), halves) for group in groups]

    def rows_of(parts, c):
        return jnp.concatenate([part[:, c] for part in parts], axis=1).reshape(num_vecs, width)

    first_row = pl.multiple_of(gx * vec_rows, vec_rows)

    def own(d, c):
        return elem_ref[2 * d + c, pl.ds(first_row, vec_rows), :]

    real_rows = [jnp.concatenate([own(d, 0), -own(d, 1)], axis=1) for d in range(3)]
    imag_rows = [jnp.concatenate([own(d, 1), own(d, 0)], axis=1) for d in range(3)]
    left = jnp.concatenate([part for d in range(3) for part in (real_rows[d], imag_rows[d])], axis=0)
    fwd_at = dict(zip(fwd_keys, fwd_in))
    bwd_at = dict(zip(bwd_keys, bwd_in))
    for t, group in enumerate(groups):
        for dx in range(gy_n):
            parts = [fwd_at[(dx,) + key] for key in group]
            right = jnp.concatenate([rows_of(parts, c) for c in range(2)], axis=0)
            result = mm(left, right).astype(BF16)
            for d in range(3):
                for c in range(2):
                    at = (d * 2 + c) * vec_rows
                    x_ref[d, c, dx, t] = result[at : at + vec_rows]
        for c in range(2):
            at = (t * 2 + c) * num_vecs
            b_ref[at : at + num_vecs, :] = rows_of([bwd_at[key] for key in group], c)

    row = lax.broadcasted_iota(jnp.int32, (row_count, row_count), 0)
    column = lax.broadcasted_iota(jnp.int32, (row_count, row_count), 1)
    row_spin = lax.rem(row, 4)
    diagonal = lax.div(row, 4) == lax.rem(column, vec_rows)
    column_spin = lax.div(column, vec_rows)
    blocks = [pl.multiple_of(back(gy, dx, gy_n) * lane, lane) for dx in range(gy_n)]

    def one_operator(op, carry):
        a = chain_ref[op, 0]
        b = chain_ref[op, 1]
        dir_a = dirs_ref[a]
        dir_b = dirs_ref[b]
        mix = jnp.zeros((row_count, row_count), F32)
        for t in range(4):
            in_t = column_spin == t
            for s in range(4):
                mix = jnp.where(in_t & (row_spin == s), spin_ref[a, s, spins[t]], mix)
        mix = jnp.where(diagonal, mix, 0.0)
        high = mix.astype(BF16)
        low = (mix - high.astype(F32)).astype(BF16)
        mix = jnp.concatenate([high, low], axis=1)
        for c in range(2):
            for dx in range(gy_n):
                source = x_ref[dir_a, c, dx].reshape(row_count, width)
                result = mm(mix, jnp.concatenate([source, source], axis=0)).astype(BF16)
                for s in range(4):
                    to = c * num_vecs + dx * lane
                    p_ref[s, :, to : to + lane] = result[:, s * lane : (s + 1) * lane]

        def elem(c):
            return jnp.concatenate([elem_ref[2 * dir_b + c, pl.ds(at, lane), :] for at in blocks], axis=0)

        real_b, imag_b = elem(0), elem(1)
        right = jnp.concatenate(
            [
                jnp.concatenate([real_b, imag_b], axis=1),
                jnp.concatenate([-imag_b, real_b], axis=1),
            ],
            axis=0,
        )
        parts = [mm(p_ref[s], right) for s in range(4)]
        for t in range(4):
            total = parts[0] * (spin_ref[b, 0, spins[t]] * inverse)
            for s in range(1, 4):
                total += parts[s] * (spin_ref[b, s, spins[t]] * inverse)
            total = total.astype(BF16)
            real, imag = total[:, :num_vecs], total[:, num_vecs:]
            at = 2 * t * num_vecs
            q_ref[:row_count, at : at + num_vecs] = real
            q_ref[:row_count, at + num_vecs : at + 2 * num_vecs] = -imag
            q_ref[row_count:, at : at + num_vecs] = imag
            q_ref[row_count:, at + num_vecs : at + 2 * num_vecs] = real
        final = mm(q_ref[...], b_ref[...]).astype(BF16)
        out_ref[op, 0] = final[:row_count]
        out_ref[op, 1] = final[row_count:]
        return carry

    lax.fori_loop(0, op_count, one_operator, 0)


def passed_in_gz(value, dy, dc):
    count = lax.axis_size("gz")
    chips = count // 2
    pairs = [(n, ((n // 2 + dy) % chips) * 2 + (n + dc) % 2) for n in range(count)]
    return lax.ppermute(value, "gz", pairs)


def line_exchange(value, axis):
    count = lax.axis_size(axis)
    gathered = value[None]
    offsets = [0]
    distance = count // 2
    while distance:
        pairs = [(n, n ^ distance) for n in range(count)]
        gathered = jnp.concatenate([gathered, lax.ppermute(gathered, axis, pairs)])
        offsets += [offset ^ distance for offset in offsets]
        distance //= 2
    return gathered, tuple(offsets)


def part_at(value, index, axis=0):
    return lax.dynamic_index_in_dim(value, index, axis, keepdims=False)


def added(*values):
    return sum(value.astype(F32) for value in values).astype(BF16)


def on_device(eigvecs, links, directions, spin_mats, forward_peram, backward_peram, chain_order):
    extent = eigvecs.shape[:3]
    num_vecs = eigvecs.shape[-1]
    gx_n, gy_n, gz_n = (lax.axis_size(name) for name in ("gx", "gy", "gz"))
    chips = gz_n // 2
    gx, gy, gz = (lax.axis_index(name).astype(jnp.int32) for name in ("gx", "gy", "gz"))
    me = jnp.stack([gx, gy, gz])
    chip, core = lax.div(gz, 2), lax.rem(gz, 2)

    ordered = eigvecs.transpose(3, 0, 1, 2, 4, 5)
    faces = []
    for e, axis in enumerate(("gx", "gy", "gz")):
        face = lax.slice_in_dim(ordered, 0, 1, axis=1 + e).reshape(-1, num_vecs)
        faces.append(passed_along(face, axis, -1))
    vec = ordered.reshape(-1, num_vecs)

    rows, cols = forward_peram.shape[1:]
    piece = rows // gz_n
    piece_shape = jax.ShapeDtypeStruct((2, piece, cols), BF16)
    fwd_piece, bwd_piece = pl.pallas_call(
        pieces_kernel,
        out_shape=[piece_shape, piece_shape],
        in_specs=[SMEM, VMEM, VMEM],
        out_specs=[VMEM, VMEM],
        compiler_params=pltpu.CompilerParams(vmem_limit_bytes=24 * 2**20),
        name="pieces",
    )(me[2:], forward_peram, backward_peram)

    bwd_piece, link_rows = lax.optimization_barrier((bwd_piece, links.reshape(-1, 54)))
    fwd_line, line = line_exchange(fwd_piece, "gx")
    bwd_line, _ = line_exchange(bwd_piece, "gx")
    fwd_parts, bwd_parts = {}, {}
    for dy in range(chips):
        mine = passed_in_gz(fwd_line, dy, 0) if dy else fwd_line
        for dx in range(gy_n):
            fwd_parts[dx, dy, 0] = passed_along(mine, "gy", dx) if dx else mine
        bwd_parts[dy, 0] = passed_in_gz(bwd_line, dy, 0) if dy else bwd_line
    for dx, dy, _ in list(fwd_parts):
        fwd_parts[dx, dy, 1] = passed_in_gz(fwd_parts[dx, dy, 0], 0, 1)
    for dy, _ in list(bwd_parts):
        bwd_parts[dy, 1] = passed_in_gz(bwd_parts[dy, 0], 0, 1)

    site_rows = 6 * math.prod(extent)
    link_mats = pl.pallas_call(
        functools.partial(links_kernel, extent),
        out_shape=[
            jax.ShapeDtypeStruct((3 * site_rows, site_rows - (0 if e else site_rows // extent[0]) + site_rows // extent[e]), BF16)
            for e in range(3)
        ],
        in_specs=[VMEM],
        out_specs=[VMEM] * 3,
        compiler_params=pltpu.CompilerParams(vmem_limit_bytes=24 * 2**20),
        name="link_matrices",
    )(link_rows)

    volume = math.prod(extent) * gx_n * gy_n * gz_n
    own_rows = num_vecs // (gz_n * gx_n)
    partial = pl.pallas_call(
        functools.partial(correlate_kernel, 1.0 / math.sqrt(12.0 * volume)),
        out_shape=jax.ShapeDtypeStruct((gz_n, gx_n, 6, own_rows, num_vecs), BF16),
        in_specs=[VMEM] * 7,
        out_specs=VMEM,
        compiler_params=pltpu.CompilerParams(vmem_limit_bytes=24 * 2**20),
        name="correlate",
    )(vec, *faces, *link_mats)

    by_core = partial.reshape((chips, 2) + partial.shape[1:])
    summed = added(part_at(by_core, core, 1), passed_in_gz(part_at(by_core, 1 - core, 1), 0, 1))
    arrived = [passed_in_gz(part_at(summed, lax.rem(chip + dy, chips)), dy, 0) for dy in range(1, chips)]
    summed = added(part_at(summed, chip), *arrived)
    summed = added(summed, *[passed_along(summed, "gy", dx) for dx in range(1, gy_n)])
    arrived = [passed_along(part_at(summed, lax.rem(gx + dz, gx_n)), "gx", dz) for dz in range(1, gx_n)]
    summed = added(part_at(summed, gx), *arrived)
    elem_line = jnp.stack([summed] + [passed_along(summed, "gx", dz) for dz in range(1, gx_n)])
    elem_parts = {(dy, 0): passed_in_gz(elem_line, dy, 0) if dy else elem_line for dy in range(chips)}
    for dy in range(chips):
        elem_parts[dy, 1] = passed_in_gz(elem_parts[dy, 0], 0, 1)

    op_count = chain_order.shape[0]
    plan = (line, tuple(elem_parts), tuple(fwd_parts), tuple(bwd_parts))
    operands = [*elem_parts.values(), *fwd_parts.values(), *bwd_parts.values()]
    return pl.pallas_call(
        functools.partial(chain_kernel, 1.0 / math.sqrt(4 * num_vecs), plan),
        out_shape=jax.ShapeDtypeStruct((op_count, 2, rows, cols), BF16),
        in_specs=[SMEM] * 4 + [VMEM] * len(operands),
        out_specs=VMEM,
        scratch_shapes=[
            pltpu.VMEM((6, gx_n, gz_n, own_rows, num_vecs), BF16),
            pltpu.VMEM((6, num_vecs, num_vecs), BF16),
            pltpu.VMEM((3, 2, gy_n, 4, rows // 4, cols), BF16),
            pltpu.VMEM((4, rows, 2 * num_vecs), BF16),
            pltpu.VMEM((2 * rows, 8 * num_vecs), BF16),
            pltpu.VMEM((8 * num_vecs, cols), BF16),
        ],
        compiler_params=pltpu.CompilerParams(vmem_limit_bytes=32 * 2**20),
        name="chain",
    )(me, directions, spin_mats, chain_order, *operands)


def solution(mesh):
    in_specs = (
        P("gx", "gy", "gz", None, None, None),
        P("gx", "gy", "gz", None, None, None, None),
        P(),
        P(),
        P(None, "gx", "gy"),
        P(None, "gx", "gy"),
        P("gz", None),
    )
    out_specs = P("gz", None, "gx", "gy")
    return jax.shard_map(
        on_device, mesh=mesh, in_specs=in_specs, out_specs=out_specs, check_vma=False
    )
```

```python
import functools
import math

import jax
import jax.numpy as jnp
from jax import lax
from jax.experimental import pallas as pl
from jax.experimental.pallas import tpu as pltpu
from jax.sharding import PartitionSpec as P

VMEM = pl.BlockSpec(memory_space=pltpu.VMEM)
SMEM = pl.BlockSpec(memory_space=pltpu.SMEM)
BF16 = jnp.bfloat16
F32 = jnp.float32


def passed_along(value, axis, steps):
    count = lax.axis_size(axis)
    pairs = [(source, (source + steps) % count) for source in range(count)]
    return lax.ppermute(value, axis, pairs)


def mm(left, right):
    return jnp.dot(left, right, preferred_element_type=F32)


def parts_of(value, divisor):
    quotient = jnp.floor((value + 0.5) * (1.0 / divisor))
    return quotient, value - quotient * divisor


def whole_numbers(shape, axis):
    return lax.broadcasted_iota(jnp.int32, shape, axis).astype(F32)


def chosen(condition):
    return jnp.where(condition, 1.0, 0.0)


def coordinates(index, extent):
    rest, third = parts_of(index, extent[2])
    first, second = parts_of(rest, extent[1])
    return [first, second, third]


def source_columns(extent, e):
    count = math.prod(extent)
    face = count // extent[e]
    inner = count - face if e == 0 else count
    total = 6 * (inner + face)
    column = whole_numbers((1, total), 1)
    beyond = chosen(column >= 6 * inner)
    site, left = parts_of(column - beyond * (6 * inner), 6)
    colour, part = parts_of(left, 2)
    within = coordinates(site, extent)
    if e == 0:
        within[0] = within[0] + 1
    flat = [n for d, n in enumerate(extent) if d != e]
    outer, last = parts_of(site, flat[1])
    edge = [outer, last]
    edge.insert(e, jnp.full_like(site, extent[e]))
    where = [w + beyond * (o - w) for w, o in zip(within, edge)]
    return total, part, where, colour


def first_kernel(extent, z_ref, fwd_ref, bwd_ref, eig_ref, fwd_out, bwd_out, vec_out, *face_outs):
    vec = eig_ref[...].astype(F32).reshape(vec_out.shape)
    vec_out[...] = vec.astype(BF16)
    strides = (6 * extent[1] * extent[2], 6 * extent[2], 6)
    for e, out in enumerate(face_outs):
        begins = [0]
        for d in range(e):
            begins = [at + n * strides[d] for at in begins for n in range(extent[d])]
        runs = [vec[at : at + strides[e]] for at in begins]
        out[...] = (jnp.concatenate(runs, axis=0) if e else runs[0]).astype(BF16)
    rows, cols = fwd_ref.shape[1:]
    piece = fwd_out.shape[1]
    per_spin = rows // 4
    lane = cols // 4
    flat = lax.broadcasted_iota(jnp.int32, (piece, 1), 0) + z_ref[0] * piece
    spin = jnp.zeros_like(flat)
    for t in range(1, 4):
        spin += jnp.where(flat >= t * per_spin, 1, 0)
    source = 4 * (flat - spin * per_spin) + spin
    select = chosen(lax.broadcasted_iota(jnp.int32, (piece, rows), 1) == source).astype(BF16)
    column = lax.broadcasted_iota(jnp.int32, (1, cols), 1)
    spin = jnp.zeros_like(column)
    for t in range(1, 4):
        spin += jnp.where(column >= t * lane, 1, 0)
    source = 4 * (column - spin * lane) + spin
    perm = chosen(lax.broadcasted_iota(jnp.int32, (cols, cols), 0) == source).astype(BF16)
    for c in range(2):
        picked = mm(select, fwd_ref[c]).astype(BF16)
        fwd_out[c] = mm(picked, perm).astype(BF16)
        bwd_out[c] = mm(select, bwd_ref[c]).astype(BF16)


def links_kernel(extent, link_ref, *outs):
    count = math.prod(extent)
    rows = 6 * count
    row = whole_numbers((rows, 1), 0)
    row_site, left = parts_of(row, 6)
    row_colour, row_part = parts_of(left, 2)
    row_where = coordinates(row_site, extent)
    link = link_ref[...]
    high = link.astype(BF16)
    rest = link - high.astype(F32)
    mid = rest.astype(BF16)
    low = (rest - mid.astype(F32)).astype(BF16)
    spread = chosen(row_site == whole_numbers((rows, count), 1)).astype(BF16)
    by_row = [mm(spread, part) for part in (high, mid, low)]
    by_row = [jnp.concatenate([part, part], axis=1) for part in by_row]

    def entry_of(entry):
        half = chosen(entry >= 54)
        direction, left = parts_of(entry - 54 * half, 18)
        part, left = parts_of(left, 9)
        into, out_of = parts_of(left, 3)
        return half, direction, part, into, out_of

    half, direction, _, into, _ = entry_of(whole_numbers((1, 108), 1))
    own_part = (half == row_part) & (into == row_colour)
    place_half, _, place_part, _, place_colour = entry_of(whole_numbers((108, 1), 0))
    for e, out in enumerate(outs):
        keep = chosen(own_part & (direction == e))
        picked = jnp.concatenate([part * keep for part in by_row], axis=0).astype(BF16)
        total, part, where, colour = source_columns(extent, e)
        sign = 1.0 - 2.0 * part * (1.0 - place_half)
        match = (place_colour == colour) & (jnp.abs(place_part - part) == place_half)
        placed = mm(picked, jnp.where(match, sign, 0.0).astype(BF16))
        same = None
        for d in range(3):
            hit = row_where[d] + (1.0 if d == e else 0.0) == where[d]
            same = hit if same is None else same & hit
        mask = chosen(same)
        for n in range(3):
            at = slice(n * rows, (n + 1) * rows)
            out[at, :] = (placed[at] * mask).astype(BF16)


def correlate_kernel(scale, vec_ref, face0, face1, face2, mat0, mat1, mat2, out_ref):
    gz_n, gx_n, split, depth, width = out_ref.shape
    each = 6 // split
    own_rows = depth // each
    vec = vec_ref[...]
    rows = vec.shape[0]
    row = lax.broadcasted_iota(jnp.int32, (rows, rows), 0)
    column = lax.broadcasted_iota(jnp.int32, (rows, rows), 1)
    odd = lax.rem(row, 2) == 1
    turn = jnp.where(odd & (column == row - 1), -1.0, chosen((column == row + 1) & ~odd)).astype(BF16)
    sources = [
        jnp.concatenate([vec[face0.shape[0] :], face0[...]], axis=0),
        jnp.concatenate([vec, face1[...]], axis=0),
        jnp.concatenate([vec, face2[...]], axis=0),
    ]
    for e, mat in enumerate((mat0, mat1, mat2)):
        terms = mm(mat[...], sources[e])
        moved = terms[:rows] + terms[rows : 2 * rows] + terms[2 * rows :]
        moved = moved.astype(BF16)
        turned = mm(turn, moved).astype(BF16)
        right = jnp.concatenate([moved, turned], axis=1)
        product = lax.dot_general(
            vec, right, (((0,), (0,)), ((), ())), preferred_element_type=F32
        )
        product = (product * scale).astype(BF16)
        for c in range(2):
            n = 2 * e + c
            half = product[:, c * width : (c + 1) * width]
            to = slice(n % each * own_rows, (n % each + 1) * own_rows)
            for g in range(gx_n):
                for z in range(gz_n):
                    at = (g * gz_n + z) * own_rows
                    out_ref[z, g, n // each, to] = half[at : at + own_rows]


def chain_kernel(inverse, plan, me_ref, dirs_ref, spin_ref, chain_ref, *refs):
    line, elem_keys, fwd_keys, bwd_keys = plan
    elem_in, refs = refs[:2], refs[2:]
    fwd_in, refs = refs[: len(fwd_keys)], refs[len(fwd_keys) :]
    bwd_in, refs = refs[: len(bwd_keys)], refs[len(bwd_keys) :]
    out_ref, elem_all, elem_ref, x_ref, p_ref, q_ref, b_ref = refs
    gx_n, gz_n, split, depth, num_vecs = elem_all.shape
    each = 6 // split
    own_rows = depth // each
    width = out_ref.shape[3]
    op_count = out_ref.shape[0]
    row_count = out_ref.shape[2]
    vec_rows = row_count // 4
    gy_n = 4 * num_vecs // width
    lane = width // 4
    halves = gz_n // 4
    gx, gy, gz = me_ref[0], me_ref[1], me_ref[2]

    def back(at, step, count):
        return lax.rem(at - step + count, count)

    def gz_from(dy, dc):
        return back(lax.div(gz, 2), dy, gz_n // 2) * 2 + back(lax.rem(gz, 2), dc, 2)

    for dc, ref in enumerate(elem_in):
        for n, (dx, dy) in enumerate(elem_keys):
            for place, offset in enumerate(line):
                to = lax.bitwise_xor(gx, offset), gz_from(dy, dc), back(gy, dx, gy_n) if split > 1 else 0
                elem_all[to] = ref[n, place]
    column = lax.broadcasted_iota(jnp.int32, (1, num_vecs), 1)
    source = jnp.zeros_like(column)
    half_rows = vec_rows // halves
    for place, offset in enumerate(line):
        for half in range(halves):
            at = place * vec_rows + half * half_rows
            from_half = lax.bitwise_xor(lax.rem(gz, 2), half) if halves == 2 else half
            begin = lax.bitwise_xor(gx, offset) * vec_rows + from_half * half_rows
            inside = (column >= at) & (column < at + half_rows)
            source = jnp.where(inside, column + (begin - at), source)
    perm = chosen(lax.broadcasted_iota(jnp.int32, (num_vecs, num_vecs), 0) == source).astype(BF16)
    for n in range(6):
        rows = slice(n % each * own_rows, (n % each + 1) * own_rows)
        whole = elem_all[:, :, n // each, rows].reshape(num_vecs, num_vecs)
        elem_ref[n] = mm(whole, perm).astype(BF16)

    if halves == 1:
        groups = [[key] for key in bwd_keys]
    else:
        groups = [[(dy, dc) for dc in range(2)] for dy in range(gz_n // 2)]
    spins = [lax.div(gz_from(*group[0]), halves) for group in groups]

    def rows_of(parts, c):
        return jnp.concatenate([part[:, c] for part in parts], axis=1).reshape(num_vecs, width)

    first_row = pl.multiple_of(gx * vec_rows, vec_rows)

    def own(d, c):
        return elem_ref[2 * d + c, pl.ds(first_row, vec_rows), :]

    real_rows = [jnp.concatenate([own(d, 0), -own(d, 1)], axis=1) for d in range(3)]
    imag_rows = [jnp.concatenate([own(d, 1), own(d, 0)], axis=1) for d in range(3)]
    left = jnp.concatenate([part for d in range(3) for part in (real_rows[d], imag_rows[d])], axis=0)
    fwd_at = dict(zip(fwd_keys, fwd_in))
    bwd_at = dict(zip(bwd_keys, bwd_in))
    for t, group in enumerate(groups):
        for dx in range(gy_n):
            parts = [fwd_at[(dx,) + key] for key in group]
            right = jnp.concatenate([rows_of(parts, c) for c in range(2)], axis=0)
            result = mm(left, right).astype(BF16)
            for d in range(3):
                for c in range(2):
                    at = (d * 2 + c) * vec_rows
                    x_ref[d, c, dx, t] = result[at : at + vec_rows]
        for c in range(2):
            at = (t * 2 + c) * num_vecs
            b_ref[at : at + num_vecs, :] = rows_of([bwd_at[key] for key in group], c)

    row = lax.broadcasted_iota(jnp.int32, (row_count, row_count), 0)
    column = lax.broadcasted_iota(jnp.int32, (row_count, row_count), 1)
    row_spin = lax.rem(row, 4)
    diagonal = lax.div(row, 4) == lax.rem(column, vec_rows)
    column_spin = lax.div(column, vec_rows)
    blocks = [pl.multiple_of(back(gy, dx, gy_n) * lane, lane) for dx in range(gy_n)]

    def one_operator(op, carry):
        a = chain_ref[op, 0]
        b = chain_ref[op, 1]
        dir_a = dirs_ref[a]
        dir_b = dirs_ref[b]
        mix = jnp.zeros((row_count, row_count), F32)
        for t in range(4):
            in_t = column_spin == t
            for s in range(4):
                mix = jnp.where(in_t & (row_spin == s), spin_ref[a, s, spins[t]], mix)
        mix = jnp.where(diagonal, mix, 0.0)
        high = mix.astype(BF16)
        low = (mix - high.astype(F32)).astype(BF16)
        mix = jnp.concatenate([high, low], axis=1)
        for c in range(2):
            for dx in range(gy_n):
                source = x_ref[dir_a, c, dx].reshape(row_count, width)
                result = mm(mix, jnp.concatenate([source, source], axis=0)).astype(BF16)
                for s in range(4):
                    to = c * num_vecs + dx * lane
                    p_ref[s, :, to : to + lane] = result[:, s * lane : (s + 1) * lane]

        def elem(c):
            return jnp.concatenate([elem_ref[2 * dir_b + c, pl.ds(at, lane), :] for at in blocks], axis=0)

        real_b, imag_b = elem(0), elem(1)
        right = jnp.concatenate(
            [
                jnp.concatenate([real_b, imag_b], axis=1),
                jnp.concatenate([-imag_b, real_b], axis=1),
            ],
            axis=0,
        )
        parts = [mm(p_ref[s], right) for s in range(4)]
        for t in range(4):
            total = parts[0] * (spin_ref[b, 0, spins[t]] * inverse)
            for s in range(1, 4):
                total += parts[s] * (spin_ref[b, s, spins[t]] * inverse)
            total = total.astype(BF16)
            real, imag = total[:, :num_vecs], total[:, num_vecs:]
            at = 2 * t * num_vecs
            q_ref[:row_count, at : at + num_vecs] = real
            q_ref[:row_count, at + num_vecs : at + 2 * num_vecs] = -imag
            q_ref[row_count:, at : at + num_vecs] = imag
            q_ref[row_count:, at + num_vecs : at + 2 * num_vecs] = real
        final = mm(q_ref[...], b_ref[...]).astype(BF16)
        out_ref[op, 0] = final[:row_count]
        out_ref[op, 1] = final[row_count:]
        return carry

    lax.fori_loop(0, op_count, one_operator, 0)


def passed_in_gz(value, dy, dc):
    count = lax.axis_size("gz")
    chips = count // 2
    pairs = [(n, ((n // 2 + dy) % chips) * 2 + (n + dc) % 2) for n in range(count)]
    return lax.ppermute(value, "gz", pairs)


def passed_in_plane(value, dx, dy):
    if not dx and not dy:
        return value
    gy_n, gz_n = lax.axis_size("gy"), lax.axis_size("gz")
    chips = gz_n // 2
    pairs = []
    for y in range(gy_n):
        for z in range(gz_n):
            to = (y + dx) % gy_n * gz_n + ((z // 2 + dy) % chips) * 2 + z % 2
            pairs.append((y * gz_n + z, to))
    return lax.ppermute(value, ("gy", "gz"), pairs)


def line_exchange(value, axis, distance, steps, offsets=(0,)):
    count = lax.axis_size(axis)
    gathered = value if len(offsets) > 1 else value[None]
    offsets = list(offsets)
    for _ in range(steps):
        pairs = [(n, n ^ distance) for n in range(count)]
        gathered = jnp.concatenate([gathered, lax.ppermute(gathered, axis, pairs)])
        offsets += [offset ^ distance for offset in offsets]
        distance //= 2
    return gathered, tuple(offsets)


def part_at(value, index, axis=0):
    return lax.dynamic_index_in_dim(value, index, axis, keepdims=False)


def added(*values):
    return sum(value.astype(F32) for value in values).astype(BF16)


def on_device(eigvecs, links, directions, spin_mats, forward_peram, backward_peram, chain_order):
    extent = eigvecs.shape[:3]
    num_vecs = eigvecs.shape[-1]
    gx_n, gy_n, gz_n = (lax.axis_size(name) for name in ("gx", "gy", "gz"))
    chips = gz_n // 2
    gx, gy, gz = (lax.axis_index(name).astype(jnp.int32) for name in ("gx", "gy", "gz"))
    me = jnp.stack([gx, gy, gz])
    chip, core = lax.div(gz, 2), lax.rem(gz, 2)

    rows, cols = forward_peram.shape[1:]
    piece = rows // gz_n
    site_rows = 6 * math.prod(extent)
    face_rows = [site_rows // n for n in extent]
    piece_shape = jax.ShapeDtypeStruct((2, piece, cols), BF16)
    fwd_piece, bwd_piece, vec, *faces = pl.pallas_call(
        functools.partial(first_kernel, extent),
        out_shape=[piece_shape, piece_shape]
        + [jax.ShapeDtypeStruct((n, num_vecs), BF16) for n in [site_rows] + face_rows],
        in_specs=[SMEM] + [VMEM] * 3,
        out_specs=[VMEM] * 6,
        compiler_params=pltpu.CompilerParams(vmem_limit_bytes=24 * 2**20),
        name="first",
    )(me[2:], forward_peram, backward_peram, eigvecs.transpose(0, 1, 2, 4, 3, 5).reshape(-1, 2, num_vecs))
    faces = [passed_along(face, axis, -1) for face, axis in zip(faces, ("gx", "gy", "gz"))]

    fwd_piece, link_rows = lax.optimization_barrier((fwd_piece, links.reshape(-1, 54)))
    fwd_line, line = line_exchange(fwd_piece, "gx", gx_n // 2, 1)

    link_mats = pl.pallas_call(
        functools.partial(links_kernel, extent),
        out_shape=[
            jax.ShapeDtypeStruct((3 * site_rows, site_rows - (0 if e else face_rows[0]) + face_rows[e]), BF16)
            for e in range(3)
        ],
        in_specs=[VMEM],
        out_specs=[VMEM] * 3,
        compiler_params=pltpu.CompilerParams(vmem_limit_bytes=24 * 2**20),
        name="link_matrices",
    )(link_rows)

    volume = math.prod(extent) * gx_n * gy_n * gz_n
    own_rows = num_vecs // (gz_n * gx_n)
    split = gy_n if 6 % gy_n == 0 and own_rows % 16 == 0 else 1
    depth = 6 * own_rows // split
    partial = pl.pallas_call(
        functools.partial(correlate_kernel, 1.0 / math.sqrt(12.0 * volume)),
        out_shape=jax.ShapeDtypeStruct((gz_n, gx_n, split, depth, num_vecs), BF16),
        in_specs=[VMEM] * 7,
        out_specs=VMEM,
        compiler_params=pltpu.CompilerParams(vmem_limit_bytes=24 * 2**20),
        name="correlate",
    )(vec, *faces, *link_mats)

    by_core = partial.reshape((chips, 2) + partial.shape[1:])
    summed = added(part_at(by_core, core, 1), passed_in_gz(part_at(by_core, 1 - core, 1), 0, 1))
    summed, fwd_line = lax.optimization_barrier((summed, fwd_line))
    rounds = gx_n.bit_length() - 1
    fwd_line, line = line_exchange(fwd_line, "gx", gx_n // 4, rounds - 1, line)
    plane = [(dx, dy) for dy in range(chips) for dx in range(gy_n)]

    def plane_part(dx, dy):
        part = part_at(summed, lax.rem(chip + dy, chips))
        return part_at(part, lax.rem(gy + dx, gy_n) if split > 1 else 0, 1)

    summed = added(*[passed_in_plane(plane_part(dx, dy), dx, dy) for dx, dy in plane])
    summed, fwd_line, bwd_piece = lax.optimization_barrier((summed, fwd_line, bwd_piece))
    fwd_parts = {(dx, dy, 0): passed_in_plane(fwd_line, dx, dy) for dx, dy in plane}
    bwd_line, _ = line_exchange(bwd_piece, "gx", gx_n // 2, rounds)
    bwd_parts = {(dy, 0): passed_in_gz(bwd_line, dy, 0) if dy else bwd_line for dy in range(chips)}
    for dx, dy in plane:
        fwd_parts[dx, dy, 1] = passed_in_gz(fwd_parts[dx, dy, 0], 0, 1)
    for dy in range(chips):
        bwd_parts[dy, 1] = passed_in_gz(bwd_parts[dy, 0], 0, 1)
    distance = gx_n // 2
    while distance:
        halves = summed.reshape((2, distance) + summed.shape[1:])
        bit = lax.rem(lax.div(gx, distance), 2)
        pairs = [(n, n ^ distance) for n in range(gx_n)]
        summed = added(part_at(halves, bit), lax.ppermute(part_at(halves, 1 - bit), "gx", pairs))
        distance //= 2
    elem_line, _ = line_exchange(summed[0], "gx", gx_n // 2, rounds)
    elem_keys = plane if split > 1 else [(0, dy) for dy in range(chips)]
    elem_own = jnp.stack([passed_in_plane(elem_line, dx, dy) for dx, dy in elem_keys])
    elem_parts = [elem_own, passed_in_gz(elem_own, 0, 1)]

    op_count = chain_order.shape[0]
    plan = (line, tuple(elem_keys), tuple(fwd_parts), tuple(bwd_parts))
    operands = [*elem_parts, *fwd_parts.values(), *bwd_parts.values()]
    return pl.pallas_call(
        functools.partial(chain_kernel, 1.0 / math.sqrt(4 * num_vecs), plan),
        out_shape=jax.ShapeDtypeStruct((op_count, 2, rows, cols), BF16),
        in_specs=[SMEM] * 4 + [VMEM] * len(operands),
        out_specs=VMEM,
        scratch_shapes=[
            pltpu.VMEM((gx_n, gz_n, split, depth, num_vecs), BF16),
            pltpu.VMEM((6, num_vecs, num_vecs), BF16),
            pltpu.VMEM((3, 2, gy_n, 4, rows // 4, cols), BF16),
            pltpu.VMEM((4, rows, 2 * num_vecs), BF16),
            pltpu.VMEM((2 * rows, 8 * num_vecs), BF16),
            pltpu.VMEM((8 * num_vecs, cols), BF16),
        ],
        compiler_params=pltpu.CompilerParams(vmem_limit_bytes=32 * 2**20),
        name="chain",
    )(me, directions, spin_mats, chain_order, *operands)


def solution(mesh):
    in_specs = (
        P("gx", "gy", "gz", None, None, None),
        P("gx", "gy", "gz", None, None, None, None),
        P(),
        P(),
        P(None, "gx", "gy"),
        P(None, "gx", "gy"),
        P("gz", None),
    )
    out_specs = P("gz", None, "gx", "gy")
    return jax.shard_map(
        on_device, mesh=mesh, in_specs=in_specs, out_specs=out_specs, check_vma=False
    )
```

```python
import functools
import math

import jax
import jax.numpy as jnp
from jax import lax
from jax.experimental import pallas as pl
from jax.experimental.pallas import tpu as pltpu
from jax.sharding import PartitionSpec as P

VMEM = pl.BlockSpec(memory_space=pltpu.VMEM)
SMEM = pl.BlockSpec(memory_space=pltpu.SMEM)
BF16 = jnp.bfloat16
F32 = jnp.float32


def passed_along(value, axis, steps):
    count = lax.axis_size(axis)
    pairs = [(source, (source + steps) % count) for source in range(count)]
    return lax.ppermute(value, axis, pairs)


def mm(left, right):
    return jnp.dot(left, right, preferred_element_type=F32)


def parts_of(value, divisor):
    quotient = jnp.floor((value + 0.5) * (1.0 / divisor))
    return quotient, value - quotient * divisor


def whole_numbers(shape, axis):
    return lax.broadcasted_iota(jnp.int32, shape, axis).astype(F32)


def chosen(condition):
    return jnp.where(condition, 1.0, 0.0)


def coordinates(index, extent):
    rest, third = parts_of(index, extent[2])
    first, second = parts_of(rest, extent[1])
    return [first, second, third]


def source_columns(extent, e):
    count = math.prod(extent)
    face = count // extent[e]
    inner = count - face if e == 0 else count
    total = 6 * (inner + face)
    column = whole_numbers((1, total), 1)
    beyond = chosen(column >= 6 * inner)
    site, left = parts_of(column - beyond * (6 * inner), 6)
    colour, part = parts_of(left, 2)
    within = coordinates(site, extent)
    if e == 0:
        within[0] = within[0] + 1
    flat = [n for d, n in enumerate(extent) if d != e]
    outer, last = parts_of(site, flat[1])
    edge = [outer, last]
    edge.insert(e, jnp.full_like(site, extent[e]))
    where = [w + beyond * (o - w) for w, o in zip(within, edge)]
    return total, part, where, colour


def first_kernel(extent, z_ref, fwd_in, bwd_in, eig_in, fwd_out, bwd_out, vec_out, *refs):
    face_outs, (fwd_ref, bwd_ref, eig_ref, sems) = refs[:3], refs[3:]
    pairs = ((eig_in, eig_ref), (fwd_in, fwd_ref), (bwd_in, bwd_ref))
    copies = [pltpu.make_async_copy(source, target, sems.at[n]) for n, (source, target) in enumerate(pairs)]
    for copy in copies:
        copy.start()
    copies[0].wait()
    vec = eig_ref[...].astype(F32).reshape(vec_out.shape)
    vec_out[...] = vec.astype(BF16)
    strides = (6 * extent[1] * extent[2], 6 * extent[2], 6)
    for e, out in enumerate(face_outs):
        begins = [0]
        for d in range(e):
            begins = [at + n * strides[d] for at in begins for n in range(extent[d])]
        runs = [vec[at : at + strides[e]] for at in begins]
        out[...] = (jnp.concatenate(runs, axis=0) if e else runs[0]).astype(BF16)
    rows, cols = fwd_ref.shape[1:]
    piece = fwd_out.shape[1]
    per_spin = rows // 4
    lane = cols // 4
    flat = lax.broadcasted_iota(jnp.int32, (piece, 1), 0) + z_ref[0] * piece
    spin = jnp.zeros_like(flat)
    for t in range(1, 4):
        spin += jnp.where(flat >= t * per_spin, 1, 0)
    source = 4 * (flat - spin * per_spin) + spin
    select = chosen(lax.broadcasted_iota(jnp.int32, (piece, rows), 1) == source).astype(BF16)
    column = lax.broadcasted_iota(jnp.int32, (1, cols), 1)
    spin = jnp.zeros_like(column)
    for t in range(1, 4):
        spin += jnp.where(column >= t * lane, 1, 0)
    source = 4 * (column - spin * lane) + spin
    perm = chosen(lax.broadcasted_iota(jnp.int32, (cols, cols), 0) == source).astype(BF16)
    copies[1].wait()
    for c in range(2):
        picked = mm(select, fwd_ref[c]).astype(BF16)
        fwd_out[c] = mm(picked, perm).astype(BF16)
    copies[2].wait()
    for c in range(2):
        bwd_out[c] = mm(select, bwd_ref[c]).astype(BF16)


def links_kernel(extent, link_ref, *outs):
    count = math.prod(extent)
    rows = 6 * count
    row = whole_numbers((rows, 1), 0)
    row_site, left = parts_of(row, 6)
    row_colour, row_part = parts_of(left, 2)
    row_where = coordinates(row_site, extent)
    link = link_ref[...]
    high = link.astype(BF16)
    rest = link - high.astype(F32)
    mid = rest.astype(BF16)
    low = (rest - mid.astype(F32)).astype(BF16)
    spread = chosen(row_site == whole_numbers((rows, count), 1)).astype(BF16)
    by_row = [mm(spread, part) for part in (high, mid, low)]
    by_row = [jnp.concatenate([part, part], axis=1) for part in by_row]

    def entry_of(entry):
        half = chosen(entry >= 54)
        direction, left = parts_of(entry - 54 * half, 18)
        part, left = parts_of(left, 9)
        into, out_of = parts_of(left, 3)
        return half, direction, part, into, out_of

    half, direction, _, into, _ = entry_of(whole_numbers((1, 108), 1))
    own_part = (half == row_part) & (into == row_colour)
    place_half, _, place_part, _, place_colour = entry_of(whole_numbers((108, 1), 0))
    for e, out in enumerate(outs):
        keep = chosen(own_part & (direction == e))
        picked = jnp.concatenate([part * keep for part in by_row], axis=0).astype(BF16)
        total, part, where, colour = source_columns(extent, e)
        sign = 1.0 - 2.0 * part * (1.0 - place_half)
        match = (place_colour == colour) & (jnp.abs(place_part - part) == place_half)
        placed = mm(picked, jnp.where(match, sign, 0.0).astype(BF16))
        same = None
        for d in range(3):
            hit = row_where[d] + (1.0 if d == e else 0.0) == where[d]
            same = hit if same is None else same & hit
        mask = chosen(same)
        for n in range(3):
            at = slice(n * rows, (n + 1) * rows)
            out[at, :] = (placed[at] * mask).astype(BF16)


def correlate_kernel(scale, vec_ref, face0, face1, face2, mat0, mat1, mat2, out_ref):
    gz_n, gx_n, split, depth, width = out_ref.shape
    each = 6 // split
    own_rows = depth // each
    vec = vec_ref[...]
    rows = vec.shape[0]
    row = lax.broadcasted_iota(jnp.int32, (rows, rows), 0)
    column = lax.broadcasted_iota(jnp.int32, (rows, rows), 1)
    odd = lax.rem(row, 2) == 1
    turn = jnp.where(odd & (column == row - 1), -1.0, chosen((column == row + 1) & ~odd)).astype(BF16)
    sources = [
        jnp.concatenate([vec[face0.shape[0] :], face0[...]], axis=0),
        jnp.concatenate([vec, face1[...]], axis=0),
        jnp.concatenate([vec, face2[...]], axis=0),
    ]
    for e, mat in enumerate((mat0, mat1, mat2)):
        terms = mm(mat[...], sources[e])
        moved = terms[:rows] + terms[rows : 2 * rows] + terms[2 * rows :]
        moved = moved.astype(BF16)
        turned = mm(turn, moved).astype(BF16)
        right = jnp.concatenate([moved, turned], axis=1)
        product = lax.dot_general(
            vec, right, (((0,), (0,)), ((), ())), preferred_element_type=F32
        )
        product = (product * scale).astype(BF16)
        for c in range(2):
            n = 2 * e + c
            half = product[:, c * width : (c + 1) * width]
            to = slice(n % each * own_rows, (n % each + 1) * own_rows)
            for g in range(gx_n):
                for z in range(gz_n):
                    at = (g * gz_n + z) * own_rows
                    out_ref[z, g, n // each, to] = half[at : at + own_rows]


def spin_groups(gz_n):
    keys = [(dy, dc) for dc in range(2) for dy in range(gz_n // 2)]
    if gz_n == 4:
        return [[key] for key in keys]
    return [[(dy, dc) for dc in range(2)] for dy in range(gz_n // 2)]


def rows_of(parts, c, count):
    rows = jnp.concatenate([part[:, c] for part in parts], axis=1)
    return rows.reshape(count, rows.shape[-1])


def right_kernel(gz_n, keys, left_ref, *refs):
    bwd_at = dict(zip(keys, refs))
    out_ref, b_ref = refs[len(keys) :]
    num_vecs = b_ref.shape[0] // 8
    op_count, _, row_count, width = out_ref.shape
    for t, group in enumerate(spin_groups(gz_n)):
        real, imag = [rows_of([bwd_at[key] for key in group], c, num_vecs) for c in range(2)]
        at = 2 * t * num_vecs
        b_ref[at : at + num_vecs, :width] = real
        b_ref[at : at + num_vecs, width:] = imag
        b_ref[at + num_vecs : at + 2 * num_vecs, :width] = -imag
        b_ref[at + num_vecs : at + 2 * num_vecs, width:] = real
    left = left_ref[...].reshape(op_count * row_count, 8 * num_vecs)
    block = min(width, 256)
    for c in range(2):
        for begin in range(0, width, block):
            at = c * width + begin
            result = mm(left, b_ref[:, at : at + block]).astype(BF16)
            out_ref[:, c, :, begin : begin + block] = result.reshape(op_count, row_count, block)


def left_kernel(inverse, plan, me_ref, dirs_ref, spin_ref, chain_ref, *refs):
    line, elem_keys, fwd_keys = plan
    elem_in, refs = refs[:2], refs[2:]
    fwd_in, refs = refs[: len(fwd_keys)], refs[len(fwd_keys) :]
    out_ref, elem_all, elem_ref, x_ref, p_ref = refs
    gx_n, gz_n, split, depth, num_vecs = elem_all.shape
    each = 6 // split
    own_rows = depth // each
    width = fwd_in[0].shape[3]
    op_count, row_count, _ = out_ref.shape
    vec_rows = row_count // 4
    gy_n = 4 * num_vecs // width
    lane = width // 4
    halves = gz_n // 4
    gx, gy, gz = me_ref[0], me_ref[1], me_ref[2]

    def back(at, step, count):
        return lax.rem(at - step + count, count)

    def gz_from(dy, dc):
        return back(lax.div(gz, 2), dy, gz_n // 2) * 2 + back(lax.rem(gz, 2), dc, 2)

    for dc, ref in enumerate(elem_in):
        for n, (dx, dy) in enumerate(elem_keys):
            for place, offset in enumerate(line):
                to = lax.bitwise_xor(gx, offset), gz_from(dy, dc), back(gy, dx, gy_n) if split > 1 else 0
                elem_all[to] = ref[n, place]
    column = lax.broadcasted_iota(jnp.int32, (1, num_vecs), 1)
    source = jnp.zeros_like(column)
    half_rows = vec_rows // halves
    for place, offset in enumerate(line):
        for half in range(halves):
            at = place * vec_rows + half * half_rows
            from_half = lax.bitwise_xor(lax.rem(gz, 2), half) if halves == 2 else half
            begin = lax.bitwise_xor(gx, offset) * vec_rows + from_half * half_rows
            inside = (column >= at) & (column < at + half_rows)
            source = jnp.where(inside, column + (begin - at), source)
    perm = chosen(lax.broadcasted_iota(jnp.int32, (num_vecs, num_vecs), 0) == source).astype(BF16)
    for n in range(6):
        rows = slice(n % each * own_rows, (n % each + 1) * own_rows)
        whole = elem_all[:, :, n // each, rows].reshape(num_vecs, num_vecs)
        elem_ref[n] = mm(whole, perm).astype(BF16)

    groups = spin_groups(gz_n)
    spins = [lax.div(gz_from(*group[0]), halves) for group in groups]

    first_row = pl.multiple_of(gx * vec_rows, vec_rows)

    def own(d, c):
        return elem_ref[2 * d + c, pl.ds(first_row, vec_rows), :]

    real_rows = [jnp.concatenate([own(d, 0), -own(d, 1)], axis=1) for d in range(3)]
    imag_rows = [jnp.concatenate([own(d, 1), own(d, 0)], axis=1) for d in range(3)]
    left = jnp.concatenate([part for d in range(3) for part in (real_rows[d], imag_rows[d])], axis=0)
    fwd_at = dict(zip(fwd_keys, fwd_in))
    for t, group in enumerate(groups):
        for dx in range(gy_n):
            parts = [fwd_at[(dx,) + key] for key in group]
            right = jnp.concatenate([rows_of(parts, c, num_vecs) for c in range(2)], axis=0)
            result = mm(left, right).astype(BF16)
            for d in range(3):
                for c in range(2):
                    at = (d * 2 + c) * vec_rows
                    x_ref[d, c, dx, t] = result[at : at + vec_rows]

    row = lax.broadcasted_iota(jnp.int32, (row_count, row_count), 0)
    column = lax.broadcasted_iota(jnp.int32, (row_count, row_count), 1)
    row_spin = lax.rem(row, 4)
    diagonal = lax.div(row, 4) == lax.rem(column, vec_rows)
    column_spin = lax.div(column, vec_rows)
    blocks = [pl.multiple_of(back(gy, dx, gy_n) * lane, lane) for dx in range(gy_n)]

    def one_operator(op, carry):
        a = chain_ref[op, 0]
        b = chain_ref[op, 1]
        dir_a = dirs_ref[a]
        dir_b = dirs_ref[b]
        mix = jnp.zeros((row_count, row_count), F32)
        for t in range(4):
            in_t = column_spin == t
            for s in range(4):
                mix = jnp.where(in_t & (row_spin == s), spin_ref[a, s, spins[t]], mix)
        mix = jnp.where(diagonal, mix, 0.0)
        high = mix.astype(BF16)
        low = (mix - high.astype(F32)).astype(BF16)
        mix = jnp.concatenate([high, low], axis=1)
        for c in range(2):
            for dx in range(gy_n):
                source = x_ref[dir_a, c, dx].reshape(row_count, width)
                result = mm(mix, jnp.concatenate([source, source], axis=0)).astype(BF16)
                for s in range(4):
                    to = c * num_vecs + dx * lane
                    p_ref[s, :, to : to + lane] = result[:, s * lane : (s + 1) * lane]

        def elem(c):
            return jnp.concatenate([elem_ref[2 * dir_b + c, pl.ds(at, lane), :] for at in blocks], axis=0)

        real_b, imag_b = elem(0), elem(1)
        right = jnp.concatenate(
            [
                jnp.concatenate([real_b, imag_b], axis=1),
                jnp.concatenate([-imag_b, real_b], axis=1),
            ],
            axis=0,
        )
        parts = [mm(p_ref[s], right) for s in range(4)]
        for t in range(4):
            total = parts[0] * (spin_ref[b, 0, spins[t]] * inverse)
            for s in range(1, 4):
                total += parts[s] * (spin_ref[b, s, spins[t]] * inverse)
            total = total.astype(BF16)
            out_ref[op, :, 2 * t * num_vecs : 2 * (t + 1) * num_vecs] = total
        return carry

    lax.fori_loop(0, op_count, one_operator, 0)


def passed_in_gz(value, dy, dc):
    count = lax.axis_size("gz")
    chips = count // 2
    pairs = [(n, ((n // 2 + dy) % chips) * 2 + (n + dc) % 2) for n in range(count)]
    return lax.ppermute(value, "gz", pairs)


def passed_in_plane(value, dx, dy):
    if not dx and not dy:
        return value
    gy_n, gz_n = lax.axis_size("gy"), lax.axis_size("gz")
    chips = gz_n // 2
    pairs = []
    for y in range(gy_n):
        for z in range(gz_n):
            to = (y + dx) % gy_n * gz_n + ((z // 2 + dy) % chips) * 2 + z % 2
            pairs.append((y * gz_n + z, to))
    return lax.ppermute(value, ("gy", "gz"), pairs)


def line_exchange(value, axis, distance, steps, offsets=(0,)):
    count = lax.axis_size(axis)
    gathered = value if len(offsets) > 1 else value[None]
    offsets = list(offsets)
    for _ in range(steps):
        pairs = [(n, n ^ distance) for n in range(count)]
        gathered = jnp.concatenate([gathered, lax.ppermute(gathered, axis, pairs)])
        offsets += [offset ^ distance for offset in offsets]
        distance //= 2
    return gathered, tuple(offsets)


def part_at(value, index, axis=0):
    return lax.dynamic_index_in_dim(value, index, axis, keepdims=False)


def added(*values):
    return sum(value.astype(F32) for value in values).astype(BF16)


def on_device(eigvecs, links, directions, spin_mats, forward_peram, backward_peram, chain_order):
    extent = eigvecs.shape[:3]
    num_vecs = eigvecs.shape[-1]
    gx_n, gy_n, gz_n = (lax.axis_size(name) for name in ("gx", "gy", "gz"))
    chips = gz_n // 2
    gx, gy, gz = (lax.axis_index(name).astype(jnp.int32) for name in ("gx", "gy", "gz"))
    me = jnp.stack([gx, gy, gz])
    chip, core = lax.div(gz, 2), lax.rem(gz, 2)

    rows, cols = forward_peram.shape[1:]
    piece = rows // gz_n
    site_rows = 6 * math.prod(extent)
    face_rows = [site_rows // n for n in extent]
    piece_shape = jax.ShapeDtypeStruct((2, piece, cols), BF16)
    fwd_piece, bwd_piece, vec, *faces = pl.pallas_call(
        functools.partial(first_kernel, extent),
        out_shape=[piece_shape, piece_shape]
        + [jax.ShapeDtypeStruct((n, num_vecs), BF16) for n in [site_rows] + face_rows],
        in_specs=[SMEM] + [pl.BlockSpec(memory_space=pl.ANY)] * 3,
        out_specs=[VMEM] * 6,
        scratch_shapes=[
            pltpu.VMEM(forward_peram.shape, BF16),
            pltpu.VMEM(backward_peram.shape, BF16),
            pltpu.VMEM((site_rows // 2, 2, num_vecs), BF16),
            pltpu.SemaphoreType.DMA((3,)),
        ],
        compiler_params=pltpu.CompilerParams(vmem_limit_bytes=60 * 2**20),
        name="first",
    )(me[2:], forward_peram, backward_peram, eigvecs.transpose(0, 1, 2, 4, 3, 5).reshape(-1, 2, num_vecs))
    faces = [passed_along(face, axis, -1) for face, axis in zip(faces, ("gx", "gy", "gz"))]

    fwd_piece, link_rows = lax.optimization_barrier((fwd_piece, links.reshape(-1, 54)))
    fwd_line, line = line_exchange(fwd_piece, "gx", gx_n // 2, 1)

    link_mats = pl.pallas_call(
        functools.partial(links_kernel, extent),
        out_shape=[
            jax.ShapeDtypeStruct((3 * site_rows, site_rows - (0 if e else face_rows[0]) + face_rows[e]), BF16)
            for e in range(3)
        ],
        in_specs=[VMEM],
        out_specs=[VMEM] * 3,
        compiler_params=pltpu.CompilerParams(vmem_limit_bytes=24 * 2**20),
        name="link_matrices",
    )(link_rows)

    volume = math.prod(extent) * gx_n * gy_n * gz_n
    own_rows = num_vecs // (gz_n * gx_n)
    split = gy_n if 6 % gy_n == 0 and own_rows % 16 == 0 else 1
    depth = 6 * own_rows // split
    partial = pl.pallas_call(
        functools.partial(correlate_kernel, 1.0 / math.sqrt(12.0 * volume)),
        out_shape=jax.ShapeDtypeStruct((gz_n, gx_n, split, depth, num_vecs), BF16),
        in_specs=[VMEM] * 7,
        out_specs=VMEM,
        compiler_params=pltpu.CompilerParams(vmem_limit_bytes=24 * 2**20),
        name="correlate",
    )(vec, *faces, *link_mats)

    partial, fwd_line = lax.optimization_barrier((partial, fwd_line))
    by_core = partial.reshape((chips, 2) + partial.shape[1:])
    summed = added(part_at(by_core, core, 1), passed_in_gz(part_at(by_core, 1 - core, 1), 0, 1))
    rounds = gx_n.bit_length() - 1
    fwd_line, line = line_exchange(fwd_line, "gx", gx_n // 4, rounds - 1, line)
    plane = [(dx, dy) for dy in range(chips) for dx in range(gy_n)]

    def plane_part(dx, dy):
        part = part_at(summed, lax.rem(chip + dy, chips))
        return part_at(part, lax.rem(gy + dx, gy_n) if split > 1 else 0, 1)

    summed = added(*[passed_in_plane(plane_part(dx, dy), dx, dy) for dx, dy in plane])
    summed, fwd_line, bwd_piece = lax.optimization_barrier((summed, fwd_line, bwd_piece))

    four = gy_n == 2 and chips == 2
    fwd_parts = {(dx, dy, 0): passed_in_plane(fwd_line, dx, dy) for dx, dy in plane if not (four and dx and dy)}
    bwd_line, _ = line_exchange(bwd_piece, "gx", gx_n // 2, rounds)
    bwd_parts = {(dy, 0): passed_in_gz(bwd_line, dy, 0) if dy else bwd_line for dy in range(chips)}

    distance = gx_n // 2
    while distance:
        halves = summed.reshape((2, distance) + summed.shape[1:])
        bit = lax.rem(lax.div(gx, distance), 2)
        pairs = [(n, n ^ distance) for n in range(gx_n)]
        summed = added(part_at(halves, bit), lax.ppermute(part_at(halves, 1 - bit), "gx", pairs))
        distance //= 2
    elem_line, offsets = line_exchange(summed[0], "gx", gx_n // 2, rounds - 1)
    if four:
        over_x, over_y = fwd_parts[1, 0, 0], fwd_parts[0, 1, 0]
        elem_line, over_x, over_y = lax.optimization_barrier((elem_line, over_x, over_y))
        fwd_parts[1, 0, 0], fwd_parts[0, 1, 0] = over_x, over_y
        corner = [passed_in_plane(over_y[:, :1], 1, 0), passed_in_plane(over_x[:, 1:], 0, 1)]
        fwd_parts[1, 1, 0] = jnp.concatenate(corner, axis=1)
    elem_line, _ = line_exchange(elem_line, "gx", 1, 1, offsets)
    for dx, dy in plane:
        fwd_parts[dx, dy, 1] = passed_in_gz(fwd_parts[dx, dy, 0], 0, 1)
    for dy in range(chips):
        bwd_parts[dy, 1] = passed_in_gz(bwd_parts[dy, 0], 0, 1)
    elem_keys = plane if split > 1 else [(0, dy) for dy in range(chips)]
    elem_own = jnp.stack([passed_in_plane(elem_line, dx, dy) for dx, dy in elem_keys])
    elem_parts = [elem_own, passed_in_gz(elem_own, 0, 1)]

    op_count = chain_order.shape[0]
    plan = (line, tuple(elem_keys), tuple(fwd_parts))
    left_shape = (op_count, rows, 8 * num_vecs)
    left = pl.pallas_call(
        functools.partial(left_kernel, 1.0 / math.sqrt(4 * num_vecs), plan),
        out_shape=jax.ShapeDtypeStruct(left_shape, BF16),
        in_specs=[SMEM] * 4 + [VMEM] * (len(elem_parts) + len(fwd_parts)),
        out_specs=VMEM,
        scratch_shapes=[
            pltpu.VMEM((gx_n, gz_n, split, depth, num_vecs), BF16),
            pltpu.VMEM((6, num_vecs, num_vecs), BF16),
            pltpu.VMEM((3, 2, gy_n, 4, rows // 4, cols), BF16),
            pltpu.VMEM((4, rows, 2 * num_vecs), BF16),
        ],
        compiler_params=pltpu.CompilerParams(vmem_limit_bytes=24 * 2**20),
        cost_estimate=pl.CostEstimate(flops=8 * 10**9, bytes_accessed=10**7, transcendentals=0),
        name="left",
    )(me, directions, spin_mats, chain_order, *elem_parts, *fwd_parts.values())
    return pl.pallas_call(
        functools.partial(right_kernel, gz_n, tuple(bwd_parts)),
        out_shape=jax.ShapeDtypeStruct((op_count, 2, rows, cols), BF16),
        in_specs=[VMEM] * (1 + len(bwd_parts)),
        out_specs=VMEM,
        scratch_shapes=[pltpu.VMEM((8 * num_vecs, 2 * cols), BF16)],
        compiler_params=pltpu.CompilerParams(vmem_limit_bytes=24 * 2**20),
        name="right",
    )(left, *bwd_parts.values())


def solution(mesh):
    in_specs = (
        P("gx", "gy", "gz", None, None, None),
        P("gx", "gy", "gz", None, None, None, None),
        P(),
        P(),
        P(None, "gx", "gy"),
        P(None, "gx", "gy"),
        P("gz", None),
    )
    out_specs = P("gz", None, "gx", "gy")
    return jax.shard_map(
        on_device, mesh=mesh, in_specs=in_specs, out_specs=out_specs, check_vma=False
    )
```

```python
import functools
import math

import jax
import jax.numpy as jnp
from jax import lax
from jax.experimental import pallas as pl
from jax.experimental.pallas import tpu as pltpu
from jax.sharding import PartitionSpec as P

VMEM = pl.BlockSpec(memory_space=pltpu.VMEM)
SMEM = pl.BlockSpec(memory_space=pltpu.SMEM)
BF16 = jnp.bfloat16
F32 = jnp.float32


def passed_along(value, axis, steps):
    count = lax.axis_size(axis)
    pairs = [(source, (source + steps) % count) for source in range(count)]
    return lax.ppermute(value, axis, pairs)


def mm(left, right):
    return jnp.dot(left, right, preferred_element_type=F32)


def parts_of(value, divisor):
    quotient = jnp.floor((value + 0.5) * (1.0 / divisor))
    return quotient, value - quotient * divisor


def whole_numbers(shape, axis):
    return lax.broadcasted_iota(jnp.int32, shape, axis).astype(F32)


def chosen(condition):
    return jnp.where(condition, 1.0, 0.0)


def coordinates(index, extent):
    rest, third = parts_of(index, extent[2])
    first, second = parts_of(rest, extent[1])
    return [first, second, third]


def source_columns(extent, e):
    count = math.prod(extent)
    face = count // extent[e]
    inner = count - face if e == 0 else count
    total = 6 * (inner + face)
    column = whole_numbers((1, total), 1)
    beyond = chosen(column >= 6 * inner)
    site, left = parts_of(column - beyond * (6 * inner), 6)
    colour, part = parts_of(left, 2)
    within = coordinates(site, extent)
    if e == 0:
        within[0] = within[0] + 1
    flat = [n for d, n in enumerate(extent) if d != e]
    outer, last = parts_of(site, flat[1])
    edge = [outer, last]
    edge.insert(e, jnp.full_like(site, extent[e]))
    where = [w + beyond * (o - w) for w, o in zip(within, edge)]
    return total, part, where, colour


def rows_kernel(extent, eig_ref, vec_out, *face_outs):
    vec = eig_ref[...].astype(F32).reshape(vec_out.shape)
    vec_out[...] = vec.astype(BF16)
    strides = (6 * extent[1] * extent[2], 6 * extent[2], 6)
    for e, out in enumerate(face_outs):
        begins = [0]
        for d in range(e):
            begins = [at + n * strides[d] for at in begins for n in range(extent[d])]
        runs = [vec[at : at + strides[e]] for at in begins]
        out[...] = (jnp.concatenate(runs, axis=0) if e else runs[0]).astype(BF16)


def pieces_kernel(z_ref, fwd_in, bwd_in, both_out, fwd_ref, bwd_ref, sems):
    pairs = ((fwd_in, fwd_ref), (bwd_in, bwd_ref))
    copies = [pltpu.make_async_copy(source, target, sems.at[n]) for n, (source, target) in enumerate(pairs)]
    for copy in copies:
        copy.start()
    rows, cols = fwd_ref.shape[1:]
    piece = both_out.shape[2]
    per_spin = rows // 4
    lane = cols // 4
    flat = lax.broadcasted_iota(jnp.int32, (piece, 1), 0) + z_ref[0] * piece
    spin = jnp.zeros_like(flat)
    for t in range(1, 4):
        spin += jnp.where(flat >= t * per_spin, 1, 0)
    source = 4 * (flat - spin * per_spin) + spin
    select = chosen(lax.broadcasted_iota(jnp.int32, (piece, rows), 1) == source).astype(BF16)
    column = lax.broadcasted_iota(jnp.int32, (1, cols), 1)
    spin = jnp.zeros_like(column)
    for t in range(1, 4):
        spin += jnp.where(column >= t * lane, 1, 0)
    source = 4 * (column - spin * lane) + spin
    perm = chosen(lax.broadcasted_iota(jnp.int32, (cols, cols), 0) == source).astype(BF16)
    copies[0].wait()
    for c in range(2):
        picked = mm(select, fwd_ref[c]).astype(BF16)
        both_out[0, c] = mm(picked, perm).astype(BF16)
    copies[1].wait()
    for c in range(2):
        both_out[1, c] = mm(select, bwd_ref[c]).astype(BF16)


def links_kernel(extent, link_ref, *outs):
    count = math.prod(extent)
    rows = 6 * count
    row = whole_numbers((rows, 1), 0)
    row_site, left = parts_of(row, 6)
    row_colour, row_part = parts_of(left, 2)
    row_where = coordinates(row_site, extent)
    link = link_ref[...]
    high = link.astype(BF16)
    rest = link - high.astype(F32)
    mid = rest.astype(BF16)
    low = (rest - mid.astype(F32)).astype(BF16)
    spread = chosen(row_site == whole_numbers((rows, count), 1)).astype(BF16)
    by_row = [mm(spread, part) for part in (high, mid, low)]
    by_row = [jnp.concatenate([part, part], axis=1) for part in by_row]

    def entry_of(entry):
        half = chosen(entry >= 54)
        direction, left = parts_of(entry - 54 * half, 18)
        part, left = parts_of(left, 9)
        into, out_of = parts_of(left, 3)
        return half, direction, part, into, out_of

    half, direction, _, into, _ = entry_of(whole_numbers((1, 108), 1))
    own_part = (half == row_part) & (into == row_colour)
    place_half, _, place_part, _, place_colour = entry_of(whole_numbers((108, 1), 0))
    for e, out in enumerate(outs):
        keep = chosen(own_part & (direction == e))
        picked = jnp.concatenate([part * keep for part in by_row], axis=0).astype(BF16)
        total, part, where, colour = source_columns(extent, e)
        sign = 1.0 - 2.0 * part * (1.0 - place_half)
        match = (place_colour == colour) & (jnp.abs(place_part - part) == place_half)
        placed = mm(picked, jnp.where(match, sign, 0.0).astype(BF16))
        same = None
        for d in range(3):
            hit = row_where[d] + (1.0 if d == e else 0.0) == where[d]
            same = hit if same is None else same & hit
        mask = chosen(same)
        for n in range(3):
            at = slice(n * rows, (n + 1) * rows)
            out[at, :] = (placed[at] * mask).astype(BF16)


def correlate_kernel(scale, vec_ref, face0, face1, face2, mat0, mat1, mat2, out_ref):
    gz_n, gx_n, split, depth, width = out_ref.shape
    each = 6 // split
    own_rows = depth // each
    vec = vec_ref[...]
    rows = vec.shape[0]
    row = lax.broadcasted_iota(jnp.int32, (rows, rows), 0)
    column = lax.broadcasted_iota(jnp.int32, (rows, rows), 1)
    odd = lax.rem(row, 2) == 1
    turn = jnp.where(odd & (column == row - 1), -1.0, chosen((column == row + 1) & ~odd)).astype(BF16)
    sources = [
        jnp.concatenate([vec[face0.shape[0] :], face0[...]], axis=0),
        jnp.concatenate([vec, face1[...]], axis=0),
        jnp.concatenate([vec, face2[...]], axis=0),
    ]
    for e, mat in enumerate((mat0, mat1, mat2)):
        terms = mm(mat[...], sources[e])
        moved = terms[:rows] + terms[rows : 2 * rows] + terms[2 * rows :]
        moved = moved.astype(BF16)
        turned = mm(turn, moved).astype(BF16)
        right = jnp.concatenate([moved, turned], axis=1)
        product = lax.dot_general(
            vec, right, (((0,), (0,)), ((), ())), preferred_element_type=F32
        )
        product = (product * scale).astype(BF16)
        for c in range(2):
            n = 2 * e + c
            half = product[:, c * width : (c + 1) * width]
            to = slice(n % each * own_rows, (n % each + 1) * own_rows)
            for g in range(gx_n):
                for z in range(gz_n):
                    at = (g * gz_n + z) * own_rows
                    out_ref[z, g, n // each, to] = half[at : at + own_rows]


def spin_groups(gz_n):
    keys = [(dy, dc) for dc in range(2) for dy in range(gz_n // 2)]
    if gz_n == 4:
        return [[key] for key in keys]
    return [[(dy, dc) for dc in range(2)] for dy in range(gz_n // 2)]


def rows_of(parts, c, count):
    rows = jnp.concatenate([part[:, c] for part in parts], axis=1)
    return rows.reshape(count, rows.shape[-1])


def right_kernel(gz_n, keys, left_ref, *refs):
    bwd_at = dict(zip(keys, refs))
    out_ref, b_ref = refs[len(keys) :]
    num_vecs = b_ref.shape[0] // 8
    op_count, _, row_count, width = out_ref.shape
    for t, group in enumerate(spin_groups(gz_n)):
        real, imag = [rows_of([bwd_at[key] for key in group], c, num_vecs) for c in range(2)]
        at = 2 * t * num_vecs
        b_ref[at : at + num_vecs, :width] = real
        b_ref[at : at + num_vecs, width:] = imag
        b_ref[at + num_vecs : at + 2 * num_vecs, :width] = -imag
        b_ref[at + num_vecs : at + 2 * num_vecs, width:] = real
    left = left_ref[...].reshape(op_count * row_count, 8 * num_vecs)
    block = min(width, 256)
    for c in range(2):
        for begin in range(0, width, block):
            at = c * width + begin
            result = mm(left, b_ref[:, at : at + block]).astype(BF16)
            out_ref[:, c, :, begin : begin + block] = result.reshape(op_count, row_count, block)


def left_kernel(inverse, plan, me_ref, dirs_ref, spin_ref, chain_ref, *refs):
    line, elem_keys, fwd_keys = plan
    elem_in, refs = refs[:2], refs[2:]
    fwd_in, refs = refs[: len(fwd_keys)], refs[len(fwd_keys) :]
    out_ref, elem_all, elem_ref, x_ref, p_ref = refs
    gx_n, gz_n, split, depth, num_vecs = elem_all.shape
    each = 6 // split
    own_rows = depth // each
    width = fwd_in[0].shape[3]
    op_count, row_count, _ = out_ref.shape
    vec_rows = row_count // 4
    gy_n = 4 * num_vecs // width
    lane = width // 4
    halves = gz_n // 4
    gx, gy, gz = me_ref[0], me_ref[1], me_ref[2]

    def back(at, step, count):
        return lax.rem(at - step + count, count)

    def gz_from(dy, dc):
        return back(lax.div(gz, 2), dy, gz_n // 2) * 2 + back(lax.rem(gz, 2), dc, 2)

    for dc, ref in enumerate(elem_in):
        for n, (dx, dy) in enumerate(elem_keys):
            for place, offset in enumerate(line):
                to = lax.bitwise_xor(gx, offset), gz_from(dy, dc), back(gy, dx, gy_n) if split > 1 else 0
                elem_all[to] = ref[n, place]
    column = lax.broadcasted_iota(jnp.int32, (1, num_vecs), 1)
    source = jnp.zeros_like(column)
    half_rows = vec_rows // halves
    for place, offset in enumerate(line):
        for half in range(halves):
            at = place * vec_rows + half * half_rows
            from_half = lax.bitwise_xor(lax.rem(gz, 2), half) if halves == 2 else half
            begin = lax.bitwise_xor(gx, offset) * vec_rows + from_half * half_rows
            inside = (column >= at) & (column < at + half_rows)
            source = jnp.where(inside, column + (begin - at), source)
    perm = chosen(lax.broadcasted_iota(jnp.int32, (num_vecs, num_vecs), 0) == source).astype(BF16)
    for n in range(6):
        rows = slice(n % each * own_rows, (n % each + 1) * own_rows)
        whole = elem_all[:, :, n // each, rows].reshape(num_vecs, num_vecs)
        elem_ref[n] = mm(whole, perm).astype(BF16)

    groups = spin_groups(gz_n)
    spins = [lax.div(gz_from(*group[0]), halves) for group in groups]

    first_row = pl.multiple_of(gx * vec_rows, vec_rows)

    def own(d, c):
        return elem_ref[2 * d + c, pl.ds(first_row, vec_rows), :]

    real_rows = [jnp.concatenate([own(d, 0), -own(d, 1)], axis=1) for d in range(3)]
    imag_rows = [jnp.concatenate([own(d, 1), own(d, 0)], axis=1) for d in range(3)]
    left = jnp.concatenate([part for d in range(3) for part in (real_rows[d], imag_rows[d])], axis=0)
    fwd_at = dict(zip(fwd_keys, fwd_in))
    for t, group in enumerate(groups):
        for dx in range(gy_n):
            parts = [fwd_at[(dx,) + key] for key in group]
            right = jnp.concatenate([rows_of(parts, c, num_vecs) for c in range(2)], axis=0)
            result = mm(left, right).astype(BF16)
            for d in range(3):
                for c in range(2):
                    at = (d * 2 + c) * vec_rows
                    x_ref[d, c, dx, t] = result[at : at + vec_rows]

    row = lax.broadcasted_iota(jnp.int32, (row_count, 1), 0)
    column = lax.broadcasted_iota(jnp.int32, (1, row_count), 1)
    row_spin = lax.rem(row, 4)
    diagonal = lax.div(row, 4) == lax.rem(column, vec_rows)
    column_spin = lax.div(column, vec_rows)
    blocks = [pl.multiple_of(back(gy, dx, gy_n) * lane, lane) for dx in range(gy_n)]

    def one_operator(op):
        a = chain_ref[op, 0]
        b = chain_ref[op, 1]
        dir_a = dirs_ref[a]
        dir_b = dirs_ref[b]
        mix = None
        for t in range(4):
            weight = jnp.full((row_count, 1), spin_ref[a, 0, spins[t]])
            for s in range(1, 4):
                weight = jnp.where(row_spin == s, spin_ref[a, s, spins[t]], weight)
            mix = weight if mix is None else jnp.where(column_spin == t, weight, mix)
        mix = jnp.where(diagonal, mix, 0.0)
        high = mix.astype(BF16)
        low = (mix - high.astype(F32)).astype(BF16)
        mix = jnp.concatenate([high, low], axis=1)
        for c in range(2):
            for dx in range(gy_n):
                source = x_ref[dir_a, c, dx].reshape(row_count, width)
                result = mm(mix, jnp.concatenate([source, source], axis=0)).astype(BF16)
                for s in range(4):
                    to = c * num_vecs + dx * lane
                    p_ref[s, :, to : to + lane] = result[:, s * lane : (s + 1) * lane]

        def elem(c):
            return jnp.concatenate([elem_ref[2 * dir_b + c, pl.ds(at, lane), :] for at in blocks], axis=0)

        real_b, imag_b = elem(0), elem(1)
        right = jnp.concatenate(
            [
                jnp.concatenate([real_b, imag_b], axis=1),
                jnp.concatenate([-imag_b, real_b], axis=1),
            ],
            axis=0,
        )
        parts = [mm(p_ref[s], right) for s in range(4)]
        for t in range(4):
            total = parts[0] * (spin_ref[b, 0, spins[t]] * inverse)
            for s in range(1, 4):
                total += parts[s] * (spin_ref[b, s, spins[t]] * inverse)
            total = total.astype(BF16)
            out_ref[op, :, 2 * t * num_vecs : 2 * (t + 1) * num_vecs] = total

    for op in range(op_count):
        one_operator(op)


def passed_in_gz(value, dy, dc):
    count = lax.axis_size("gz")
    chips = count // 2
    pairs = [(n, ((n // 2 + dy) % chips) * 2 + (n + dc) % 2) for n in range(count)]
    return lax.ppermute(value, "gz", pairs)


def passed_in_plane(value, dx, dy):
    if not dx and not dy:
        return value
    gy_n, gz_n = lax.axis_size("gy"), lax.axis_size("gz")
    chips = gz_n // 2
    pairs = []
    for y in range(gy_n):
        for z in range(gz_n):
            to = (y + dx) % gy_n * gz_n + ((z // 2 + dy) % chips) * 2 + z % 2
            pairs.append((y * gz_n + z, to))
    return lax.ppermute(value, ("gy", "gz"), pairs)


def line_exchange(value, axis, distance, steps, offsets=(0,)):
    count = lax.axis_size(axis)
    gathered = value if len(offsets) > 1 else value[None]
    offsets = list(offsets)
    for _ in range(steps):
        pairs = [(n, n ^ distance) for n in range(count)]
        gathered = jnp.concatenate([gathered, lax.ppermute(gathered, axis, pairs)])
        offsets += [offset ^ distance for offset in offsets]
        distance //= 2
    return gathered, tuple(offsets)


def part_at(value, index, axis=0):
    return lax.dynamic_index_in_dim(value, index, axis, keepdims=False)


def added(*values):
    return sum(value.astype(F32) for value in values).astype(BF16)


def on_device(eigvecs, links, directions, spin_mats, forward_peram, backward_peram, chain_order):
    extent = eigvecs.shape[:3]
    num_vecs = eigvecs.shape[-1]
    gx_n, gy_n, gz_n = (lax.axis_size(name) for name in ("gx", "gy", "gz"))
    chips = gz_n // 2
    gx, gy, gz = (lax.axis_index(name).astype(jnp.int32) for name in ("gx", "gy", "gz"))
    me = jnp.stack([gx, gy, gz])
    chip, core = lax.div(gz, 2), lax.rem(gz, 2)

    rows, cols = forward_peram.shape[1:]
    piece = rows // gz_n
    site_rows = 6 * math.prod(extent)
    face_rows = [site_rows // n for n in extent]
    vec, *faces = pl.pallas_call(
        functools.partial(rows_kernel, extent),
        out_shape=[jax.ShapeDtypeStruct((n, num_vecs), BF16) for n in [site_rows] + face_rows],
        in_specs=[VMEM],
        out_specs=[VMEM] * 4,
        compiler_params=pltpu.CompilerParams(vmem_limit_bytes=24 * 2**20),
        name="rows",
    )(eigvecs.transpose(0, 1, 2, 4, 3, 5).reshape(-1, 2, num_vecs))
    faces = [passed_along(face, axis, -1) for face, axis in zip(faces, ("gx", "gy", "gz"))]

    both_pieces = pl.pallas_call(
        pieces_kernel,
        out_shape=jax.ShapeDtypeStruct((2, 2, piece, cols), BF16),
        in_specs=[SMEM] + [pl.BlockSpec(memory_space=pl.ANY)] * 2,
        out_specs=VMEM,
        scratch_shapes=[
            pltpu.VMEM(forward_peram.shape, BF16),
            pltpu.VMEM(backward_peram.shape, BF16),
            pltpu.SemaphoreType.DMA((2,)),
        ],
        compiler_params=pltpu.CompilerParams(vmem_limit_bytes=60 * 2**20),
        name="pieces",
    )(me[2:], forward_peram, backward_peram)
    both_pieces, links = lax.optimization_barrier((both_pieces, links))
    both_line, line = line_exchange(both_pieces, "gx", gx_n // 2, 1)

    link_mats = pl.pallas_call(
        functools.partial(links_kernel, extent),
        out_shape=[
            jax.ShapeDtypeStruct((3 * site_rows, site_rows - (0 if e else face_rows[0]) + face_rows[e]), BF16)
            for e in range(3)
        ],
        in_specs=[VMEM],
        out_specs=[VMEM] * 3,
        compiler_params=pltpu.CompilerParams(vmem_limit_bytes=24 * 2**20),
        name="link_matrices",
    )(links.reshape(-1, 54))

    volume = math.prod(extent) * gx_n * gy_n * gz_n
    own_rows = num_vecs // (gz_n * gx_n)
    split = gy_n if 6 % gy_n == 0 and own_rows % 16 == 0 else 1
    depth = 6 * own_rows // split
    partial = pl.pallas_call(
        functools.partial(correlate_kernel, 1.0 / math.sqrt(12.0 * volume)),
        out_shape=jax.ShapeDtypeStruct((gz_n, gx_n, split, depth, num_vecs), BF16),
        in_specs=[VMEM] * 7,
        out_specs=VMEM,
        compiler_params=pltpu.CompilerParams(vmem_limit_bytes=24 * 2**20),
        name="correlate",
    )(vec, *faces, *link_mats)

    partial, both_line = lax.optimization_barrier((partial, both_line))
    by_core = partial.reshape((chips, 2) + partial.shape[1:])
    summed = added(part_at(by_core, core, 1), passed_in_gz(part_at(by_core, 1 - core, 1), 0, 1))
    rounds = gx_n.bit_length() - 1
    first_line = line
    fwd_line, line = line_exchange(both_line[:, 0], "gx", gx_n // 4, rounds - 1, first_line)
    bwd_line, _ = line_exchange(both_line[:, 1], "gx", gx_n // 4, rounds - 1, first_line)
    plane = [(dx, dy) for dy in range(chips) for dx in range(gy_n)]

    def plane_part(dx, dy):
        part = part_at(summed, lax.rem(chip + dy, chips))
        return part_at(part, lax.rem(gy + dx, gy_n) if split > 1 else 0, 1)

    summed = added(*[passed_in_plane(plane_part(dx, dy), dx, dy) for dx, dy in plane])
    summed, fwd_line, bwd_line = lax.optimization_barrier((summed, fwd_line, bwd_line))

    four = gy_n == 2 and chips == 2
    fwd_parts = {(dx, dy, 0): passed_in_plane(fwd_line, dx, dy) for dx, dy in plane if not (four and dx and dy)}

    distance = gx_n // 2
    while distance:
        halves = summed.reshape((2, distance) + summed.shape[1:])
        bit = lax.rem(lax.div(gx, distance), 2)
        pairs = [(n, n ^ distance) for n in range(gx_n)]
        summed = added(part_at(halves, bit), lax.ppermute(part_at(halves, 1 - bit), "gx", pairs))
        distance //= 2
    elem_line, offsets = line_exchange(summed[0], "gx", gx_n // 2, rounds - 1)
    if four:
        over_x, over_y = fwd_parts[1, 0, 0], fwd_parts[0, 1, 0]
        elem_line, over_x, over_y = lax.optimization_barrier((elem_line, over_x, over_y))
        fwd_parts[1, 0, 0], fwd_parts[0, 1, 0] = over_x, over_y
        corner = [passed_in_plane(over_y[:, :1], 1, 0), passed_in_plane(over_x[:, 1:], 0, 1)]
        fwd_parts[1, 1, 0] = jnp.concatenate(corner, axis=1)
    elem_line, _ = line_exchange(elem_line, "gx", 1, 1, offsets)
    for dx, dy in plane:
        fwd_parts[dx, dy, 1] = passed_in_gz(fwd_parts[dx, dy, 0], 0, 1)
    elem_keys = plane if split > 1 else [(0, dy) for dy in range(chips)]
    elem_own = jnp.stack([passed_in_plane(elem_line, dx, dy) for dx, dy in elem_keys])
    elem_own, bwd_line = lax.optimization_barrier((elem_own, bwd_line))
    elem_parts = [elem_own, passed_in_gz(elem_own, 0, 1)]
    bwd_parts = {(dy, 0): passed_in_gz(bwd_line, dy, 0) if dy else bwd_line for dy in range(chips)}
    for dy in range(chips):
        bwd_parts[dy, 1] = passed_in_gz(bwd_parts[dy, 0], 0, 1)

    op_count = chain_order.shape[0]
    plan = (line, tuple(elem_keys), tuple(fwd_parts))
    left_shape = (op_count, rows, 8 * num_vecs)
    left = pl.pallas_call(
        functools.partial(left_kernel, 1.0 / math.sqrt(4 * num_vecs), plan),
        out_shape=jax.ShapeDtypeStruct(left_shape, BF16),
        in_specs=[SMEM] * 4 + [VMEM] * (len(elem_parts) + len(fwd_parts)),
        out_specs=VMEM,
        scratch_shapes=[
            pltpu.VMEM((gx_n, gz_n, split, depth, num_vecs), BF16),
            pltpu.VMEM((6, num_vecs, num_vecs), BF16),
            pltpu.VMEM((3, 2, gy_n, 4, rows // 4, cols), BF16),
            pltpu.VMEM((4, rows, 2 * num_vecs), BF16),
        ],
        compiler_params=pltpu.CompilerParams(vmem_limit_bytes=24 * 2**20),
        cost_estimate=pl.CostEstimate(flops=8 * 10**9, bytes_accessed=10**7, transcendentals=0),
        name="left",
    )(me, directions, spin_mats, chain_order, *elem_parts, *fwd_parts.values())
    return pl.pallas_call(
        functools.partial(right_kernel, gz_n, tuple(bwd_parts)),
        out_shape=jax.ShapeDtypeStruct((op_count, 2, rows, cols), BF16),
        in_specs=[VMEM] * (1 + len(bwd_parts)),
        out_specs=VMEM,
        scratch_shapes=[pltpu.VMEM((8 * num_vecs, 2 * cols), BF16)],
        compiler_params=pltpu.CompilerParams(vmem_limit_bytes=24 * 2**20),
        name="right",
    )(left, *bwd_parts.values())


def solution(mesh):
    in_specs = (
        P("gx", "gy", "gz", None, None, None),
        P("gx", "gy", "gz", None, None, None, None),
        P(),
        P(),
        P(None, "gx", "gy"),
        P(None, "gx", "gy"),
        P("gz", None),
    )
    out_specs = P("gz", None, "gx", "gy")
    return jax.shard_map(
        on_device, mesh=mesh, in_specs=in_specs, out_specs=out_specs, check_vma=False
    )
```

```python
import functools
import math

import jax
import jax.numpy as jnp
from jax import lax
from jax.experimental import pallas as pl
from jax.experimental.pallas import tpu as pltpu
from jax.sharding import PartitionSpec as P

VMEM = pl.BlockSpec(memory_space=pltpu.VMEM)
SMEM = pl.BlockSpec(memory_space=pltpu.SMEM)
BF16 = jnp.bfloat16
F32 = jnp.float32


def passed_along(value, axis, steps):
    count = lax.axis_size(axis)
    pairs = [(source, (source + steps) % count) for source in range(count)]
    return lax.ppermute(value, axis, pairs)


def mm(left, right):
    return jnp.dot(left, right, preferred_element_type=F32)


def parts_of(value, divisor):
    quotient = jnp.floor((value + 0.5) * (1.0 / divisor))
    return quotient, value - quotient * divisor


def whole_numbers(shape, axis):
    return lax.broadcasted_iota(jnp.int32, shape, axis).astype(F32)


def chosen(condition):
    return jnp.where(condition, 1.0, 0.0)


def coordinates(index, extent):
    rest, third = parts_of(index, extent[2])
    first, second = parts_of(rest, extent[1])
    return [first, second, third]


def source_columns(extent, e):
    count = math.prod(extent)
    face = count // extent[e]
    inner = count - face if e == 0 else count
    total = 6 * (inner + face)
    column = whole_numbers((1, total), 1)
    beyond = chosen(column >= 6 * inner)
    site, left = parts_of(column - beyond * (6 * inner), 6)
    colour, part = parts_of(left, 2)
    within = coordinates(site, extent)
    if e == 0:
        within[0] = within[0] + 1
    flat = [n for d, n in enumerate(extent) if d != e]
    outer, last = parts_of(site, flat[1])
    edge = [outer, last]
    edge.insert(e, jnp.full_like(site, extent[e]))
    where = [w + beyond * (o - w) for w, o in zip(within, edge)]
    return total, part, where, colour


def rows_kernel(extent, eig_ref, vec_out, *face_outs):
    vec = eig_ref[...].astype(F32).reshape(vec_out.shape)
    vec_out[...] = vec.astype(BF16)
    strides = (6 * extent[1] * extent[2], 6 * extent[2], 6)
    for e, out in enumerate(face_outs):
        begins = [0]
        for d in range(e):
            begins = [at + n * strides[d] for at in begins for n in range(extent[d])]
        runs = [vec[at : at + strides[e]] for at in begins]
        out[...] = (jnp.concatenate(runs, axis=0) if e else runs[0]).astype(BF16)


def pieces_kernel(z_ref, fwd_in, bwd_in, fwd_out, bwd_out, fwd_ref, bwd_ref, sems):
    pairs = ((fwd_in, fwd_ref), (bwd_in, bwd_ref))
    copies = [pltpu.make_async_copy(source, target, sems.at[n]) for n, (source, target) in enumerate(pairs)]
    for copy in copies:
        copy.start()
    rows, cols = fwd_ref.shape[1:]
    piece = fwd_out.shape[1]
    per_spin = rows // 4
    lane = cols // 4
    flat = lax.broadcasted_iota(jnp.int32, (piece, 1), 0) + z_ref[0] * piece
    spin = jnp.zeros_like(flat)
    for t in range(1, 4):
        spin += jnp.where(flat >= t * per_spin, 1, 0)
    source = 4 * (flat - spin * per_spin) + spin
    select = chosen(lax.broadcasted_iota(jnp.int32, (piece, rows), 1) == source).astype(BF16)
    column = lax.broadcasted_iota(jnp.int32, (1, cols), 1)
    spin = jnp.zeros_like(column)
    for t in range(1, 4):
        spin += jnp.where(column >= t * lane, 1, 0)
    source = 4 * (column - spin * lane) + spin
    perm = chosen(lax.broadcasted_iota(jnp.int32, (cols, cols), 0) == source).astype(BF16)
    copies[0].wait()
    for c in range(2):
        picked = mm(select, fwd_ref[c]).astype(BF16)
        fwd_out[c] = mm(picked, perm).astype(BF16)
    copies[1].wait()
    for c in range(2):
        bwd_out[c] = mm(select, bwd_ref[c]).astype(BF16)


def links_kernel(extent, link_ref, *outs):
    count = math.prod(extent)
    rows = 6 * count
    row = whole_numbers((rows, 1), 0)
    row_site, left = parts_of(row, 6)
    row_colour, row_part = parts_of(left, 2)
    row_where = coordinates(row_site, extent)
    link = link_ref[...]
    high = link.astype(BF16)
    rest = link - high.astype(F32)
    mid = rest.astype(BF16)
    low = (rest - mid.astype(F32)).astype(BF16)
    spread = chosen(row_site == whole_numbers((rows, count), 1)).astype(BF16)
    by_row = [mm(spread, part) for part in (high, mid, low)]
    by_row = [jnp.concatenate([part, part], axis=1) for part in by_row]

    def entry_of(entry):
        half = chosen(entry >= 54)
        direction, left = parts_of(entry - 54 * half, 18)
        part, left = parts_of(left, 9)
        into, out_of = parts_of(left, 3)
        return half, direction, part, into, out_of

    half, direction, _, into, _ = entry_of(whole_numbers((1, 108), 1))
    own_part = (half == row_part) & (into == row_colour)
    place_half, _, place_part, _, place_colour = entry_of(whole_numbers((108, 1), 0))
    for e, out in enumerate(outs):
        keep = chosen(own_part & (direction == e))
        picked = jnp.concatenate([part * keep for part in by_row], axis=0).astype(BF16)
        total, part, where, colour = source_columns(extent, e)
        sign = 1.0 - 2.0 * part * (1.0 - place_half)
        match = (place_colour == colour) & (jnp.abs(place_part - part) == place_half)
        placed = mm(picked, jnp.where(match, sign, 0.0).astype(BF16))
        same = None
        for d in range(3):
            hit = row_where[d] + (1.0 if d == e else 0.0) == where[d]
            same = hit if same is None else same & hit
        mask = chosen(same)
        for n in range(3):
            at = slice(n * rows, (n + 1) * rows)
            out[at, :] = (placed[at] * mask).astype(BF16)


def correlate_kernel(scale, vec_ref, face0, face1, face2, mat0, mat1, mat2, out_ref):
    gz_n, gx_n, split, depth, width = out_ref.shape
    each = 6 // split
    own_rows = depth // each
    vec = vec_ref[...]
    rows = vec.shape[0]
    row = lax.broadcasted_iota(jnp.int32, (rows, rows), 0)
    column = lax.broadcasted_iota(jnp.int32, (rows, rows), 1)
    odd = lax.rem(row, 2) == 1
    turn = jnp.where(odd & (column == row - 1), -1.0, chosen((column == row + 1) & ~odd)).astype(BF16)
    sources = [
        jnp.concatenate([vec[face0.shape[0] :], face0[...]], axis=0),
        jnp.concatenate([vec, face1[...]], axis=0),
        jnp.concatenate([vec, face2[...]], axis=0),
    ]
    for e, mat in enumerate((mat0, mat1, mat2)):
        terms = mm(mat[...], sources[e])
        moved = terms[:rows] + terms[rows : 2 * rows] + terms[2 * rows :]
        moved = moved.astype(BF16)
        turned = mm(turn, moved).astype(BF16)
        right = jnp.concatenate([moved, turned], axis=1)
        product = lax.dot_general(
            vec, right, (((0,), (0,)), ((), ())), preferred_element_type=F32
        )
        product = (product * scale).astype(BF16)
        for c in range(2):
            n = 2 * e + c
            half = product[:, c * width : (c + 1) * width]
            to = slice(n % each * own_rows, (n % each + 1) * own_rows)
            for g in range(gx_n):
                for z in range(gz_n):
                    at = (g * gz_n + z) * own_rows
                    out_ref[z, g, n // each, to] = half[at : at + own_rows]


def spin_groups(gz_n):
    keys = [(dy, dc) for dc in range(2) for dy in range(gz_n // 2)]
    if gz_n == 4:
        return [[key] for key in keys]
    return [[(dy, dc) for dc in range(2)] for dy in range(gz_n // 2)]


def rows_of(parts, c, count):
    rows = jnp.concatenate([part[:, c] for part in parts], axis=1)
    return rows.reshape(count, rows.shape[-1])


def right_kernel(gz_n, keys, left_ref, *refs):
    bwd_at = dict(zip(keys, refs))
    out_ref, b_ref = refs[len(keys) :]
    num_vecs = b_ref.shape[0] // 8
    op_count, _, row_count, width = out_ref.shape
    for t, group in enumerate(spin_groups(gz_n)):
        real, imag = [rows_of([bwd_at[key] for key in group], c, num_vecs) for c in range(2)]
        at = 2 * t * num_vecs
        b_ref[at : at + num_vecs, :width] = real
        b_ref[at : at + num_vecs, width:] = imag
        b_ref[at + num_vecs : at + 2 * num_vecs, :width] = -imag
        b_ref[at + num_vecs : at + 2 * num_vecs, width:] = real
    left = left_ref[...].reshape(op_count * row_count, 8 * num_vecs)
    block = min(width, 256)
    for c in range(2):
        for begin in range(0, width, block):
            at = c * width + begin
            result = mm(left, b_ref[:, at : at + block]).astype(BF16)
            out_ref[:, c, :, begin : begin + block] = result.reshape(op_count, row_count, block)


def left_kernel(inverse, plan, me_ref, dirs_ref, spin_ref, chain_ref, *refs):
    line, elem_keys, fwd_keys = plan
    elem_in, refs = refs[:2], refs[2:]
    fwd_in, refs = refs[: len(fwd_keys)], refs[len(fwd_keys) :]
    out_ref, elem_all, elem_ref, x_ref, p_ref = refs
    gx_n, gz_n, split, depth, num_vecs = elem_all.shape
    each = 6 // split
    own_rows = depth // each
    width = fwd_in[0].shape[3]
    op_count, row_count, _ = out_ref.shape
    vec_rows = row_count // 4
    gy_n = 4 * num_vecs // width
    lane = width // 4
    halves = gz_n // 4
    gx, gy, gz = me_ref[0], me_ref[1], me_ref[2]

    def back(at, step, count):
        return lax.rem(at - step + count, count)

    def gz_from(dy, dc):
        return back(lax.div(gz, 2), dy, gz_n // 2) * 2 + back(lax.rem(gz, 2), dc, 2)

    for dc, ref in enumerate(elem_in):
        for n, (dx, dy) in enumerate(elem_keys):
            for place, offset in enumerate(line):
                to = lax.bitwise_xor(gx, offset), gz_from(dy, dc), back(gy, dx, gy_n) if split > 1 else 0
                elem_all[to] = ref[n, place]
    column = lax.broadcasted_iota(jnp.int32, (1, num_vecs), 1)
    source = jnp.zeros_like(column)
    half_rows = vec_rows // halves
    for place, offset in enumerate(line):
        for half in range(halves):
            at = place * vec_rows + half * half_rows
            from_half = lax.bitwise_xor(lax.rem(gz, 2), half) if halves == 2 else half
            begin = lax.bitwise_xor(gx, offset) * vec_rows + from_half * half_rows
            inside = (column >= at) & (column < at + half_rows)
            source = jnp.where(inside, column + (begin - at), source)
    perm = chosen(lax.broadcasted_iota(jnp.int32, (num_vecs, num_vecs), 0) == source).astype(BF16)
    for n in range(6):
        rows = slice(n % each * own_rows, (n % each + 1) * own_rows)
        whole = elem_all[:, :, n // each, rows].reshape(num_vecs, num_vecs)
        elem_ref[n] = mm(whole, perm).astype(BF16)

    groups = spin_groups(gz_n)
    spins = [lax.div(gz_from(*group[0]), halves) for group in groups]

    first_row = pl.multiple_of(gx * vec_rows, vec_rows)

    def own(d, c):
        return elem_ref[2 * d + c, pl.ds(first_row, vec_rows), :]

    real_rows = [jnp.concatenate([own(d, 0), -own(d, 1)], axis=1) for d in range(3)]
    imag_rows = [jnp.concatenate([own(d, 1), own(d, 0)], axis=1) for d in range(3)]
    left = jnp.concatenate([part for d in range(3) for part in (real_rows[d], imag_rows[d])], axis=0)
    fwd_at = dict(zip(fwd_keys, fwd_in))
    for t, group in enumerate(groups):
        for dx in range(gy_n):
            parts = [fwd_at[(dx,) + key] for key in group]
            right = jnp.concatenate([rows_of(parts, c, num_vecs) for c in range(2)], axis=0)
            result = mm(left, right).astype(BF16)
            for d in range(3):
                for c in range(2):
                    at = (d * 2 + c) * vec_rows
                    x_ref[d, c, dx, t] = result[at : at + vec_rows]

    row = lax.broadcasted_iota(jnp.int32, (row_count, 1), 0)
    column = lax.broadcasted_iota(jnp.int32, (1, row_count), 1)
    row_spin = lax.rem(row, 4)
    diagonal = lax.div(row, 4) == lax.rem(column, vec_rows)
    column_spin = lax.div(column, vec_rows)
    blocks = [pl.multiple_of(back(gy, dx, gy_n) * lane, lane) for dx in range(gy_n)]

    def one_operator(op):
        a = chain_ref[op, 0]
        b = chain_ref[op, 1]
        dir_a = dirs_ref[a]
        dir_b = dirs_ref[b]
        mix = None
        for t in range(4):
            weight = jnp.full((row_count, 1), spin_ref[a, 0, spins[t]])
            for s in range(1, 4):
                weight = jnp.where(row_spin == s, spin_ref[a, s, spins[t]], weight)
            mix = weight if mix is None else jnp.where(column_spin == t, weight, mix)
        mix = jnp.where(diagonal, mix, 0.0)
        high = mix.astype(BF16)
        low = (mix - high.astype(F32)).astype(BF16)
        mix = jnp.concatenate([high, low], axis=1)
        for c in range(2):
            for dx in range(gy_n):
                source = x_ref[dir_a, c, dx].reshape(row_count, width)
                result = mm(mix, jnp.concatenate([source, source], axis=0)).astype(BF16)
                for s in range(4):
                    to = c * num_vecs + dx * lane
                    p_ref[s, :, to : to + lane] = result[:, s * lane : (s + 1) * lane]

        def elem(c):
            return jnp.concatenate([elem_ref[2 * dir_b + c, pl.ds(at, lane), :] for at in blocks], axis=0)

        real_b, imag_b = elem(0), elem(1)
        right = jnp.concatenate(
            [
                jnp.concatenate([real_b, imag_b], axis=1),
                jnp.concatenate([-imag_b, real_b], axis=1),
            ],
            axis=0,
        )
        parts = [mm(p_ref[s], right) for s in range(4)]
        for t in range(4):
            total = parts[0] * (spin_ref[b, 0, spins[t]] * inverse)
            for s in range(1, 4):
                total += parts[s] * (spin_ref[b, s, spins[t]] * inverse)
            total = total.astype(BF16)
            out_ref[op, :, 2 * t * num_vecs : 2 * (t + 1) * num_vecs] = total

    for op in range(op_count):
        one_operator(op)


def passed_in_gz(value, dy, dc):
    count = lax.axis_size("gz")
    chips = count // 2
    pairs = [(n, ((n // 2 + dy) % chips) * 2 + (n + dc) % 2) for n in range(count)]
    return lax.ppermute(value, "gz", pairs)


def passed_in_plane(value, dx, dy):
    if not dx and not dy:
        return value
    gy_n, gz_n = lax.axis_size("gy"), lax.axis_size("gz")
    chips = gz_n // 2
    pairs = []
    for y in range(gy_n):
        for z in range(gz_n):
            to = (y + dx) % gy_n * gz_n + ((z // 2 + dy) % chips) * 2 + z % 2
            pairs.append((y * gz_n + z, to))
    return lax.ppermute(value, ("gy", "gz"), pairs)


def line_exchange(value, axis, distance, steps, offsets=(0,)):
    count = lax.axis_size(axis)
    gathered = value if len(offsets) > 1 else value[None]
    offsets = list(offsets)
    for _ in range(steps):
        pairs = [(n, n ^ distance) for n in range(count)]
        gathered = jnp.concatenate([gathered, lax.ppermute(gathered, axis, pairs)])
        offsets += [offset ^ distance for offset in offsets]
        distance //= 2
    return gathered, tuple(offsets)


def part_at(value, index, axis=0):
    return lax.dynamic_index_in_dim(value, index, axis, keepdims=False)


def added(*values):
    return sum(value.astype(F32) for value in values).astype(BF16)


def on_device(eigvecs, links, directions, spin_mats, forward_peram, backward_peram, chain_order):
    extent = eigvecs.shape[:3]
    num_vecs = eigvecs.shape[-1]
    gx_n, gy_n, gz_n = (lax.axis_size(name) for name in ("gx", "gy", "gz"))
    chips = gz_n // 2
    gx, gy, gz = (lax.axis_index(name).astype(jnp.int32) for name in ("gx", "gy", "gz"))
    me = jnp.stack([gx, gy, gz])
    chip, core = lax.div(gz, 2), lax.rem(gz, 2)

    rows, cols = forward_peram.shape[1:]
    piece = rows // gz_n
    site_rows = 6 * math.prod(extent)
    face_rows = [site_rows // n for n in extent]
    vec, *faces = pl.pallas_call(
        functools.partial(rows_kernel, extent),
        out_shape=[jax.ShapeDtypeStruct((n, num_vecs), BF16) for n in [site_rows] + face_rows],
        in_specs=[VMEM],
        out_specs=[VMEM] * 4,
        compiler_params=pltpu.CompilerParams(vmem_limit_bytes=24 * 2**20),
        name="rows",
    )(eigvecs.transpose(0, 1, 2, 4, 3, 5).reshape(-1, 2, num_vecs))
    faces = [passed_along(face, axis, -1) for face, axis in zip(faces, ("gx", "gy", "gz"))]

    piece_shape = jax.ShapeDtypeStruct((2, piece, cols), BF16)
    fwd_piece, bwd_piece = pl.pallas_call(
        pieces_kernel,
        out_shape=[piece_shape] * 2,
        in_specs=[SMEM] + [pl.BlockSpec(memory_space=pl.ANY)] * 2,
        out_specs=[VMEM] * 2,
        scratch_shapes=[
            pltpu.VMEM(forward_peram.shape, BF16),
            pltpu.VMEM(backward_peram.shape, BF16),
            pltpu.SemaphoreType.DMA((2,)),
        ],
        compiler_params=pltpu.CompilerParams(vmem_limit_bytes=60 * 2**20),
        cost_estimate=pl.CostEstimate(flops=10**8, bytes_accessed=10**7, transcendentals=0),
        name="pieces",
    )(me[2:], forward_peram, backward_peram)
    fwd_piece, links = lax.optimization_barrier((fwd_piece, links))
    fwd_line, line = line_exchange(fwd_piece, "gx", gx_n // 2, 1)

    link_mats = pl.pallas_call(
        functools.partial(links_kernel, extent),
        out_shape=[
            jax.ShapeDtypeStruct((3 * site_rows, site_rows - (0 if e else face_rows[0]) + face_rows[e]), BF16)
            for e in range(3)
        ],
        in_specs=[VMEM],
        out_specs=[VMEM] * 3,
        compiler_params=pltpu.CompilerParams(vmem_limit_bytes=24 * 2**20),
        name="link_matrices",
    )(links.reshape(-1, 54))

    volume = math.prod(extent) * gx_n * gy_n * gz_n
    own_rows = num_vecs // (gz_n * gx_n)
    split = gy_n if 6 % gy_n == 0 and own_rows % 16 == 0 else 1
    depth = 6 * own_rows // split
    partial = pl.pallas_call(
        functools.partial(correlate_kernel, 1.0 / math.sqrt(12.0 * volume)),
        out_shape=jax.ShapeDtypeStruct((gz_n, gx_n, split, depth, num_vecs), BF16),
        in_specs=[VMEM] * 7,
        out_specs=VMEM,
        compiler_params=pltpu.CompilerParams(vmem_limit_bytes=24 * 2**20),
        name="correlate",
    )(vec, *faces, *link_mats)

    partial, fwd_line = lax.optimization_barrier((partial, fwd_line))
    by_core = partial.reshape((chips, 2) + partial.shape[1:])
    summed = added(part_at(by_core, core, 1), passed_in_gz(part_at(by_core, 1 - core, 1), 0, 1))
    rounds = gx_n.bit_length() - 1
    fwd_line, line = line_exchange(fwd_line, "gx", gx_n // 4, rounds - 1, line)
    plane = [(dx, dy) for dy in range(chips) for dx in range(gy_n)]

    def plane_part(dx, dy):
        part = part_at(summed, lax.rem(chip + dy, chips))
        return part_at(part, lax.rem(gy + dx, gy_n) if split > 1 else 0, 1)

    summed = added(*[passed_in_plane(plane_part(dx, dy), dx, dy) for dx, dy in plane])
    summed, fwd_line, bwd_piece = lax.optimization_barrier((summed, fwd_line, bwd_piece))
    bwd_line, _ = line_exchange(bwd_piece, "gx", gx_n // 2, rounds)

    four = gy_n == 2 and chips == 2
    fwd_parts = {(dx, dy, 0): passed_in_plane(fwd_line, dx, dy) for dx, dy in plane if not (four and dx and dy)}

    distance = gx_n // 2
    while distance:
        halves = summed.reshape((2, distance) + summed.shape[1:])
        bit = lax.rem(lax.div(gx, distance), 2)
        pairs = [(n, n ^ distance) for n in range(gx_n)]
        summed = added(part_at(halves, bit), lax.ppermute(part_at(halves, 1 - bit), "gx", pairs))
        distance //= 2
    elem_line, offsets = line_exchange(summed[0], "gx", gx_n // 2, rounds - 1)
    fwd_parts[0, 0, 1] = passed_in_gz(fwd_line, 0, 1)
    if four:
        keys = [(1, 0, 0), (0, 1, 0), (0, 0, 1)]
        elem_line, bwd_line, *parts = lax.optimization_barrier((elem_line, bwd_line, *[fwd_parts[key] for key in keys]))
        fwd_parts.update(zip(keys, parts))
        fwd_parts[1, 1, 0] = passed_in_plane(fwd_parts[0, 1, 0], 1, 0)
    bwd_parts = {(dy, 0): passed_in_gz(bwd_line, dy, 0) if dy else bwd_line for dy in range(chips)}
    elem_line, _ = line_exchange(elem_line, "gx", 1, 1, offsets)
    elem_keys = plane if split > 1 else [(0, dy) for dy in range(chips)]
    elem_own = jnp.stack([passed_in_plane(elem_line, dx, dy) for dx, dy in elem_keys])
    late = [(1, 1, 0)] if four else []
    elem_own, *parts = lax.optimization_barrier((elem_own, *[fwd_parts[key] for key in late], *bwd_parts.values()))
    fwd_parts.update(zip(late, parts))
    bwd_parts.update(zip(list(bwd_parts), parts[len(late) :]))
    elem_parts = [elem_own, passed_in_gz(elem_own, 0, 1)]
    for dx, dy in plane[1:]:
        fwd_parts[dx, dy, 1] = passed_in_gz(fwd_parts[dx, dy, 0], 0, 1)
    for dy in range(chips):
        bwd_parts[dy, 1] = passed_in_gz(bwd_parts[dy, 0], 0, 1)

    op_count = chain_order.shape[0]
    plan = (line, tuple(elem_keys), tuple(fwd_parts))
    left_shape = (op_count, rows, 8 * num_vecs)
    left = pl.pallas_call(
        functools.partial(left_kernel, 1.0 / math.sqrt(4 * num_vecs), plan),
        out_shape=jax.ShapeDtypeStruct(left_shape, BF16),
        in_specs=[SMEM] * 4 + [VMEM] * (len(elem_parts) + len(fwd_parts)),
        out_specs=VMEM,
        scratch_shapes=[
            pltpu.VMEM((gx_n, gz_n, split, depth, num_vecs), BF16),
            pltpu.VMEM((6, num_vecs, num_vecs), BF16),
            pltpu.VMEM((3, 2, gy_n, 4, rows // 4, cols), BF16),
            pltpu.VMEM((4, rows, 2 * num_vecs), BF16),
        ],
        compiler_params=pltpu.CompilerParams(vmem_limit_bytes=24 * 2**20),
        cost_estimate=pl.CostEstimate(flops=8 * 10**9, bytes_accessed=10**7, transcendentals=0),
        name="left",
    )(me, directions, spin_mats, chain_order, *elem_parts, *fwd_parts.values())
    return pl.pallas_call(
        functools.partial(right_kernel, gz_n, tuple(bwd_parts)),
        out_shape=jax.ShapeDtypeStruct((op_count, 2, rows, cols), BF16),
        in_specs=[VMEM] * (1 + len(bwd_parts)),
        out_specs=VMEM,
        scratch_shapes=[pltpu.VMEM((8 * num_vecs, 2 * cols), BF16)],
        compiler_params=pltpu.CompilerParams(vmem_limit_bytes=24 * 2**20),
        name="right",
    )(left, *bwd_parts.values())


def solution(mesh):
    in_specs = (
        P("gx", "gy", "gz", None, None, None),
        P("gx", "gy", "gz", None, None, None, None),
        P(),
        P(),
        P(None, "gx", "gy"),
        P(None, "gx", "gy"),
        P("gz", None),
    )
    out_specs = P("gz", None, "gx", "gy")
    return jax.shard_map(
        on_device, mesh=mesh, in_specs=in_specs, out_specs=out_specs, check_vma=False
    )
```

```python
import functools
import math

import jax
import jax.numpy as jnp
from jax import lax
from jax.experimental import pallas as pl
from jax.experimental.pallas import tpu as pltpu
from jax.sharding import PartitionSpec as P

VMEM = pl.BlockSpec(memory_space=pltpu.VMEM)
SMEM = pl.BlockSpec(memory_space=pltpu.SMEM)
BF16 = jnp.bfloat16
F32 = jnp.float32


def passed_along(value, axis, steps):
    count = lax.axis_size(axis)
    pairs = [(source, (source + steps) % count) for source in range(count)]
    return lax.ppermute(value, axis, pairs)


def mm(left, right):
    return jnp.dot(left, right, preferred_element_type=F32)


def parts_of(value, divisor):
    quotient = jnp.floor((value + 0.5) * (1.0 / divisor))
    return quotient, value - quotient * divisor


def whole_numbers(shape, axis):
    return lax.broadcasted_iota(jnp.int32, shape, axis).astype(F32)


def chosen(condition):
    return jnp.where(condition, 1.0, 0.0)


def coordinates(index, extent):
    rest, third = parts_of(index, extent[2])
    first, second = parts_of(rest, extent[1])
    return [first, second, third]


def source_columns(extent, e):
    count = math.prod(extent)
    face = count // extent[e]
    inner = count - face if e == 0 else count
    total = 6 * (inner + face)
    column = whole_numbers((1, total), 1)
    beyond = chosen(column >= 6 * inner)
    site, left = parts_of(column - beyond * (6 * inner), 6)
    colour, part = parts_of(left, 2)
    within = coordinates(site, extent)
    if e == 0:
        within[0] = within[0] + 1
    flat = [n for d, n in enumerate(extent) if d != e]
    outer, last = parts_of(site, flat[1])
    edge = [outer, last]
    edge.insert(e, jnp.full_like(site, extent[e]))
    where = [w + beyond * (o - w) for w, o in zip(within, edge)]
    return total, part, where, colour


def rows_kernel(extent, eig_ref, vec_out, *face_outs):
    vec = eig_ref[...].astype(F32).reshape(vec_out.shape)
    vec_out[...] = vec.astype(BF16)
    strides = (6 * extent[1] * extent[2], 6 * extent[2], 6)
    for e, out in enumerate(face_outs):
        begins = [0]
        for d in range(e):
            begins = [at + n * strides[d] for at in begins for n in range(extent[d])]
        runs = [vec[at : at + strides[e]] for at in begins]
        out[...] = (jnp.concatenate(runs, axis=0) if e else runs[0]).astype(BF16)


def pieces_kernel(z_ref, fwd_in, bwd_in, fwd_out, bwd_out, fwd_ref, bwd_ref, sems):
    pairs = ((fwd_in, fwd_ref), (bwd_in, bwd_ref))
    copies = [pltpu.make_async_copy(source, target, sems.at[n]) for n, (source, target) in enumerate(pairs)]
    for copy in copies:
        copy.start()
    rows, cols = fwd_ref.shape[1:]
    piece = fwd_out.shape[1]
    per_spin = rows // 4
    lane = cols // 4
    flat = lax.broadcasted_iota(jnp.int32, (piece, 1), 0) + z_ref[0] * piece
    spin = jnp.zeros_like(flat)
    for t in range(1, 4):
        spin += jnp.where(flat >= t * per_spin, 1, 0)
    source = 4 * (flat - spin * per_spin) + spin
    select = chosen(lax.broadcasted_iota(jnp.int32, (piece, rows), 1) == source).astype(BF16)
    column = lax.broadcasted_iota(jnp.int32, (1, cols), 1)
    spin = jnp.zeros_like(column)
    for t in range(1, 4):
        spin += jnp.where(column >= t * lane, 1, 0)
    source = 4 * (column - spin * lane) + spin
    perm = chosen(lax.broadcasted_iota(jnp.int32, (cols, cols), 0) == source).astype(BF16)
    copies[0].wait()
    for c in range(2):
        picked = mm(select, fwd_ref[c]).astype(BF16)
        fwd_out[c] = mm(picked, perm).astype(BF16)
    copies[1].wait()
    for c in range(2):
        bwd_out[c] = mm(select, bwd_ref[c]).astype(BF16)


def links_kernel(extent, link_ref, *outs):
    count = math.prod(extent)
    rows = 6 * count
    row = whole_numbers((rows, 1), 0)
    row_site, left = parts_of(row, 6)
    row_colour, row_part = parts_of(left, 2)
    row_where = coordinates(row_site, extent)
    link = link_ref[...]
    high = link.astype(BF16)
    rest = link - high.astype(F32)
    mid = rest.astype(BF16)
    low = (rest - mid.astype(F32)).astype(BF16)
    spread = chosen(row_site == whole_numbers((rows, count), 1)).astype(BF16)
    by_row = [mm(spread, part) for part in (high, mid, low)]
    by_row = [jnp.concatenate([part, part], axis=1) for part in by_row]

    def entry_of(entry):
        half = chosen(entry >= 54)
        direction, left = parts_of(entry - 54 * half, 18)
        part, left = parts_of(left, 9)
        into, out_of = parts_of(left, 3)
        return half, direction, part, into, out_of

    half, direction, _, into, _ = entry_of(whole_numbers((1, 108), 1))
    own_part = (half == row_part) & (into == row_colour)
    place_half, _, place_part, _, place_colour = entry_of(whole_numbers((108, 1), 0))
    for e, out in enumerate(outs):
        keep = chosen(own_part & (direction == e))
        picked = jnp.concatenate([part * keep for part in by_row], axis=0).astype(BF16)
        total, part, where, colour = source_columns(extent, e)
        sign = 1.0 - 2.0 * part * (1.0 - place_half)
        match = (place_colour == colour) & (jnp.abs(place_part - part) == place_half)
        placed = mm(picked, jnp.where(match, sign, 0.0).astype(BF16))
        same = None
        for d in range(3):
            hit = row_where[d] + (1.0 if d == e else 0.0) == where[d]
            same = hit if same is None else same & hit
        mask = chosen(same)
        for n in range(3):
            at = slice(n * rows, (n + 1) * rows)
            out[at, :] = (placed[at] * mask).astype(BF16)


def correlate_kernel(scale, vec_ref, face0, face1, face2, mat0, mat1, mat2, out_ref):
    gz_n, gx_n, split, depth, width = out_ref.shape
    each = 6 // split
    own_rows = depth // each
    vec = vec_ref[...]
    rows = vec.shape[0]
    row = lax.broadcasted_iota(jnp.int32, (rows, rows), 0)
    column = lax.broadcasted_iota(jnp.int32, (rows, rows), 1)
    odd = lax.rem(row, 2) == 1
    turn = jnp.where(odd & (column == row - 1), -1.0, chosen((column == row + 1) & ~odd)).astype(BF16)
    sources = [
        jnp.concatenate([vec[face0.shape[0] :], face0[...]], axis=0),
        jnp.concatenate([vec, face1[...]], axis=0),
        jnp.concatenate([vec, face2[...]], axis=0),
    ]
    for e, mat in enumerate((mat0, mat1, mat2)):
        terms = mm(mat[...], sources[e])
        moved = terms[:rows] + terms[rows : 2 * rows] + terms[2 * rows :]
        moved = moved.astype(BF16)
        turned = mm(turn, moved).astype(BF16)
        right = jnp.concatenate([moved, turned], axis=1)
        product = lax.dot_general(
            vec, right, (((0,), (0,)), ((), ())), preferred_element_type=F32
        )
        product = (product * scale).astype(BF16)
        for c in range(2):
            n = 2 * e + c
            half = product[:, c * width : (c + 1) * width]
            to = slice(n % each * own_rows, (n % each + 1) * own_rows)
            for g in range(gx_n):
                for z in range(gz_n):
                    at = (g * gz_n + z) * own_rows
                    out_ref[z, g, n // each, to] = half[at : at + own_rows]


def spin_groups(gz_n):
    keys = [(dy, dc) for dc in range(2) for dy in range(gz_n // 2)]
    if gz_n == 4:
        return [[key] for key in keys]
    return [[(dy, dc) for dc in range(2)] for dy in range(gz_n // 2)]


def rows_of(parts, c, count):
    rows = jnp.concatenate([part[:, c] for part in parts], axis=1)
    return rows.reshape(count, rows.shape[-1])


def right_kernel(gz_n, keys, left_ref, *refs):
    bwd_at = dict(zip(keys, refs))
    out_ref, b_ref = refs[len(keys) :]
    num_vecs = b_ref.shape[0] // 8
    op_count, _, row_count, width = out_ref.shape
    for t, group in enumerate(spin_groups(gz_n)):
        real, imag = [rows_of([bwd_at[key] for key in group], c, num_vecs) for c in range(2)]
        at = 2 * t * num_vecs
        b_ref[at : at + num_vecs, :width] = real
        b_ref[at : at + num_vecs, width:] = imag
        b_ref[at + num_vecs : at + 2 * num_vecs, :width] = -imag
        b_ref[at + num_vecs : at + 2 * num_vecs, width:] = real
    left = left_ref[...].reshape(op_count * row_count, 8 * num_vecs)
    block = min(width, 256)
    for c in range(2):
        for begin in range(0, width, block):
            at = c * width + begin
            result = mm(left, b_ref[:, at : at + block]).astype(BF16)
            out_ref[:, c, :, begin : begin + block] = result.reshape(op_count, row_count, block)


def left_kernel(inverse, plan, me_ref, dirs_ref, spin_ref, chain_ref, *refs):
    line, fwd_keys = plan
    elem_in, refs = refs[:2], refs[2:]
    fwd_in, refs = refs[: len(fwd_keys)], refs[len(fwd_keys) :]
    out_ref, elem_all, elem_ref, x_ref, p_ref = refs
    gx_n, gz_n, split, depth, num_vecs = elem_all.shape
    each = 6 // split
    own_rows = depth // each
    width = fwd_in[0].shape[3]
    op_count, row_count, _ = out_ref.shape
    vec_rows = row_count // 4
    gy_n = 4 * num_vecs // width
    lane = width // 4
    halves = gz_n // 4
    gx, gy, gz = me_ref[0], me_ref[1], me_ref[2]

    def back(at, step, count):
        return lax.rem(at - step + count, count)

    def gz_from(dy, dc):
        return back(lax.div(gz, 2), dy, gz_n // 2) * 2 + back(lax.rem(gz, 2), dc, 2)

    for dc, ref in enumerate(elem_in):
        for dy in range(gz_n // 2):
            for n in range(gx_n * split):
                elem_all[n // split, gz_from(dy, dc), n % split] = ref[dy, n]
    column = lax.broadcasted_iota(jnp.int32, (1, num_vecs), 1)
    source = jnp.zeros_like(column)
    half_rows = vec_rows // halves
    for place, offset in enumerate(line):
        for half in range(halves):
            at = place * vec_rows + half * half_rows
            from_half = lax.bitwise_xor(lax.rem(gz, 2), half) if halves == 2 else half
            begin = lax.bitwise_xor(gx, offset) * vec_rows + from_half * half_rows
            inside = (column >= at) & (column < at + half_rows)
            source = jnp.where(inside, column + (begin - at), source)
    perm = chosen(lax.broadcasted_iota(jnp.int32, (num_vecs, num_vecs), 0) == source).astype(BF16)
    for n in range(6):
        rows = slice(n % each * own_rows, (n % each + 1) * own_rows)
        whole = elem_all[:, :, n // each, rows].reshape(num_vecs, num_vecs)
        elem_ref[n] = mm(whole, perm).astype(BF16)

    groups = spin_groups(gz_n)
    spins = [lax.div(gz_from(*group[0]), halves) for group in groups]

    first_row = pl.multiple_of(gx * vec_rows, vec_rows)

    def own(d, c):
        return elem_ref[2 * d + c, pl.ds(first_row, vec_rows), :]

    real_rows = [jnp.concatenate([own(d, 0), -own(d, 1)], axis=1) for d in range(3)]
    imag_rows = [jnp.concatenate([own(d, 1), own(d, 0)], axis=1) for d in range(3)]
    left = jnp.concatenate([part for d in range(3) for part in (real_rows[d], imag_rows[d])], axis=0)
    fwd_at = dict(zip(fwd_keys, fwd_in))
    for t, group in enumerate(groups):
        for dx in range(gy_n):
            parts = [fwd_at[(dx,) + key] for key in group]
            right = jnp.concatenate([rows_of(parts, c, num_vecs) for c in range(2)], axis=0)
            result = mm(left, right).astype(BF16)
            for d in range(3):
                for c in range(2):
                    at = (d * 2 + c) * vec_rows
                    x_ref[d, c, dx, t] = result[at : at + vec_rows]

    row = lax.broadcasted_iota(jnp.int32, (row_count, 1), 0)
    column = lax.broadcasted_iota(jnp.int32, (1, row_count), 1)
    row_spin = lax.rem(row, 4)
    diagonal = lax.div(row, 4) == lax.rem(column, vec_rows)
    column_spin = lax.div(column, vec_rows)
    blocks = [pl.multiple_of(back(gy, dx, gy_n) * lane, lane) for dx in range(gy_n)]

    def one_operator(op):
        a = chain_ref[op, 0]
        b = chain_ref[op, 1]
        dir_a = dirs_ref[a]
        dir_b = dirs_ref[b]
        mix = None
        for t in range(4):
            weight = jnp.full((row_count, 1), spin_ref[a, 0, spins[t]])
            for s in range(1, 4):
                weight = jnp.where(row_spin == s, spin_ref[a, s, spins[t]], weight)
            mix = weight if mix is None else jnp.where(column_spin == t, weight, mix)
        mix = jnp.where(diagonal, mix, 0.0)
        high = mix.astype(BF16)
        low = (mix - high.astype(F32)).astype(BF16)
        mix = jnp.concatenate([high, low], axis=1)
        for c in range(2):
            for dx in range(gy_n):
                source = x_ref[dir_a, c, dx].reshape(row_count, width)
                result = mm(mix, jnp.concatenate([source, source], axis=0)).astype(BF16)
                for s in range(4):
                    to = c * num_vecs + dx * lane
                    p_ref[s, :, to : to + lane] = result[:, s * lane : (s + 1) * lane]

        def elem(c):
            return jnp.concatenate([elem_ref[2 * dir_b + c, pl.ds(at, lane), :] for at in blocks], axis=0)

        real_b, imag_b = elem(0), elem(1)
        right = jnp.concatenate(
            [
                jnp.concatenate([real_b, imag_b], axis=1),
                jnp.concatenate([-imag_b, real_b], axis=1),
            ],
            axis=0,
        )
        parts = [mm(p_ref[s], right) for s in range(4)]
        for t in range(4):
            total = parts[0] * (spin_ref[b, 0, spins[t]] * inverse)
            for s in range(1, 4):
                total += parts[s] * (spin_ref[b, s, spins[t]] * inverse)
            total = total.astype(BF16)
            out_ref[op, :, 2 * t * num_vecs : 2 * (t + 1) * num_vecs] = total

    for op in range(op_count):
        one_operator(op)


def passed_in_gz(value, dy, dc):
    count = lax.axis_size("gz")
    chips = count // 2
    pairs = [(n, ((n // 2 + dy) % chips) * 2 + (n + dc) % 2) for n in range(count)]
    return lax.ppermute(value, "gz", pairs)


def passed_in_plane(value, dx, dy):
    if not dx and not dy:
        return value
    gy_n, gz_n = lax.axis_size("gy"), lax.axis_size("gz")
    chips = gz_n // 2
    pairs = []
    for y in range(gy_n):
        for z in range(gz_n):
            to = (y + dx) % gy_n * gz_n + ((z // 2 + dy) % chips) * 2 + z % 2
            pairs.append((y * gz_n + z, to))
    return lax.ppermute(value, ("gy", "gz"), pairs)


def line_exchange(value, axis, distance, steps, offsets=(0,)):
    count = lax.axis_size(axis)
    gathered = value if len(offsets) > 1 else value[None]
    offsets = list(offsets)
    for _ in range(steps):
        pairs = [(n, n ^ distance) for n in range(count)]
        gathered = jnp.concatenate([gathered, lax.ppermute(gathered, axis, pairs)])
        offsets += [offset ^ distance for offset in offsets]
        distance //= 2
    return gathered, tuple(offsets)


def part_at(value, index, axis=0):
    return lax.dynamic_index_in_dim(value, index, axis, keepdims=False)


def added(*values):
    return sum(value.astype(F32) for value in values).astype(BF16)


def on_device(eigvecs, links, directions, spin_mats, forward_peram, backward_peram, chain_order):
    extent = eigvecs.shape[:3]
    num_vecs = eigvecs.shape[-1]
    gx_n, gy_n, gz_n = (lax.axis_size(name) for name in ("gx", "gy", "gz"))
    chips = gz_n // 2
    gx, gy, gz = (lax.axis_index(name).astype(jnp.int32) for name in ("gx", "gy", "gz"))
    me = jnp.stack([gx, gy, gz])
    chip, core = lax.div(gz, 2), lax.rem(gz, 2)

    rows, cols = forward_peram.shape[1:]
    piece = rows // gz_n
    site_rows = 6 * math.prod(extent)
    face_rows = [site_rows // n for n in extent]
    vec, *faces = pl.pallas_call(
        functools.partial(rows_kernel, extent),
        out_shape=[jax.ShapeDtypeStruct((n, num_vecs), BF16) for n in [site_rows] + face_rows],
        in_specs=[VMEM],
        out_specs=[VMEM] * 4,
        compiler_params=pltpu.CompilerParams(vmem_limit_bytes=24 * 2**20),
        name="rows",
    )(eigvecs.transpose(0, 1, 2, 4, 3, 5).reshape(-1, 2, num_vecs))
    faces = [passed_along(face, axis, -1) for face, axis in zip(faces, ("gx", "gy", "gz"))]

    piece_shape = jax.ShapeDtypeStruct((2, piece, cols), BF16)
    fwd_piece, bwd_piece = pl.pallas_call(
        pieces_kernel,
        out_shape=[piece_shape] * 2,
        in_specs=[SMEM] + [pl.BlockSpec(memory_space=pl.ANY)] * 2,
        out_specs=[VMEM] * 2,
        scratch_shapes=[
            pltpu.VMEM(forward_peram.shape, BF16),
            pltpu.VMEM(backward_peram.shape, BF16),
            pltpu.SemaphoreType.DMA((2,)),
        ],
        compiler_params=pltpu.CompilerParams(vmem_limit_bytes=60 * 2**20),
        cost_estimate=pl.CostEstimate(flops=10**8, bytes_accessed=10**7, transcendentals=0),
        name="pieces",
    )(me[2:], forward_peram, backward_peram)
    fwd_piece, links = lax.optimization_barrier((fwd_piece, links))
    fwd_half = lax.ppermute(fwd_piece, "gx", [(n, n ^ (gx_n // 2)) for n in range(gx_n)])

    link_mats = pl.pallas_call(
        functools.partial(links_kernel, extent),
        out_shape=[
            jax.ShapeDtypeStruct((3 * site_rows, site_rows - (0 if e else face_rows[0]) + face_rows[e]), BF16)
            for e in range(3)
        ],
        in_specs=[VMEM],
        out_specs=[VMEM] * 3,
        compiler_params=pltpu.CompilerParams(vmem_limit_bytes=24 * 2**20),
        name="link_matrices",
    )(links.reshape(-1, 54))

    volume = math.prod(extent) * gx_n * gy_n * gz_n
    own_rows = num_vecs // (gz_n * gx_n)
    split = gy_n if 6 % gy_n == 0 and own_rows % 16 == 0 else 1
    depth = 6 * own_rows // split
    partial = pl.pallas_call(
        functools.partial(correlate_kernel, 1.0 / math.sqrt(12.0 * volume)),
        out_shape=jax.ShapeDtypeStruct((gz_n, gx_n, split, depth, num_vecs), BF16),
        in_specs=[VMEM] * 7,
        out_specs=VMEM,
        compiler_params=pltpu.CompilerParams(vmem_limit_bytes=24 * 2**20),
        name="correlate",
    )(vec, *faces, *link_mats)

    rounds = gx_n.bit_length() - 1
    partial, fwd_half = lax.optimization_barrier((partial, fwd_half))
    by_core = partial.reshape((chips, 2) + partial.shape[1:])
    summed = added(part_at(by_core, core, 1), passed_in_gz(part_at(by_core, 1 - core, 1), 0, 1))
    fwd_line = jnp.stack([fwd_piece, fwd_half])
    fwd_line, line = line_exchange(fwd_line, "gx", gx_n // 4, rounds - 1, (0, gx_n // 2))
    summed = added(*[passed_in_gz(part_at(summed, lax.rem(chip + dy, chips)), dy, 0) if dy else part_at(summed, chip) for dy in range(chips)])
    summed, fwd_line, bwd_piece = lax.optimization_barrier((summed, fwd_line, bwd_piece))
    bwd_line, _ = line_exchange(bwd_piece, "gx", gx_n // 2, rounds)

    plane = [(dx, dy) for dy in range(chips) for dx in range(gy_n)]
    four = gy_n == 2 and chips == 2
    fwd_parts = {(dx, dy, 0): passed_in_plane(fwd_line, dx, dy) for dx, dy in plane if not (four and dx and dy)}
    fwd_parts[0, 0, 1] = passed_in_gz(fwd_line, 0, 1)

    area = ("gx", "gy") if split > 1 else "gx"
    if split == 1:
        summed = added(summed, *[passed_along(summed, "gy", dx) for dx in range(1, gy_n)])
    summed = lax.all_to_all(summed.reshape(gx_n * split, depth, num_vecs), area, 0, 0, tiled=True)
    summed = jnp.sum(summed.astype(F32), axis=0).astype(BF16)
    elem_line = lax.all_to_all(jnp.broadcast_to(summed, (gx_n * split, depth, num_vecs)), area, 0, 0, tiled=True)
    if four:
        keys = [(1, 0, 0), (0, 1, 0), (0, 0, 1)]
        elem_line, bwd_line, *parts = lax.optimization_barrier((elem_line, bwd_line, *[fwd_parts[key] for key in keys]))
        fwd_parts.update(zip(keys, parts))
        fwd_parts[1, 1, 0] = passed_in_plane(fwd_parts[0, 1, 0], 1, 0)
    bwd_parts = {(dy, 0): passed_in_gz(bwd_line, dy, 0) if dy else bwd_line for dy in range(chips)}
    elem_own = jnp.stack([passed_in_gz(elem_line, dy, 0) if dy else elem_line for dy in range(chips)])
    late = [(1, 1, 0)] if four else []
    elem_own, *parts = lax.optimization_barrier((elem_own, *[fwd_parts[key] for key in late], *bwd_parts.values()))
    fwd_parts.update(zip(late, parts))
    bwd_parts.update(zip(list(bwd_parts), parts[len(late) :]))
    elem_parts = [elem_own, passed_in_gz(elem_own, 0, 1)]
    for dx, dy in plane[1:]:
        fwd_parts[dx, dy, 1] = passed_in_gz(fwd_parts[dx, dy, 0], 0, 1)
    for dy in range(chips):
        bwd_parts[dy, 1] = passed_in_gz(bwd_parts[dy, 0], 0, 1)

    op_count = chain_order.shape[0]
    plan = (line, tuple(fwd_parts))
    left_shape = (op_count, rows, 8 * num_vecs)
    left = pl.pallas_call(
        functools.partial(left_kernel, 1.0 / math.sqrt(4 * num_vecs), plan),
        out_shape=jax.ShapeDtypeStruct(left_shape, BF16),
        in_specs=[SMEM] * 4 + [VMEM] * (len(elem_parts) + len(fwd_parts)),
        out_specs=VMEM,
        scratch_shapes=[
            pltpu.VMEM((gx_n, gz_n, split, depth, num_vecs), BF16),
            pltpu.VMEM((6, num_vecs, num_vecs), BF16),
            pltpu.VMEM((3, 2, gy_n, 4, rows // 4, cols), BF16),
            pltpu.VMEM((4, rows, 2 * num_vecs), BF16),
        ],
        compiler_params=pltpu.CompilerParams(vmem_limit_bytes=24 * 2**20),
        cost_estimate=pl.CostEstimate(flops=8 * 10**9, bytes_accessed=10**7, transcendentals=0),
        name="left",
    )(me, directions, spin_mats, chain_order, *elem_parts, *fwd_parts.values())
    return pl.pallas_call(
        functools.partial(right_kernel, gz_n, tuple(bwd_parts)),
        out_shape=jax.ShapeDtypeStruct((op_count, 2, rows, cols), BF16),
        in_specs=[VMEM] * (1 + len(bwd_parts)),
        out_specs=VMEM,
        scratch_shapes=[pltpu.VMEM((8 * num_vecs, 2 * cols), BF16)],
        compiler_params=pltpu.CompilerParams(vmem_limit_bytes=24 * 2**20),
        name="right",
    )(left, *bwd_parts.values())


def solution(mesh):
    in_specs = (
        P("gx", "gy", "gz", None, None, None),
        P("gx", "gy", "gz", None, None, None, None),
        P(),
        P(),
        P(None, "gx", "gy"),
        P(None, "gx", "gy"),
        P("gz", None),
    )
    out_specs = P("gz", None, "gx", "gy")
    return jax.shard_map(
        on_device, mesh=mesh, in_specs=in_specs, out_specs=out_specs, check_vma=False
    )
```

```python
import functools
import math

import jax
import jax.numpy as jnp
from jax import lax
from jax.experimental import pallas as pl
from jax.experimental.pallas import tpu as pltpu
from jax.sharding import PartitionSpec as P

VMEM = pl.BlockSpec(memory_space=pltpu.VMEM)
SMEM = pl.BlockSpec(memory_space=pltpu.SMEM)
BF16 = jnp.bfloat16
F32 = jnp.float32


def passed_along(value, axis, steps):
    count = lax.axis_size(axis)
    pairs = [(source, (source + steps) % count) for source in range(count)]
    return lax.ppermute(value, axis, pairs)


def mm(left, right):
    return jnp.dot(left, right, preferred_element_type=F32)


def parts_of(value, divisor):
    quotient = jnp.floor((value + 0.5) * (1.0 / divisor))
    return quotient, value - quotient * divisor


def whole_numbers(shape, axis):
    return lax.broadcasted_iota(jnp.int32, shape, axis).astype(F32)


def chosen(condition):
    return jnp.where(condition, 1.0, 0.0)


def coordinates(index, extent):
    rest, third = parts_of(index, extent[2])
    first, second = parts_of(rest, extent[1])
    return [first, second, third]


def source_columns(extent, e):
    count = math.prod(extent)
    face = count // extent[e]
    inner = count - face if e == 0 else count
    total = 6 * (inner + face)
    column = whole_numbers((1, total), 1)
    beyond = chosen(column >= 6 * inner)
    site, left = parts_of(column - beyond * (6 * inner), 6)
    colour, part = parts_of(left, 2)
    within = coordinates(site, extent)
    if e == 0:
        within[0] = within[0] + 1
    flat = [n for d, n in enumerate(extent) if d != e]
    outer, last = parts_of(site, flat[1])
    edge = [outer, last]
    edge.insert(e, jnp.full_like(site, extent[e]))
    where = [w + beyond * (o - w) for w, o in zip(within, edge)]
    return total, part, where, colour


def eig_rows(eig_ref):
    return eig_ref[...].astype(F32).reshape(2 * eig_ref.shape[0], eig_ref.shape[2])


def faces_kernel(extent, eig_ref, *face_outs):
    vec = eig_rows(eig_ref)
    strides = (6 * extent[1] * extent[2], 6 * extent[2], 6)
    for e, out in enumerate(face_outs):
        begins = [0]
        for d in range(e):
            begins = [at + n * strides[d] for at in begins for n in range(extent[d])]
        runs = [vec[at : at + strides[e]] for at in begins]
        out[...] = (jnp.concatenate(runs, axis=0) if e else runs[0]).astype(BF16)


def pieces_kernel(z_ref, fwd_in, bwd_in, fwd_out, bwd_out, fwd_ref, bwd_ref, sems):
    pairs = ((fwd_in, fwd_ref), (bwd_in, bwd_ref))
    copies = [pltpu.make_async_copy(source, target, sems.at[n]) for n, (source, target) in enumerate(pairs)]
    for copy in copies:
        copy.start()
    rows, cols = fwd_ref.shape[1:]
    piece = fwd_out.shape[1]
    per_spin = rows // 4
    lane = cols // 4
    flat = lax.broadcasted_iota(jnp.int32, (piece, 1), 0) + z_ref[0] * piece
    spin = jnp.zeros_like(flat)
    for t in range(1, 4):
        spin += jnp.where(flat >= t * per_spin, 1, 0)
    source = 4 * (flat - spin * per_spin) + spin
    select = chosen(lax.broadcasted_iota(jnp.int32, (piece, rows), 1) == source).astype(BF16)
    column = lax.broadcasted_iota(jnp.int32, (1, cols), 1)
    spin = jnp.zeros_like(column)
    for t in range(1, 4):
        spin += jnp.where(column >= t * lane, 1, 0)
    source = 4 * (column - spin * lane) + spin
    perm = chosen(lax.broadcasted_iota(jnp.int32, (cols, cols), 0) == source).astype(BF16)
    copies[0].wait()
    for c in range(2):
        picked = mm(select, fwd_ref[c]).astype(BF16)
        fwd_out[c] = mm(picked, perm).astype(BF16)
    copies[1].wait()
    for c in range(2):
        bwd_out[c] = mm(select, bwd_ref[c]).astype(BF16)


def links_kernel(extent, link_ref, *outs):
    count = math.prod(extent)
    rows = 6 * count
    row = whole_numbers((rows, 1), 0)
    row_site, left = parts_of(row, 6)
    row_colour, row_part = parts_of(left, 2)
    row_where = coordinates(row_site, extent)
    link = link_ref[...]
    high = link.astype(BF16)
    rest = link - high.astype(F32)
    mid = rest.astype(BF16)
    low = (rest - mid.astype(F32)).astype(BF16)
    spread = chosen(row_site == whole_numbers((rows, count), 1)).astype(BF16)
    by_row = [mm(spread, part) for part in (high, mid, low)]
    by_row = [jnp.concatenate([part, part], axis=1) for part in by_row]

    def entry_of(entry):
        half = chosen(entry >= 54)
        direction, left = parts_of(entry - 54 * half, 18)
        part, left = parts_of(left, 9)
        into, out_of = parts_of(left, 3)
        return half, direction, part, into, out_of

    half, direction, _, into, _ = entry_of(whole_numbers((1, 108), 1))
    own_part = (half == row_part) & (into == row_colour)
    place_half, _, place_part, _, place_colour = entry_of(whole_numbers((108, 1), 0))
    for e, out in enumerate(outs):
        keep = chosen(own_part & (direction == e))
        picked = jnp.concatenate([part * keep for part in by_row], axis=0).astype(BF16)
        total, part, where, colour = source_columns(extent, e)
        sign = 1.0 - 2.0 * part * (1.0 - place_half)
        match = (place_colour == colour) & (jnp.abs(place_part - part) == place_half)
        placed = mm(picked, jnp.where(match, sign, 0.0).astype(BF16))
        same = None
        for d in range(3):
            hit = row_where[d] + (1.0 if d == e else 0.0) == where[d]
            same = hit if same is None else same & hit
        mask = chosen(same)
        for n in range(3):
            at = slice(n * rows, (n + 1) * rows)
            out[at, :] = (placed[at] * mask).astype(BF16)


def correlate_kernel(scale, eig_ref, face0, face1, face2, mat0, mat1, mat2, out_ref):
    gz_n, gx_n, split, depth, width = out_ref.shape
    each = 6 // split
    own_rows = depth // each
    vec = eig_rows(eig_ref).astype(BF16)
    rows = vec.shape[0]
    row = lax.broadcasted_iota(jnp.int32, (rows, rows), 0)
    column = lax.broadcasted_iota(jnp.int32, (rows, rows), 1)
    odd = lax.rem(row, 2) == 1
    turn = jnp.where(odd & (column == row - 1), -1.0, chosen((column == row + 1) & ~odd)).astype(BF16)
    sources = [
        jnp.concatenate([vec[face0.shape[0] :], face0[...]], axis=0),
        jnp.concatenate([vec, face1[...]], axis=0),
        jnp.concatenate([vec, face2[...]], axis=0),
    ]
    for e, mat in enumerate((mat0, mat1, mat2)):
        terms = mm(mat[...], sources[e])
        moved = terms[:rows] + terms[rows : 2 * rows] + terms[2 * rows :]
        moved = moved.astype(BF16)
        turned = mm(turn, moved).astype(BF16)
        right = jnp.concatenate([moved, turned], axis=1)
        product = lax.dot_general(
            vec, right, (((0,), (0,)), ((), ())), preferred_element_type=F32
        )
        product = (product * scale).astype(BF16)
        for c in range(2):
            n = 2 * e + c
            half = product[:, c * width : (c + 1) * width]
            to = slice(n % each * own_rows, (n % each + 1) * own_rows)
            for g in range(gx_n):
                for z in range(gz_n):
                    at = (g * gz_n + z) * own_rows
                    out_ref[z, g, n // each, to] = half[at : at + own_rows]


def spin_groups(gz_n):
    keys = [(dy, dc) for dc in range(2) for dy in range(gz_n // 2)]
    if gz_n == 4:
        return [[key] for key in keys]
    return [[(dy, dc) for dc in range(2)] for dy in range(gz_n // 2)]


def rows_of(parts, c, count):
    rows = jnp.concatenate([part[:, c] for part in parts], axis=1)
    return rows.reshape(count, rows.shape[-1])


def right_kernel(gz_n, keys, left_ref, *refs):
    bwd_at = dict(zip(keys, refs))
    out_ref, b_ref = refs[len(keys) :]
    num_vecs = b_ref.shape[0] // 8
    op_count, _, row_count, width = out_ref.shape
    for t, group in enumerate(spin_groups(gz_n)):
        real, imag = [rows_of([bwd_at[key] for key in group], c, num_vecs) for c in range(2)]
        at = 2 * t * num_vecs
        b_ref[at : at + num_vecs, :width] = real
        b_ref[at : at + num_vecs, width:] = imag
        b_ref[at + num_vecs : at + 2 * num_vecs, :width] = -imag
        b_ref[at + num_vecs : at + 2 * num_vecs, width:] = real
    left = left_ref[...].reshape(op_count * row_count, 8 * num_vecs)
    block = min(width, 256)
    for c in range(2):
        for begin in range(0, width, block):
            at = c * width + begin
            result = mm(left, b_ref[:, at : at + block]).astype(BF16)
            out_ref[:, c, :, begin : begin + block] = result.reshape(op_count, row_count, block)


def left_kernel(inverse, plan, me_ref, dirs_ref, spin_ref, chain_ref, *refs):
    line, fwd_keys = plan
    elem_in, refs = refs[:2], refs[2:]
    fwd_in, refs = refs[: len(fwd_keys)], refs[len(fwd_keys) :]
    out_ref, elem_all, elem_ref, x_ref, p_ref = refs
    gx_n, gz_n, split, depth, num_vecs = elem_all.shape
    each = 6 // split
    own_rows = depth // each
    width = fwd_in[0].shape[3]
    op_count, row_count, _ = out_ref.shape
    vec_rows = row_count // 4
    gy_n = 4 * num_vecs // width
    lane = width // 4
    halves = gz_n // 4
    gx, gy, gz = me_ref[0], me_ref[1], me_ref[2]

    def back(at, step, count):
        return lax.rem(at - step + count, count)

    def gz_from(dy, dc):
        return back(lax.div(gz, 2), dy, gz_n // 2) * 2 + back(lax.rem(gz, 2), dc, 2)

    for dc, ref in enumerate(elem_in):
        for dy in range(gz_n // 2):
            for n in range(gx_n * split):
                elem_all[n // split, gz_from(dy, dc), n % split] = ref[dy, n]
    column = lax.broadcasted_iota(jnp.int32, (1, num_vecs), 1)
    source = jnp.zeros_like(column)
    half_rows = vec_rows // halves
    for place, offset in enumerate(line):
        for half in range(halves):
            at = place * vec_rows + half * half_rows
            from_half = lax.bitwise_xor(lax.rem(gz, 2), half) if halves == 2 else half
            begin = lax.bitwise_xor(gx, offset) * vec_rows + from_half * half_rows
            inside = (column >= at) & (column < at + half_rows)
            source = jnp.where(inside, column + (begin - at), source)
    perm = chosen(lax.broadcasted_iota(jnp.int32, (num_vecs, num_vecs), 0) == source).astype(BF16)
    for n in range(6):
        rows = slice(n % each * own_rows, (n % each + 1) * own_rows)
        whole = elem_all[:, :, n // each, rows].reshape(num_vecs, num_vecs)
        elem_ref[n] = mm(whole, perm).astype(BF16)

    groups = spin_groups(gz_n)
    spins = [lax.div(gz_from(*group[0]), halves) for group in groups]

    first_row = pl.multiple_of(gx * vec_rows, vec_rows)

    def own(d, c):
        return elem_ref[2 * d + c, pl.ds(first_row, vec_rows), :]

    real_rows = [jnp.concatenate([own(d, 0), -own(d, 1)], axis=1) for d in range(3)]
    imag_rows = [jnp.concatenate([own(d, 1), own(d, 0)], axis=1) for d in range(3)]
    left = jnp.concatenate([part for d in range(3) for part in (real_rows[d], imag_rows[d])], axis=0)
    fwd_at = dict(zip(fwd_keys, fwd_in))
    for t, group in enumerate(groups):
        for dx in range(gy_n):
            parts = [fwd_at[(dx,) + key] for key in group]
            right = jnp.concatenate([rows_of(parts, c, num_vecs) for c in range(2)], axis=0)
            result = mm(left, right).astype(BF16)
            for d in range(3):
                for c in range(2):
                    at = (d * 2 + c) * vec_rows
                    x_ref[d, c, dx, t] = result[at : at + vec_rows]

    row = lax.broadcasted_iota(jnp.int32, (row_count, 1), 0)
    column = lax.broadcasted_iota(jnp.int32, (1, row_count), 1)
    row_spin = lax.rem(row, 4)
    diagonal = lax.div(row, 4) == lax.rem(column, vec_rows)
    column_spin = lax.div(column, vec_rows)
    blocks = [pl.multiple_of(back(gy, dx, gy_n) * lane, lane) for dx in range(gy_n)]

    def one_operator(op):
        a = chain_ref[2 * op]
        b = chain_ref[2 * op + 1]
        dir_a = dirs_ref[a]
        dir_b = dirs_ref[b]
        mix = None
        for t in range(4):
            weight = jnp.full((row_count, 1), spin_ref[a, 0, spins[t]])
            for s in range(1, 4):
                weight = jnp.where(row_spin == s, spin_ref[a, s, spins[t]], weight)
            mix = weight if mix is None else jnp.where(column_spin == t, weight, mix)
        mix = jnp.where(diagonal, mix, 0.0)
        high = mix.astype(BF16)
        low = (mix - high.astype(F32)).astype(BF16)
        mix = jnp.concatenate([high, low], axis=1)
        for c in range(2):
            for dx in range(gy_n):
                source = x_ref[dir_a, c, dx].reshape(row_count, width)
                result = mm(mix, jnp.concatenate([source, source], axis=0)).astype(BF16)
                for s in range(4):
                    to = c * num_vecs + dx * lane
                    p_ref[s, :, to : to + lane] = result[:, s * lane : (s + 1) * lane]

        def elem(c):
            return jnp.concatenate([elem_ref[2 * dir_b + c, pl.ds(at, lane), :] for at in blocks], axis=0)

        real_b, imag_b = elem(0), elem(1)
        right = jnp.concatenate(
            [
                jnp.concatenate([real_b, imag_b], axis=1),
                jnp.concatenate([-imag_b, real_b], axis=1),
            ],
            axis=0,
        )
        parts = [mm(p_ref[s], right) for s in range(4)]
        for t in range(4):
            total = parts[0] * (spin_ref[b, 0, spins[t]] * inverse)
            for s in range(1, 4):
                total += parts[s] * (spin_ref[b, s, spins[t]] * inverse)
            total = total.astype(BF16)
            out_ref[op, :, 2 * t * num_vecs : 2 * (t + 1) * num_vecs] = total

    for op in range(op_count):
        one_operator(op)


def passed_in_gz(value, dy, dc):
    count = lax.axis_size("gz")
    chips = count // 2
    pairs = [(n, ((n // 2 + dy) % chips) * 2 + (n + dc) % 2) for n in range(count)]
    return lax.ppermute(value, "gz", pairs)


def passed_in_plane(value, dx, dy):
    if not dx and not dy:
        return value
    gy_n, gz_n = lax.axis_size("gy"), lax.axis_size("gz")
    chips = gz_n // 2
    pairs = []
    for y in range(gy_n):
        for z in range(gz_n):
            to = (y + dx) % gy_n * gz_n + ((z // 2 + dy) % chips) * 2 + z % 2
            pairs.append((y * gz_n + z, to))
    return lax.ppermute(value, ("gy", "gz"), pairs)


def xor_passed(value, axis, offset):
    return lax.ppermute(value, axis, [(n, n ^ offset) for n in range(lax.axis_size(axis))])


def line_exchange(value, axis, distance, steps, offsets=(0,)):
    gathered = value if len(offsets) > 1 else value[None]
    offsets = list(offsets)
    for _ in range(steps):
        gathered = jnp.concatenate([gathered, xor_passed(gathered, axis, distance)])
        offsets += [offset ^ distance for offset in offsets]
        distance //= 2
    return gathered, tuple(offsets)


def part_at(value, index, axis=0):
    return lax.dynamic_index_in_dim(value, index, axis, keepdims=False)


def added(*values):
    return sum(value.astype(F32) for value in values).astype(BF16)


def on_device(eigvecs, links, directions, spin_mats, forward_peram, backward_peram, chain_order):
    extent = eigvecs.shape[:3]
    num_vecs = eigvecs.shape[-1]
    gx_n, gy_n, gz_n = (lax.axis_size(name) for name in ("gx", "gy", "gz"))
    chips = gz_n // 2
    gx, gy, gz = (lax.axis_index(name).astype(jnp.int32) for name in ("gx", "gy", "gz"))
    me = jnp.stack([gx, gy, gz])
    chip, core = lax.div(gz, 2), lax.rem(gz, 2)

    rows, cols = forward_peram.shape[1:]
    piece = rows // gz_n
    site_rows = 6 * math.prod(extent)
    face_rows = [site_rows // n for n in extent]
    eig = eigvecs.transpose(0, 1, 2, 4, 3, 5).reshape(-1, 2, num_vecs)
    faces = pl.pallas_call(
        functools.partial(faces_kernel, extent),
        out_shape=[jax.ShapeDtypeStruct((n, num_vecs), BF16) for n in face_rows],
        in_specs=[VMEM],
        out_specs=[VMEM] * 3,
        compiler_params=pltpu.CompilerParams(vmem_limit_bytes=24 * 2**20),
        name="faces",
    )(eig)
    faces = [passed_along(face, axis, -1) for face, axis in zip(faces, ("gx", "gy", "gz"))]

    piece_shape = jax.ShapeDtypeStruct((2, piece, cols), BF16)
    fwd_piece, bwd_piece = pl.pallas_call(
        pieces_kernel,
        out_shape=[piece_shape] * 2,
        in_specs=[SMEM] + [pl.BlockSpec(memory_space=pl.ANY)] * 2,
        out_specs=[VMEM] * 2,
        scratch_shapes=[
            pltpu.VMEM(forward_peram.shape, BF16),
            pltpu.VMEM(backward_peram.shape, BF16),
            pltpu.SemaphoreType.DMA((2,)),
        ],
        compiler_params=pltpu.CompilerParams(vmem_limit_bytes=60 * 2**20),
        cost_estimate=pl.CostEstimate(flops=10**8, bytes_accessed=10**7, transcendentals=0),
        name="pieces",
    )(me[2:], forward_peram, backward_peram)
    pairs = chain_order.reshape(-1)
    fwd_piece, links, pairs = lax.optimization_barrier((fwd_piece, links, pairs))
    fwd_half = xor_passed(fwd_piece, "gx", gx_n // 2)

    link_mats = pl.pallas_call(
        functools.partial(links_kernel, extent),
        out_shape=[
            jax.ShapeDtypeStruct((3 * site_rows, site_rows - (0 if e else face_rows[0]) + face_rows[e]), BF16)
            for e in range(3)
        ],
        in_specs=[VMEM],
        out_specs=[VMEM] * 3,
        compiler_params=pltpu.CompilerParams(vmem_limit_bytes=24 * 2**20),
        name="link_matrices",
    )(links.reshape(-1, 54))

    volume = math.prod(extent) * gx_n * gy_n * gz_n
    own_rows = num_vecs // (gz_n * gx_n)
    split = gy_n if 6 % gy_n == 0 and own_rows % 16 == 0 else 1
    depth = 6 * own_rows // split
    partial = pl.pallas_call(
        functools.partial(correlate_kernel, 1.0 / math.sqrt(12.0 * volume)),
        out_shape=jax.ShapeDtypeStruct((gz_n, gx_n, split, depth, num_vecs), BF16),
        in_specs=[VMEM] * 7,
        out_specs=VMEM,
        compiler_params=pltpu.CompilerParams(vmem_limit_bytes=24 * 2**20),
        name="correlate",
    )(eig, *faces, *link_mats)

    rounds = gx_n.bit_length() - 1
    partial, fwd_half = lax.optimization_barrier((partial, fwd_half))
    by_core = partial.reshape((chips, 2) + partial.shape[1:])
    summed = added(part_at(by_core, core, 1), passed_in_gz(part_at(by_core, 1 - core, 1), 0, 1))
    fwd_line = jnp.stack([fwd_piece, fwd_half])
    fwd_line, line = line_exchange(fwd_line, "gx", gx_n // 4, rounds - 1, (0, gx_n // 2))
    summed, bwd_piece = lax.optimization_barrier((summed, bwd_piece))
    bwd_line = jnp.stack([bwd_piece] + [xor_passed(bwd_piece, "gx", offset) for offset in line[1:]])
    summed = added(*[passed_in_gz(part_at(summed, lax.rem(chip + dy, chips)), dy, 0) if dy else part_at(summed, chip) for dy in range(chips)])

    plane = [(dx, dy) for dy in range(chips) for dx in range(gy_n)]
    four = gy_n == 2 and chips == 2
    fwd_parts = {(dx, dy, 0): passed_in_plane(fwd_line, dx, dy) for dx, dy in plane if not (four and dx and dy)}
    fwd_parts[0, 0, 1] = passed_in_gz(fwd_line, 0, 1)

    area = ("gx", "gy") if split > 1 else "gx"
    if split == 1:
        summed = added(summed, *[passed_along(summed, "gy", dx) for dx in range(1, gy_n)])
    summed = lax.all_to_all(summed.reshape(gx_n * split, depth, num_vecs), area, 0, 0, tiled=True)
    summed = jnp.sum(summed.astype(F32), axis=0).astype(BF16)
    over_x = [key for key in fwd_parts if key[0] and not key[1] and not key[2]]
    summed, bwd_line, *parts = lax.optimization_barrier((summed, bwd_line, *[fwd_parts[key] for key in over_x]))
    fwd_parts.update(zip(over_x, parts))
    bwd_parts = {(dy, 0): passed_in_gz(bwd_line, dy, 0) if dy else bwd_line for dy in range(chips)}
    elem_line = lax.all_to_all(jnp.broadcast_to(summed, (gx_n * split, depth, num_vecs)), area, 0, 0, tiled=True)
    if four:
        fwd_parts[1, 1, 0] = passed_in_plane(fwd_parts[0, 1, 0], 1, 0)
    keys = [(0, 0, 1)]
    tied = lax.optimization_barrier((elem_line, *[fwd_parts[key] for key in keys], *bwd_parts.values()))
    elem_line = tied[0]
    fwd_parts.update(zip(keys, tied[1:]))
    bwd_parts.update(zip(list(bwd_parts), tied[2:]))
    elem_own = jnp.stack([passed_in_gz(elem_line, dy, 0) if dy else elem_line for dy in range(chips)])
    elem_parts = [elem_own, passed_in_gz(elem_own, 0, 1)]
    for dx, dy in plane[1:]:
        fwd_parts[dx, dy, 1] = passed_in_gz(fwd_parts[dx, dy, 0], 0, 1)
    for dy in range(chips):
        bwd_parts[dy, 1] = passed_in_gz(bwd_parts[dy, 0], 0, 1)

    op_count = chain_order.shape[0]
    plan = (line, tuple(fwd_parts))
    left_shape = (op_count, rows, 8 * num_vecs)
    left = pl.pallas_call(
        functools.partial(left_kernel, 1.0 / math.sqrt(4 * num_vecs), plan),
        out_shape=jax.ShapeDtypeStruct(left_shape, BF16),
        in_specs=[SMEM] * 4 + [VMEM] * (len(elem_parts) + len(fwd_parts)),
        out_specs=VMEM,
        scratch_shapes=[
            pltpu.VMEM((gx_n, gz_n, split, depth, num_vecs), BF16),
            pltpu.VMEM((6, num_vecs, num_vecs), BF16),
            pltpu.VMEM((3, 2, gy_n, 4, rows // 4, cols), BF16),
            pltpu.VMEM((4, rows, 2 * num_vecs), BF16),
        ],
        compiler_params=pltpu.CompilerParams(vmem_limit_bytes=24 * 2**20),
        cost_estimate=pl.CostEstimate(flops=8 * 10**9, bytes_accessed=10**7, transcendentals=0),
        name="left",
    )(me, directions, spin_mats, pairs, *elem_parts, *fwd_parts.values())
    return pl.pallas_call(
        functools.partial(right_kernel, gz_n, tuple(bwd_parts)),
        out_shape=jax.ShapeDtypeStruct((op_count, 2, rows, cols), BF16),
        in_specs=[VMEM] * (1 + len(bwd_parts)),
        out_specs=VMEM,
        scratch_shapes=[pltpu.VMEM((8 * num_vecs, 2 * cols), BF16)],
        compiler_params=pltpu.CompilerParams(vmem_limit_bytes=24 * 2**20),
        name="right",
    )(left, *bwd_parts.values())


def solution(mesh):
    in_specs = (
        P("gx", "gy", "gz", None, None, None),
        P("gx", "gy", "gz", None, None, None, None),
        P(),
        P(),
        P(None, "gx", "gy"),
        P(None, "gx", "gy"),
        P("gz", None),
    )
    out_specs = P("gz", None, "gx", "gy")
    return jax.shard_map(
        on_device, mesh=mesh, in_specs=in_specs, out_specs=out_specs, check_vma=False
    )
```

```python
import functools
import math

import jax
import jax.numpy as jnp
from jax import lax
from jax.experimental import pallas as pl
from jax.experimental.pallas import tpu as pltpu
from jax.sharding import PartitionSpec as P

VMEM = pl.BlockSpec(memory_space=pltpu.VMEM)
SMEM = pl.BlockSpec(memory_space=pltpu.SMEM)
BF16 = jnp.bfloat16
F32 = jnp.float32


def passed_along(value, axis, steps):
    count = lax.axis_size(axis)
    pairs = [(source, (source + steps) % count) for source in range(count)]
    return lax.ppermute(value, axis, pairs)


def mm(left, right):
    return jnp.dot(left, right, preferred_element_type=F32)


def parts_of(value, divisor):
    quotient = jnp.floor((value + 0.5) * (1.0 / divisor))
    return quotient, value - quotient * divisor


def whole_numbers(shape, axis):
    return lax.broadcasted_iota(jnp.int32, shape, axis).astype(F32)


def chosen(condition):
    return jnp.where(condition, 1.0, 0.0)


def coordinates(index, extent):
    rest, third = parts_of(index, extent[2])
    first, second = parts_of(rest, extent[1])
    return [first, second, third]


def source_columns(extent, e):
    count = math.prod(extent)
    face = count // extent[e]
    inner = count - face if e == 0 else count
    total = 6 * (inner + face)
    column = whole_numbers((1, total), 1)
    beyond = chosen(column >= 6 * inner)
    site, left = parts_of(column - beyond * (6 * inner), 6)
    colour, part = parts_of(left, 2)
    within = coordinates(site, extent)
    if e == 0:
        within[0] = within[0] + 1
    flat = [n for d, n in enumerate(extent) if d != e]
    outer, last = parts_of(site, flat[1])
    edge = [outer, last]
    edge.insert(e, jnp.full_like(site, extent[e]))
    where = [w + beyond * (o - w) for w, o in zip(within, edge)]
    return total, part, where, colour


def rows_kernel(extent, eig_ref, vec_out, *face_outs):
    vec = eig_ref[...].astype(F32).reshape(vec_out.shape)
    vec_out[...] = vec.astype(BF16)
    strides = (6 * extent[1] * extent[2], 6 * extent[2], 6)
    for e, out in enumerate(face_outs):
        begins = [0]
        for d in range(e):
            begins = [at + n * strides[d] for at in begins for n in range(extent[d])]
        runs = [vec[at : at + strides[e]] for at in begins]
        out[...] = (jnp.concatenate(runs, axis=0) if e else runs[0]).astype(BF16)


def pieces_kernel(z_ref, fwd_in, bwd_in, fwd_out, bwd_out, fwd_ref, bwd_ref, sems):
    pairs = ((fwd_in, fwd_ref), (bwd_in, bwd_ref))
    copies = [pltpu.make_async_copy(source, target, sems.at[n]) for n, (source, target) in enumerate(pairs)]
    for copy in copies:
        copy.start()
    rows, cols = fwd_ref.shape[1:]
    piece = fwd_out.shape[1]
    per_spin = rows // 4
    lane = cols // 4
    flat = lax.broadcasted_iota(jnp.int32, (piece, 1), 0) + z_ref[0] * piece
    spin = jnp.zeros_like(flat)
    for t in range(1, 4):
        spin += jnp.where(flat >= t * per_spin, 1, 0)
    source = 4 * (flat - spin * per_spin) + spin
    select = chosen(lax.broadcasted_iota(jnp.int32, (piece, rows), 1) == source).astype(BF16)
    column = lax.broadcasted_iota(jnp.int32, (1, cols), 1)
    spin = jnp.zeros_like(column)
    for t in range(1, 4):
        spin += jnp.where(column >= t * lane, 1, 0)
    source = 4 * (column - spin * lane) + spin
    perm = chosen(lax.broadcasted_iota(jnp.int32, (cols, cols), 0) == source).astype(BF16)
    copies[0].wait()
    for c in range(2):
        picked = mm(select, fwd_ref[c]).astype(BF16)
        fwd_out[c] = mm(picked, perm).astype(BF16)
    copies[1].wait()
    for c in range(2):
        bwd_out[c] = mm(select, bwd_ref[c]).astype(BF16)


def links_kernel(extent, link_ref, *outs):
    count = math.prod(extent)
    rows = 6 * count
    row = whole_numbers((rows, 1), 0)
    row_site, left = parts_of(row, 6)
    row_colour, row_part = parts_of(left, 2)
    row_where = coordinates(row_site, extent)
    link = link_ref[...]
    high = link.astype(BF16)
    rest = link - high.astype(F32)
    mid = rest.astype(BF16)
    low = (rest - mid.astype(F32)).astype(BF16)
    spread = chosen(row_site == whole_numbers((rows, count), 1)).astype(BF16)
    by_row = [mm(spread, part) for part in (high, mid, low)]
    by_row = [jnp.concatenate([part, part], axis=1) for part in by_row]

    def entry_of(entry):
        half = chosen(entry >= 54)
        direction, left = parts_of(entry - 54 * half, 18)
        part, left = parts_of(left, 9)
        into, out_of = parts_of(left, 3)
        return half, direction, part, into, out_of

    half, direction, _, into, _ = entry_of(whole_numbers((1, 108), 1))
    own_part = (half == row_part) & (into == row_colour)
    place_half, _, place_part, _, place_colour = entry_of(whole_numbers((108, 1), 0))
    for e, out in enumerate(outs):
        keep = chosen(own_part & (direction == e))
        picked = jnp.concatenate([part * keep for part in by_row], axis=0).astype(BF16)
        total, part, where, colour = source_columns(extent, e)
        sign = 1.0 - 2.0 * part * (1.0 - place_half)
        match = (place_colour == colour) & (jnp.abs(place_part - part) == place_half)
        placed = mm(picked, jnp.where(match, sign, 0.0).astype(BF16))
        same = None
        for d in range(3):
            hit = row_where[d] + (1.0 if d == e else 0.0) == where[d]
            same = hit if same is None else same & hit
        mask = chosen(same)
        for n in range(3):
            at = slice(n * rows, (n + 1) * rows)
            out[at, :] = (placed[at] * mask).astype(BF16)


def correlate_kernel(scale, vec_ref, face0, face1, face2, mat0, mat1, mat2, out_ref):
    gz_n, gx_n, split, depth, width = out_ref.shape
    each = 6 // split
    own_rows = depth // each
    vec = vec_ref[...]
    rows = vec.shape[0]
    row = lax.broadcasted_iota(jnp.int32, (rows, rows), 0)
    column = lax.broadcasted_iota(jnp.int32, (rows, rows), 1)
    odd = lax.rem(row, 2) == 1
    turn = jnp.where(odd & (column == row - 1), -1.0, chosen((column == row + 1) & ~odd)).astype(BF16)
    sources = [
        jnp.concatenate([vec[face0.shape[0] :], face0[...]], axis=0),
        jnp.concatenate([vec, face1[...]], axis=0),
        jnp.concatenate([vec, face2[...]], axis=0),
    ]
    for e, mat in enumerate((mat0, mat1, mat2)):
        terms = mm(mat[...], sources[e])
        moved = terms[:rows] + terms[rows : 2 * rows] + terms[2 * rows :]
        moved = moved.astype(BF16)
        turned = mm(turn, moved).astype(BF16)
        right = jnp.concatenate([moved, turned], axis=1)
        product = lax.dot_general(
            vec, right, (((0,), (0,)), ((), ())), preferred_element_type=F32
        )
        product = (product * scale).astype(BF16)
        for c in range(2):
            n = 2 * e + c
            half = product[:, c * width : (c + 1) * width]
            to = slice(n % each * own_rows, (n % each + 1) * own_rows)
            for g in range(gx_n):
                for z in range(gz_n):
                    at = (g * gz_n + z) * own_rows
                    out_ref[z, g, n // each, to] = half[at : at + own_rows]


def spin_groups(gz_n):
    keys = [(dy, dc) for dc in range(2) for dy in range(gz_n // 2)]
    if gz_n == 4:
        return [[key] for key in keys]
    return [[(dy, dc) for dc in range(2)] for dy in range(gz_n // 2)]


def rows_of(parts, c, count):
    rows = jnp.concatenate([part[:, c] for part in parts], axis=1)
    return rows.reshape(count, rows.shape[-1])


def right_kernel(gz_n, keys, left_ref, *refs):
    bwd_at = dict(zip(keys, refs))
    out_ref, b_ref = refs[len(keys) :]
    num_vecs = b_ref.shape[0] // 8
    op_count, _, row_count, width = out_ref.shape
    for t, group in enumerate(spin_groups(gz_n)):
        real, imag = [rows_of([bwd_at[key] for key in group], c, num_vecs) for c in range(2)]
        at = 2 * t * num_vecs
        b_ref[at : at + num_vecs, :width] = real
        b_ref[at : at + num_vecs, width:] = imag
        b_ref[at + num_vecs : at + 2 * num_vecs, :width] = -imag
        b_ref[at + num_vecs : at + 2 * num_vecs, width:] = real
    left = left_ref[...].reshape(op_count * row_count, 8 * num_vecs)
    block = min(width, 256)
    for c in range(2):
        for begin in range(0, width, block):
            at = c * width + begin
            result = mm(left, b_ref[:, at : at + block]).astype(BF16)
            out_ref[:, c, :, begin : begin + block] = result.reshape(op_count, row_count, block)


def left_kernel(inverse, plan, me_ref, dirs_ref, spin_ref, chain_ref, *refs):
    line, elem_keys, fwd_keys = plan
    elem_in, refs = refs[:2], refs[2:]
    fwd_in, refs = refs[: len(fwd_keys)], refs[len(fwd_keys) :]
    out_ref, elem_all, elem_ref, x_ref, p_ref = refs
    gx_n, gz_n, split, depth, num_vecs = elem_all.shape
    each = 6 // split
    own_rows = depth // each
    width = fwd_in[0].shape[3]
    op_count, row_count, _ = out_ref.shape
    vec_rows = row_count // 4
    gy_n = 4 * num_vecs // width
    lane = width // 4
    halves = gz_n // 4
    gx, gy, gz = me_ref[0], me_ref[1], me_ref[2]

    def back(at, step, count):
        return lax.rem(at - step + count, count)

    def gz_from(dy, dc):
        return back(lax.div(gz, 2), dy, gz_n // 2) * 2 + back(lax.rem(gz, 2), dc, 2)

    for dc, ref in enumerate(elem_in):
        for n, (dx, dy) in enumerate(elem_keys):
            for place, offset in enumerate(line):
                to = lax.bitwise_xor(gx, offset), gz_from(dy, dc), back(gy, dx, gy_n) if split > 1 else 0
                elem_all[to] = ref[n, place]
    column = lax.broadcasted_iota(jnp.int32, (1, num_vecs), 1)
    source = jnp.zeros_like(column)
    half_rows = vec_rows // halves
    for place, offset in enumerate(line):
        for half in range(halves):
            at = place * vec_rows + half * half_rows
            from_half = lax.bitwise_xor(lax.rem(gz, 2), half) if halves == 2 else half
            begin = lax.bitwise_xor(gx, offset) * vec_rows + from_half * half_rows
            inside = (column >= at) & (column < at + half_rows)
            source = jnp.where(inside, column + (begin - at), source)
    perm = chosen(lax.broadcasted_iota(jnp.int32, (num_vecs, num_vecs), 0) == source).astype(BF16)
    for n in range(6):
        rows = slice(n % each * own_rows, (n % each + 1) * own_rows)
        whole = elem_all[:, :, n // each, rows].reshape(num_vecs, num_vecs)
        elem_ref[n] = mm(whole, perm).astype(BF16)

    groups = spin_groups(gz_n)
    spins = [lax.div(gz_from(*group[0]), halves) for group in groups]

    first_row = pl.multiple_of(gx * vec_rows, vec_rows)

    def own(d, c):
        return elem_ref[2 * d + c, pl.ds(first_row, vec_rows), :]

    real_rows = [jnp.concatenate([own(d, 0), -own(d, 1)], axis=1) for d in range(3)]
    imag_rows = [jnp.concatenate([own(d, 1), own(d, 0)], axis=1) for d in range(3)]
    left = jnp.concatenate([part for d in range(3) for part in (real_rows[d], imag_rows[d])], axis=0)
    fwd_at = dict(zip(fwd_keys, fwd_in))
    for t, group in enumerate(groups):
        for dx in range(gy_n):
            parts = [fwd_at[(dx,) + key] for key in group]
            right = jnp.concatenate([rows_of(parts, c, num_vecs) for c in range(2)], axis=0)
            result = mm(left, right).astype(BF16)
            for d in range(3):
                for c in range(2):
                    at = (d * 2 + c) * vec_rows
                    x_ref[d, c, dx, t] = result[at : at + vec_rows]

    row = lax.broadcasted_iota(jnp.int32, (row_count, 1), 0)
    column = lax.broadcasted_iota(jnp.int32, (1, row_count), 1)
    row_spin = lax.rem(row, 4)
    diagonal = lax.div(row, 4) == lax.rem(column, vec_rows)
    column_spin = lax.div(column, vec_rows)
    blocks = [pl.multiple_of(back(gy, dx, gy_n) * lane, lane) for dx in range(gy_n)]

    def one_operator(op):
        a = chain_ref[op, 0]
        b = chain_ref[op, 1]
        dir_a = dirs_ref[a]
        dir_b = dirs_ref[b]
        mix = None
        for t in range(4):
            weight = jnp.full((row_count, 1), spin_ref[a, 0, spins[t]])
            for s in range(1, 4):
                weight = jnp.where(row_spin == s, spin_ref[a, s, spins[t]], weight)
            mix = weight if mix is None else jnp.where(column_spin == t, weight, mix)
        mix = jnp.where(diagonal, mix, 0.0)
        high = mix.astype(BF16)
        low = (mix - high.astype(F32)).astype(BF16)
        mix = jnp.concatenate([high, low], axis=0)
        for c in range(2):
            for dx in range(gy_n):
                source = x_ref[dir_a, c, dx].reshape(row_count, width)
                both = mm(mix, source)
                result = (both[:row_count] + both[row_count:]).astype(BF16)
                for s in range(4):
                    to = c * num_vecs + dx * lane
                    p_ref[s, :, to : to + lane] = result[:, s * lane : (s + 1) * lane]

        def elem(c):
            return jnp.concatenate([elem_ref[2 * dir_b + c, pl.ds(at, lane), :] for at in blocks], axis=0)

        real_b, imag_b = elem(0), elem(1)
        right = jnp.concatenate(
            [
                jnp.concatenate([real_b, imag_b], axis=1),
                jnp.concatenate([-imag_b, real_b], axis=1),
            ],
            axis=0,
        )
        product = mm(p_ref[...].reshape(4 * row_count, 2 * num_vecs), right)
        parts = [product[s * row_count : (s + 1) * row_count] for s in range(4)]
        for t in range(4):
            total = parts[0] * (spin_ref[b, 0, spins[t]] * inverse)
            for s in range(1, 4):
                total += parts[s] * (spin_ref[b, s, spins[t]] * inverse)
            total = total.astype(BF16)
            out_ref[op, :, 2 * t * num_vecs : 2 * (t + 1) * num_vecs] = total

    for op in range(op_count):
        one_operator(op)


def passed_in_gz(value, dy, dc):
    count = lax.axis_size("gz")
    chips = count // 2
    pairs = [(n, ((n // 2 + dy) % chips) * 2 + (n + dc) % 2) for n in range(count)]
    return lax.ppermute(value, "gz", pairs)


def passed_in_plane(value, dx, dy):
    if not dx and not dy:
        return value
    gy_n, gz_n = lax.axis_size("gy"), lax.axis_size("gz")
    chips = gz_n // 2
    pairs = []
    for y in range(gy_n):
        for z in range(gz_n):
            to = (y + dx) % gy_n * gz_n + ((z // 2 + dy) % chips) * 2 + z % 2
            pairs.append((y * gz_n + z, to))
    return lax.ppermute(value, ("gy", "gz"), pairs)


def xor_passed(value, axis, offset):
    if not offset:
        return value
    return lax.ppermute(value, axis, [(n, n ^ offset) for n in range(lax.axis_size(axis))])


def line_exchange(value, axis, distance, steps, offsets=(0,)):
    gathered = value if len(offsets) > 1 else value[None]
    offsets = list(offsets)
    for _ in range(steps):
        gathered = jnp.concatenate([gathered, xor_passed(gathered, axis, distance)])
        offsets += [offset ^ distance for offset in offsets]
        distance //= 2
    return gathered, tuple(offsets)


def part_at(value, index, axis=0):
    return lax.dynamic_index_in_dim(value, index, axis, keepdims=False)


def added(*values):
    return sum(value.astype(F32) for value in values).astype(BF16)


def on_device(eigvecs, links, directions, spin_mats, forward_peram, backward_peram, chain_order):
    extent = eigvecs.shape[:3]
    num_vecs = eigvecs.shape[-1]
    gx_n, gy_n, gz_n = (lax.axis_size(name) for name in ("gx", "gy", "gz"))
    chips = gz_n // 2
    gx, gy, gz = (lax.axis_index(name).astype(jnp.int32) for name in ("gx", "gy", "gz"))
    me = jnp.stack([gx, gy, gz])
    chip, core = lax.div(gz, 2), lax.rem(gz, 2)

    rows, cols = forward_peram.shape[1:]
    piece = rows // gz_n
    site_rows = 6 * math.prod(extent)
    face_rows = [site_rows // n for n in extent]
    vec, *faces = pl.pallas_call(
        functools.partial(rows_kernel, extent),
        out_shape=[jax.ShapeDtypeStruct((n, num_vecs), BF16) for n in [site_rows] + face_rows],
        in_specs=[VMEM],
        out_specs=[VMEM] * 4,
        compiler_params=pltpu.CompilerParams(vmem_limit_bytes=24 * 2**20),
        name="rows",
    )(eigvecs.transpose(0, 1, 2, 4, 3, 5).reshape(-1, 2, num_vecs))
    faces = [passed_along(face, axis, -1) for face, axis in zip(faces, ("gx", "gy", "gz"))]

    piece_shape = jax.ShapeDtypeStruct((2, piece, cols), BF16)
    fwd_piece, bwd_piece = pl.pallas_call(
        pieces_kernel,
        out_shape=[piece_shape] * 2,
        in_specs=[SMEM] + [pl.BlockSpec(memory_space=pl.ANY)] * 2,
        out_specs=[VMEM] * 2,
        scratch_shapes=[
            pltpu.VMEM(forward_peram.shape, BF16),
            pltpu.VMEM(backward_peram.shape, BF16),
            pltpu.SemaphoreType.DMA((2,)),
        ],
        compiler_params=pltpu.CompilerParams(vmem_limit_bytes=60 * 2**20),
        cost_estimate=pl.CostEstimate(flops=10**8, bytes_accessed=10**7, transcendentals=0),
        name="pieces",
    )(me[2:], forward_peram, backward_peram)
    fwd_piece, links = lax.optimization_barrier((fwd_piece, links))
    fwd_half = xor_passed(fwd_piece, "gx", gx_n // 2)

    link_mats = pl.pallas_call(
        functools.partial(links_kernel, extent),
        out_shape=[
            jax.ShapeDtypeStruct((3 * site_rows, site_rows - (0 if e else face_rows[0]) + face_rows[e]), BF16)
            for e in range(3)
        ],
        in_specs=[VMEM],
        out_specs=[VMEM] * 3,
        compiler_params=pltpu.CompilerParams(vmem_limit_bytes=24 * 2**20),
        name="link_matrices",
    )(links.reshape(-1, 54))

    volume = math.prod(extent) * gx_n * gy_n * gz_n
    own_rows = num_vecs // (gz_n * gx_n)
    split = gy_n if 6 % gy_n == 0 and own_rows % 16 == 0 else 1
    depth = 6 * own_rows // split
    partial = pl.pallas_call(
        functools.partial(correlate_kernel, 1.0 / math.sqrt(12.0 * volume)),
        out_shape=jax.ShapeDtypeStruct((gz_n, gx_n, split, depth, num_vecs), BF16),
        in_specs=[VMEM] * 7,
        out_specs=VMEM,
        compiler_params=pltpu.CompilerParams(vmem_limit_bytes=24 * 2**20),
        name="correlate",
    )(vec, *faces, *link_mats)

    rounds = gx_n.bit_length() - 1
    partial, fwd_half = lax.optimization_barrier((partial, fwd_half))
    by_core = partial.reshape((chips, 2) + partial.shape[1:])
    summed = added(part_at(by_core, core, 1), passed_in_gz(part_at(by_core, 1 - core, 1), 0, 1))
    fwd_line, line = line_exchange(jnp.stack([fwd_piece, fwd_half]), "gx", gx_n // 4, rounds - 1, (0, gx_n // 2))
    plane = [(dx, dy) for dy in range(chips) for dx in range(gy_n)]

    def plane_part(dx, dy):
        part = part_at(summed, lax.rem(chip + dy, chips))
        return part_at(part, lax.rem(gy + dx, gy_n) if split > 1 else 0, 1)

    summed = added(*[passed_in_plane(plane_part(dx, dy), dx, dy) for dx, dy in plane])
    if split == 1:
        summed = added(summed, *[passed_along(summed, "gy", dx) for dx in range(1, gy_n)])
    summed, fwd_line = lax.optimization_barrier((summed, fwd_line))

    four = gy_n == 2 and chips == 2
    fwd_parts = {(dx, dy, 0): passed_in_plane(fwd_line, dx, dy) for dx, dy in plane if not (four and dx and dy)}
    others = [lax.bitwise_xor(gx, offset) for offset in line]
    summed = added(*[xor_passed(part_at(summed, to), "gx", offset) for to, offset in zip(others, line)])
    elem_line = jnp.stack([xor_passed(summed, "gx", offset) for offset in line])
    keys = [key for key in fwd_parts if key != (0, 0, 0)]
    elem_line, bwd_piece, *parts = lax.optimization_barrier((elem_line, bwd_piece, *[fwd_parts[key] for key in keys]))
    fwd_parts.update(zip(keys, parts))
    elem_keys = plane if split > 1 else [(0, dy) for dy in range(chips)]
    elem_own = jnp.stack([passed_in_plane(elem_line, dx, dy) for dx, dy in elem_keys])
    if four:
        fwd_parts[1, 1, 0] = passed_in_plane(fwd_parts[0, 1, 0], 1, 0)
    bwd_half = xor_passed(bwd_piece, "gx", gx_n // 2)
    elem_own, bwd_half = lax.optimization_barrier((elem_own, bwd_half))
    elem_parts = [elem_own, passed_in_gz(elem_own, 0, 1)]
    for dx, dy in plane:
        fwd_parts[dx, dy, 1] = passed_in_gz(fwd_parts[dx, dy, 0], 0, 1)
    bwd_line, _ = line_exchange(jnp.stack([bwd_piece, bwd_half]), "gx", gx_n // 4, rounds - 1, (0, gx_n // 2))
    bwd_parts = {(dy, 0): passed_in_gz(bwd_line, dy, 0) if dy else bwd_line for dy in range(chips)}

    op_count = chain_order.shape[0]
    plan = (line, tuple(elem_keys), tuple(fwd_parts))
    left_shape = (op_count, rows, 8 * num_vecs)
    left = pl.pallas_call(
        functools.partial(left_kernel, 1.0 / math.sqrt(4 * num_vecs), plan),
        out_shape=jax.ShapeDtypeStruct(left_shape, BF16),
        in_specs=[SMEM] * 4 + [VMEM] * (len(elem_parts) + len(fwd_parts)),
        out_specs=VMEM,
        scratch_shapes=[
            pltpu.VMEM((gx_n, gz_n, split, depth, num_vecs), BF16),
            pltpu.VMEM((6, num_vecs, num_vecs), BF16),
            pltpu.VMEM((3, 2, gy_n, 4, rows // 4, cols), BF16),
            pltpu.VMEM((4, rows, 2 * num_vecs), BF16),
        ],
        compiler_params=pltpu.CompilerParams(vmem_limit_bytes=24 * 2**20),
        cost_estimate=pl.CostEstimate(flops=8 * 10**9, bytes_accessed=10**7, transcendentals=0),
        name="left",
    )(me, directions, spin_mats, chain_order, *elem_parts, *fwd_parts.values())
    left, *parts = lax.optimization_barrier((left, *bwd_parts.values()))
    bwd_parts = dict(zip(list(bwd_parts), parts))
    for dy in range(chips):
        bwd_parts[dy, 1] = passed_in_gz(bwd_parts[dy, 0], 0, 1)
    return pl.pallas_call(
        functools.partial(right_kernel, gz_n, tuple(bwd_parts)),
        out_shape=jax.ShapeDtypeStruct((op_count, 2, rows, cols), BF16),
        in_specs=[VMEM] * (1 + len(bwd_parts)),
        out_specs=VMEM,
        scratch_shapes=[pltpu.VMEM((8 * num_vecs, 2 * cols), BF16)],
        compiler_params=pltpu.CompilerParams(vmem_limit_bytes=24 * 2**20),
        name="right",
    )(left, *bwd_parts.values())


def solution(mesh):
    in_specs = (
        P("gx", "gy", "gz", None, None, None),
        P("gx", "gy", "gz", None, None, None, None),
        P(),
        P(),
        P(None, "gx", "gy"),
        P(None, "gx", "gy"),
        P("gz", None),
    )
    out_specs = P("gz", None, "gx", "gy")
    return jax.shard_map(
        on_device, mesh=mesh, in_specs=in_specs, out_specs=out_specs, check_vma=False
    )
```

```python
import functools
import math

import jax
import jax.numpy as jnp
from jax import lax
from jax.experimental import pallas as pl
from jax.experimental.pallas import tpu as pltpu
from jax.sharding import PartitionSpec as P

VMEM = pl.BlockSpec(memory_space=pltpu.VMEM)
SMEM = pl.BlockSpec(memory_space=pltpu.SMEM)
BF16 = jnp.bfloat16
F32 = jnp.float32


def passed_along(value, axis, steps):
    count = lax.axis_size(axis)
    pairs = [(source, (source + steps) % count) for source in range(count)]
    return lax.ppermute(value, axis, pairs)


def mm(left, right):
    return jnp.dot(left, right, preferred_element_type=F32)


def parts_of(value, divisor):
    quotient = jnp.floor((value + 0.5) * (1.0 / divisor))
    return quotient, value - quotient * divisor


def whole_numbers(shape, axis):
    return lax.broadcasted_iota(jnp.int32, shape, axis).astype(F32)


def chosen(condition):
    return jnp.where(condition, 1.0, 0.0)


def coordinates(index, extent):
    rest, third = parts_of(index, extent[2])
    first, second = parts_of(rest, extent[1])
    return [first, second, third]


def source_columns(extent, e):
    count = math.prod(extent)
    face = count // extent[e]
    inner = count - face if e == 0 else count
    total = 6 * (inner + face)
    column = whole_numbers((1, total), 1)
    beyond = chosen(column >= 6 * inner)
    site, left = parts_of(column - beyond * (6 * inner), 6)
    colour, part = parts_of(left, 2)
    within = coordinates(site, extent)
    if e == 0:
        within[0] = within[0] + 1
    flat = [n for d, n in enumerate(extent) if d != e]
    outer, last = parts_of(site, flat[1])
    edge = [outer, last]
    edge.insert(e, jnp.full_like(site, extent[e]))
    where = [w + beyond * (o - w) for w, o in zip(within, edge)]
    return total, part, where, colour


def rows_kernel(extent, eig_ref, vec_out, *face_outs):
    vec = eig_ref[...].astype(F32).reshape(vec_out.shape)
    vec_out[...] = vec.astype(BF16)
    strides = (6 * extent[1] * extent[2], 6 * extent[2], 6)
    for e, out in enumerate(face_outs):
        begins = [0]
        for d in range(e):
            begins = [at + n * strides[d] for at in begins for n in range(extent[d])]
        runs = [vec[at : at + strides[e]] for at in begins]
        out[...] = (jnp.concatenate(runs, axis=0) if e else runs[0]).astype(BF16)


def pieces_kernel(z_ref, fwd_in, bwd_in, fwd_out, bwd_out, fwd_ref, bwd_ref, sems):
    pairs = ((fwd_in, fwd_ref), (bwd_in, bwd_ref))
    copies = [pltpu.make_async_copy(source, target, sems.at[n]) for n, (source, target) in enumerate(pairs)]
    for copy in copies:
        copy.start()
    rows, cols = fwd_ref.shape[1:]
    piece = fwd_out.shape[1]
    per_spin = rows // 4
    lane = cols // 4
    flat = lax.broadcasted_iota(jnp.int32, (piece, 1), 0) + z_ref[0] * piece
    spin = jnp.zeros_like(flat)
    for t in range(1, 4):
        spin += jnp.where(flat >= t * per_spin, 1, 0)
    source = 4 * (flat - spin * per_spin) + spin
    select = chosen(lax.broadcasted_iota(jnp.int32, (piece, rows), 1) == source).astype(BF16)
    column = lax.broadcasted_iota(jnp.int32, (1, cols), 1)
    spin = jnp.zeros_like(column)
    for t in range(1, 4):
        spin += jnp.where(column >= t * lane, 1, 0)
    source = 4 * (column - spin * lane) + spin
    perm = chosen(lax.broadcasted_iota(jnp.int32, (cols, cols), 0) == source).astype(BF16)
    copies[0].wait()
    for c in range(2):
        picked = mm(select, fwd_ref[c]).astype(BF16)
        fwd_out[c] = mm(picked, perm).astype(BF16)
    copies[1].wait()
    for c in range(2):
        bwd_out[c] = mm(select, bwd_ref[c]).astype(BF16)


def links_kernel(extent, link_ref, *outs):
    count = math.prod(extent)
    rows = 6 * count
    row = whole_numbers((rows, 1), 0)
    row_site, left = parts_of(row, 6)
    row_colour, row_part = parts_of(left, 2)
    row_where = coordinates(row_site, extent)
    link = link_ref[...]
    high = link.astype(BF16)
    rest = link - high.astype(F32)
    mid = rest.astype(BF16)
    low = (rest - mid.astype(F32)).astype(BF16)
    spread = chosen(row_site == whole_numbers((rows, count), 1)).astype(BF16)
    by_row = [mm(spread, part) for part in (high, mid, low)]
    by_row = [jnp.concatenate([part, part], axis=1) for part in by_row]

    def entry_of(entry):
        half = chosen(entry >= 54)
        direction, left = parts_of(entry - 54 * half, 18)
        part, left = parts_of(left, 9)
        into, out_of = parts_of(left, 3)
        return half, direction, part, into, out_of

    half, direction, _, into, _ = entry_of(whole_numbers((1, 108), 1))
    own_part = (half == row_part) & (into == row_colour)
    place_half, _, place_part, _, place_colour = entry_of(whole_numbers((108, 1), 0))
    for e, out in enumerate(outs):
        keep = chosen(own_part & (direction == e))
        picked = jnp.concatenate([part * keep for part in by_row], axis=0).astype(BF16)
        total, part, where, colour = source_columns(extent, e)
        sign = 1.0 - 2.0 * part * (1.0 - place_half)
        match = (place_colour == colour) & (jnp.abs(place_part - part) == place_half)
        placed = mm(picked, jnp.where(match, sign, 0.0).astype(BF16))
        same = None
        for d in range(3):
            hit = row_where[d] + (1.0 if d == e else 0.0) == where[d]
            same = hit if same is None else same & hit
        mask = chosen(same)
        for n in range(3):
            at = slice(n * rows, (n + 1) * rows)
            out[at, :] = (placed[at] * mask).astype(BF16)


def correlate_kernel(scale, vec_ref, face0, face1, face2, mat0, mat1, mat2, out_ref):
    gz_n, gx_n, split, depth, width = out_ref.shape
    each = 6 // split
    own_rows = depth // each
    vec = vec_ref[...]
    rows = vec.shape[0]
    row = lax.broadcasted_iota(jnp.int32, (rows, rows), 0)
    column = lax.broadcasted_iota(jnp.int32, (rows, rows), 1)
    odd = lax.rem(row, 2) == 1
    turn = jnp.where(odd & (column == row - 1), -1.0, chosen((column == row + 1) & ~odd)).astype(BF16)
    sources = [
        jnp.concatenate([vec[face0.shape[0] :], face0[...]], axis=0),
        jnp.concatenate([vec, face1[...]], axis=0),
        jnp.concatenate([vec, face2[...]], axis=0),
    ]
    for e, mat in enumerate((mat0, mat1, mat2)):
        terms = mm(mat[...], sources[e])
        moved = terms[:rows] + terms[rows : 2 * rows] + terms[2 * rows :]
        moved = moved.astype(BF16)
        turned = mm(turn, moved).astype(BF16)
        right = jnp.concatenate([moved, turned], axis=1)
        product = lax.dot_general(
            vec, right, (((0,), (0,)), ((), ())), preferred_element_type=F32
        )
        product = (product * scale).astype(BF16)
        for c in range(2):
            n = 2 * e + c
            half = product[:, c * width : (c + 1) * width]
            to = slice(n % each * own_rows, (n % each + 1) * own_rows)
            for g in range(gx_n):
                for z in range(gz_n):
                    at = (g * gz_n + z) * own_rows
                    out_ref[z, g, n // each, to] = half[at : at + own_rows]


def spin_groups(gz_n):
    keys = [(dy, dc) for dc in range(2) for dy in range(gz_n // 2)]
    if gz_n == 4:
        return [[key] for key in keys]
    return [[(dy, dc) for dc in range(2)] for dy in range(gz_n // 2)]


def rows_of(parts, c, count):
    rows = jnp.concatenate([part[:, c] for part in parts], axis=1)
    return rows.reshape(count, rows.shape[-1])


def right_kernel(gz_n, keys, left_ref, *refs):
    bwd_at = dict(zip(keys, refs))
    out_ref, b_ref = refs[len(keys) :]
    num_vecs = b_ref.shape[0] // 8
    op_count, _, row_count, width = out_ref.shape
    for t, group in enumerate(spin_groups(gz_n)):
        real, imag = [rows_of([bwd_at[key] for key in group], c, num_vecs) for c in range(2)]
        at = 2 * t * num_vecs
        b_ref[at : at + num_vecs, :width] = real
        b_ref[at : at + num_vecs, width:] = imag
        b_ref[at + num_vecs : at + 2 * num_vecs, :width] = -imag
        b_ref[at + num_vecs : at + 2 * num_vecs, width:] = real
    left = left_ref[...].reshape(op_count * row_count, 8 * num_vecs)
    block = min(width, 256)
    for c in range(2):
        for begin in range(0, width, block):
            at = c * width + begin
            result = mm(left, b_ref[:, at : at + block]).astype(BF16)
            out_ref[:, c, :, begin : begin + block] = result.reshape(op_count, row_count, block)


def left_kernel(inverse, plan, me_ref, dirs_ref, spin_ref, chain_ref, *refs):
    line, elem_keys, fwd_keys = plan
    elem_in, refs = refs[:2], refs[2:]
    fwd_in, refs = refs[: len(fwd_keys)], refs[len(fwd_keys) :]
    out_ref, elem_all, elem_ref, x_ref, p_ref = refs
    gx_n, gz_n, split, depth, num_vecs = elem_all.shape
    each = 6 // split
    own_rows = depth // each
    width = fwd_in[0].shape[3]
    op_count, row_count, _ = out_ref.shape
    vec_rows = row_count // 4
    gy_n = 4 * num_vecs // width
    lane = width // 4
    halves = gz_n // 4
    gx, gy, gz = me_ref[0], me_ref[1], me_ref[2]

    def back(at, step, count):
        return lax.rem(at - step + count, count)

    def gz_from(dy, dc):
        return back(lax.div(gz, 2), dy, gz_n // 2) * 2 + back(lax.rem(gz, 2), dc, 2)

    for dc, ref in enumerate(elem_in):
        for n, (dx, dy) in enumerate(elem_keys):
            for place, offset in enumerate(line):
                to = lax.bitwise_xor(gx, offset), gz_from(dy, dc), back(gy, dx, gy_n) if split > 1 else 0
                elem_all[to] = ref[n, place]
    column = lax.broadcasted_iota(jnp.int32, (1, num_vecs), 1)
    source = jnp.zeros_like(column)
    half_rows = vec_rows // halves
    for place, offset in enumerate(line):
        for half in range(halves):
            at = place * vec_rows + half * half_rows
            from_half = lax.bitwise_xor(lax.rem(gz, 2), half) if halves == 2 else half
            begin = lax.bitwise_xor(gx, offset) * vec_rows + from_half * half_rows
            inside = (column >= at) & (column < at + half_rows)
            source = jnp.where(inside, column + (begin - at), source)
    perm = chosen(lax.broadcasted_iota(jnp.int32, (num_vecs, num_vecs), 0) == source).astype(BF16)
    for n in range(6):
        rows = slice(n % each * own_rows, (n % each + 1) * own_rows)
        whole = elem_all[:, :, n // each, rows].reshape(num_vecs, num_vecs)
        elem_ref[n] = mm(whole, perm).astype(BF16)

    groups = spin_groups(gz_n)
    spins = [lax.div(gz_from(*group[0]), halves) for group in groups]

    first_row = pl.multiple_of(gx * vec_rows, vec_rows)

    def own(d, c):
        return elem_ref[2 * d + c, pl.ds(first_row, vec_rows), :]

    real_rows = [jnp.concatenate([own(d, 0), -own(d, 1)], axis=1) for d in range(3)]
    imag_rows = [jnp.concatenate([own(d, 1), own(d, 0)], axis=1) for d in range(3)]
    left = jnp.concatenate([part for d in range(3) for part in (real_rows[d], imag_rows[d])], axis=0)
    fwd_at = dict(zip(fwd_keys, fwd_in))
    for t, group in enumerate(groups):
        for dx in range(gy_n):
            parts = [fwd_at[(dx,) + key] for key in group]
            right = jnp.concatenate([rows_of(parts, c, num_vecs) for c in range(2)], axis=0)
            result = mm(left, right).astype(BF16)
            for d in range(3):
                for c in range(2):
                    at = (d * 2 + c) * vec_rows
                    x_ref[d, c, dx, t] = result[at : at + vec_rows]

    row = lax.broadcasted_iota(jnp.int32, (row_count, 1), 0)
    column = lax.broadcasted_iota(jnp.int32, (1, row_count), 1)
    row_spin = lax.rem(row, 4)
    diagonal = lax.div(row, 4) == lax.rem(column, vec_rows)
    column_spin = lax.div(column, vec_rows)
    blocks = [pl.multiple_of(back(gy, dx, gy_n) * lane, lane) for dx in range(gy_n)]

    def one_operator(op):
        a = chain_ref[2 * op]
        b = chain_ref[2 * op + 1]
        dir_a = dirs_ref[a]
        dir_b = dirs_ref[b]
        mix = None
        for t in range(4):
            weight = jnp.full((row_count, 1), spin_ref[a, 0, spins[t]])
            for s in range(1, 4):
                weight = jnp.where(row_spin == s, spin_ref[a, s, spins[t]], weight)
            mix = weight if mix is None else jnp.where(column_spin == t, weight, mix)
        mix = jnp.where(diagonal, mix, 0.0)
        high = mix.astype(BF16)
        low = (mix - high.astype(F32)).astype(BF16)
        mix = jnp.concatenate([high, low], axis=0)
        for c in range(2):
            for dx in range(gy_n):
                source = x_ref[dir_a, c, dx].reshape(row_count, width)
                both = mm(mix, source)
                result = (both[:row_count] + both[row_count:]).astype(BF16)
                for s in range(4):
                    to = c * num_vecs + dx * lane
                    p_ref[s, :, to : to + lane] = result[:, s * lane : (s + 1) * lane]

        def elem(c):
            return jnp.concatenate([elem_ref[2 * dir_b + c, pl.ds(at, lane), :] for at in blocks], axis=0)

        real_b, imag_b = elem(0), elem(1)
        right = jnp.concatenate(
            [
                jnp.concatenate([real_b, imag_b], axis=1),
                jnp.concatenate([-imag_b, real_b], axis=1),
            ],
            axis=0,
        )
        product = mm(p_ref[...].reshape(4 * row_count, 2 * num_vecs), right)
        parts = [product[s * row_count : (s + 1) * row_count] for s in range(4)]
        for t in range(4):
            total = parts[0] * (spin_ref[b, 0, spins[t]] * inverse)
            for s in range(1, 4):
                total += parts[s] * (spin_ref[b, s, spins[t]] * inverse)
            total = total.astype(BF16)
            out_ref[op, :, 2 * t * num_vecs : 2 * (t + 1) * num_vecs] = total

    for op in range(op_count):
        one_operator(op)


def passed_in_gz(value, dy, dc):
    count = lax.axis_size("gz")
    chips = count // 2
    pairs = [(n, ((n // 2 + dy) % chips) * 2 + (n + dc) % 2) for n in range(count)]
    return lax.ppermute(value, "gz", pairs)


def passed_in_plane(value, dx, dy):
    if not dx and not dy:
        return value
    gy_n, gz_n = lax.axis_size("gy"), lax.axis_size("gz")
    chips = gz_n // 2
    pairs = []
    for y in range(gy_n):
        for z in range(gz_n):
            to = (y + dx) % gy_n * gz_n + ((z // 2 + dy) % chips) * 2 + z % 2
            pairs.append((y * gz_n + z, to))
    return lax.ppermute(value, ("gy", "gz"), pairs)


def xor_passed(value, axis, offset):
    if not offset:
        return value
    return lax.ppermute(value, axis, [(n, n ^ offset) for n in range(lax.axis_size(axis))])


def line_exchange(value, axis, distance, steps, offsets=(0,)):
    gathered = value if len(offsets) > 1 else value[None]
    offsets = list(offsets)
    for _ in range(steps):
        gathered = jnp.concatenate([gathered, xor_passed(gathered, axis, distance)])
        offsets += [offset ^ distance for offset in offsets]
        distance //= 2
    return gathered, tuple(offsets)


def part_at(value, index, axis=0):
    return lax.dynamic_index_in_dim(value, index, axis, keepdims=False)


def added(*values):
    return sum(value.astype(F32) for value in values).astype(BF16)


def on_device(eigvecs, links, directions, spin_mats, forward_peram, backward_peram, chain_order):
    extent = eigvecs.shape[:3]
    num_vecs = eigvecs.shape[-1]
    gx_n, gy_n, gz_n = (lax.axis_size(name) for name in ("gx", "gy", "gz"))
    chips = gz_n // 2
    gx, gy, gz = (lax.axis_index(name).astype(jnp.int32) for name in ("gx", "gy", "gz"))
    me = jnp.stack([gx, gy, gz])
    chip, core = lax.div(gz, 2), lax.rem(gz, 2)

    rows, cols = forward_peram.shape[1:]
    piece = rows // gz_n
    site_rows = 6 * math.prod(extent)
    face_rows = [site_rows // n for n in extent]
    vec, *faces = pl.pallas_call(
        functools.partial(rows_kernel, extent),
        out_shape=[jax.ShapeDtypeStruct((n, num_vecs), BF16) for n in [site_rows] + face_rows],
        in_specs=[VMEM],
        out_specs=[VMEM] * 4,
        compiler_params=pltpu.CompilerParams(vmem_limit_bytes=24 * 2**20),
        name="rows",
    )(eigvecs.transpose(0, 1, 2, 4, 3, 5).reshape(-1, 2, num_vecs))
    faces = [passed_along(face, axis, -1) for face, axis in zip(faces, ("gx", "gy", "gz"))]

    piece_shape = jax.ShapeDtypeStruct((2, piece, cols), BF16)
    fwd_piece, bwd_piece = pl.pallas_call(
        pieces_kernel,
        out_shape=[piece_shape] * 2,
        in_specs=[SMEM] + [pl.BlockSpec(memory_space=pl.ANY)] * 2,
        out_specs=[VMEM] * 2,
        scratch_shapes=[
            pltpu.VMEM(forward_peram.shape, BF16),
            pltpu.VMEM(backward_peram.shape, BF16),
            pltpu.SemaphoreType.DMA((2,)),
        ],
        compiler_params=pltpu.CompilerParams(vmem_limit_bytes=60 * 2**20),
        cost_estimate=pl.CostEstimate(flops=10**8, bytes_accessed=10**7, transcendentals=0),
        name="pieces",
    )(me[2:], forward_peram, backward_peram)
    fwd_piece, links = lax.optimization_barrier((fwd_piece, links))
    fwd_half = xor_passed(fwd_piece, "gx", gx_n // 2)

    link_mats = pl.pallas_call(
        functools.partial(links_kernel, extent),
        out_shape=[
            jax.ShapeDtypeStruct((3 * site_rows, site_rows - (0 if e else face_rows[0]) + face_rows[e]), BF16)
            for e in range(3)
        ],
        in_specs=[VMEM],
        out_specs=[VMEM] * 3,
        compiler_params=pltpu.CompilerParams(vmem_limit_bytes=24 * 2**20),
        name="link_matrices",
    )(links.reshape(-1, 54))

    volume = math.prod(extent) * gx_n * gy_n * gz_n
    own_rows = num_vecs // (gz_n * gx_n)
    split = gy_n if 6 % gy_n == 0 and own_rows % 16 == 0 else 1
    depth = 6 * own_rows // split
    partial = pl.pallas_call(
        functools.partial(correlate_kernel, 1.0 / math.sqrt(12.0 * volume)),
        out_shape=jax.ShapeDtypeStruct((gz_n, gx_n, split, depth, num_vecs), BF16),
        in_specs=[VMEM] * 7,
        out_specs=VMEM,
        compiler_params=pltpu.CompilerParams(vmem_limit_bytes=24 * 2**20),
        name="correlate",
    )(vec, *faces, *link_mats)

    rounds = gx_n.bit_length() - 1
    partial, fwd_half = lax.optimization_barrier((partial, fwd_half))
    by_core = partial.reshape((chips, 2) + partial.shape[1:])
    summed = added(part_at(by_core, core, 1), passed_in_gz(part_at(by_core, 1 - core, 1), 0, 1))
    fwd_line, line = line_exchange(jnp.stack([fwd_piece, fwd_half]), "gx", gx_n // 4, rounds - 1, (0, gx_n // 2))
    plane = [(dx, dy) for dy in range(chips) for dx in range(gy_n)]

    def plane_part(dx, dy):
        part = part_at(summed, lax.rem(chip + dy, chips))
        return part_at(part, lax.rem(gy + dx, gy_n) if split > 1 else 0, 1)

    summed = added(*[passed_in_plane(plane_part(dx, dy), dx, dy) for dx, dy in plane])
    if split == 1:
        summed = added(summed, *[passed_along(summed, "gy", dx) for dx in range(1, gy_n)])
    summed, fwd_line = lax.optimization_barrier((summed, fwd_line))

    four = gy_n == 2 and chips == 2
    fwd_parts = {(dx, dy, 0): passed_in_plane(fwd_line, dx, dy) for dx, dy in plane if not (four and dx and dy)}
    others = [lax.bitwise_xor(gx, offset) for offset in line]
    summed = added(*[xor_passed(part_at(summed, to), "gx", offset) for to, offset in zip(others, line)])
    elem_line = jnp.stack([xor_passed(summed, "gx", offset) for offset in line])
    keys = [key for key in fwd_parts if key != (0, 0, 0)]
    pairs = chain_order.reshape(-1)
    elem_line, bwd_piece, pairs, *parts = lax.optimization_barrier(
        (elem_line, bwd_piece, pairs, *[fwd_parts[key] for key in keys])
    )
    fwd_parts.update(zip(keys, parts))
    elem_keys = plane if split > 1 else [(0, dy) for dy in range(chips)]
    elem_own = jnp.stack([passed_in_plane(elem_line, dx, dy) for dx, dy in elem_keys])
    bwd_half = xor_passed(bwd_piece, "gx", gx_n // 2)
    if four:
        tied = (elem_own, bwd_half, fwd_parts[1, 0, 0], fwd_parts[0, 1, 0])
        elem_own, bwd_half, over_x, over_y = lax.optimization_barrier(tied)
        fwd_parts[1, 0, 0], fwd_parts[0, 1, 0] = over_x, over_y
        corner = [passed_in_plane(over_y[:, :1], 1, 0), passed_in_plane(over_x[:, 1:], 0, 1)]
        fwd_parts[1, 1, 0] = jnp.concatenate(corner, axis=1)
    elem_parts = [elem_own, passed_in_gz(elem_own, 0, 1)]
    for dx, dy in plane:
        fwd_parts[dx, dy, 1] = passed_in_gz(fwd_parts[dx, dy, 0], 0, 1)
    bwd_line, _ = line_exchange(jnp.stack([bwd_piece, bwd_half]), "gx", gx_n // 4, rounds - 1, (0, gx_n // 2))
    bwd_parts = {(dy, 0): passed_in_gz(bwd_line, dy, 0) if dy else bwd_line for dy in range(chips)}

    op_count = chain_order.shape[0]
    plan = (line, tuple(elem_keys), tuple(fwd_parts))
    left_shape = (op_count, rows, 8 * num_vecs)
    left = pl.pallas_call(
        functools.partial(left_kernel, 1.0 / math.sqrt(4 * num_vecs), plan),
        out_shape=jax.ShapeDtypeStruct(left_shape, BF16),
        in_specs=[SMEM] * 4 + [VMEM] * (len(elem_parts) + len(fwd_parts)),
        out_specs=VMEM,
        scratch_shapes=[
            pltpu.VMEM((gx_n, gz_n, split, depth, num_vecs), BF16),
            pltpu.VMEM((6, num_vecs, num_vecs), BF16),
            pltpu.VMEM((3, 2, gy_n, 4, rows // 4, cols), BF16),
            pltpu.VMEM((4, rows, 2 * num_vecs), BF16),
        ],
        compiler_params=pltpu.CompilerParams(vmem_limit_bytes=24 * 2**20),
        cost_estimate=pl.CostEstimate(flops=8 * 10**9, bytes_accessed=10**7, transcendentals=0),
        name="left",
    )(me, directions, spin_mats, pairs, *elem_parts, *fwd_parts.values())
    late = [key for key in bwd_parts if key[0]]
    left, *parts = lax.optimization_barrier((left, *[bwd_parts[key] for key in late]))
    bwd_parts.update(zip(late, parts))
    for dy in range(chips):
        bwd_parts[dy, 1] = passed_in_gz(bwd_parts[dy, 0], 0, 1)
    return pl.pallas_call(
        functools.partial(right_kernel, gz_n, tuple(bwd_parts)),
        out_shape=jax.ShapeDtypeStruct((op_count, 2, rows, cols), BF16),
        in_specs=[VMEM] * (1 + len(bwd_parts)),
        out_specs=VMEM,
        scratch_shapes=[pltpu.VMEM((8 * num_vecs, 2 * cols), BF16)],
        compiler_params=pltpu.CompilerParams(vmem_limit_bytes=24 * 2**20),
        name="right",
    )(left, *bwd_parts.values())


def solution(mesh):
    in_specs = (
        P("gx", "gy", "gz", None, None, None),
        P("gx", "gy", "gz", None, None, None, None),
        P(),
        P(),
        P(None, "gx", "gy"),
        P(None, "gx", "gy"),
        P("gz", None),
    )
    out_specs = P("gz", None, "gx", "gy")
    return jax.shard_map(
        on_device, mesh=mesh, in_specs=in_specs, out_specs=out_specs, check_vma=False
    )
```

```python
import functools
import math

import jax
import jax.numpy as jnp
from jax import lax
from jax.experimental import pallas as pl
from jax.experimental.pallas import tpu as pltpu
from jax.sharding import PartitionSpec as P

VMEM = pl.BlockSpec(memory_space=pltpu.VMEM)
SMEM = pl.BlockSpec(memory_space=pltpu.SMEM)
BF16 = jnp.bfloat16
F32 = jnp.float32


def passed_along(value, axis, steps):
    count = lax.axis_size(axis)
    pairs = [(source, (source + steps) % count) for source in range(count)]
    return lax.ppermute(value, axis, pairs)


def mm(left, right):
    return jnp.dot(left, right, preferred_element_type=F32)


def parts_of(value, divisor):
    quotient = jnp.floor((value + 0.5) * (1.0 / divisor))
    return quotient, value - quotient * divisor


def whole_numbers(shape, axis):
    return lax.broadcasted_iota(jnp.int32, shape, axis).astype(F32)


def chosen(condition):
    return jnp.where(condition, 1.0, 0.0)


def coordinates(index, extent):
    rest, third = parts_of(index, extent[2])
    first, second = parts_of(rest, extent[1])
    return [first, second, third]


def source_columns(extent, e):
    count = math.prod(extent)
    face = count // extent[e]
    inner = count - face if e == 0 else count
    total = 6 * (inner + face)
    column = whole_numbers((1, total), 1)
    beyond = chosen(column >= 6 * inner)
    site, left = parts_of(column - beyond * (6 * inner), 6)
    colour, part = parts_of(left, 2)
    within = coordinates(site, extent)
    if e == 0:
        within[0] = within[0] + 1
    flat = [n for d, n in enumerate(extent) if d != e]
    outer, last = parts_of(site, flat[1])
    edge = [outer, last]
    edge.insert(e, jnp.full_like(site, extent[e]))
    where = [w + beyond * (o - w) for w, o in zip(within, edge)]
    return total, part, where, colour


def rows_kernel(extent, eig_ref, vec_out, *face_outs):
    vec = eig_ref[...].astype(F32).reshape(vec_out.shape)
    vec_out[...] = vec.astype(BF16)
    strides = (6 * extent[1] * extent[2], 6 * extent[2], 6)
    for e, out in enumerate(face_outs):
        begins = [0]
        for d in range(e):
            begins = [at + n * strides[d] for at in begins for n in range(extent[d])]
        runs = [vec[at : at + strides[e]] for at in begins]
        out[...] = (jnp.concatenate(runs, axis=0) if e else runs[0]).astype(BF16)


def pieces_kernel(z_ref, fwd_in, bwd_in, fwd_out, bwd_out, fwd_ref, bwd_ref, sems):
    pairs = ((fwd_in, fwd_ref), (bwd_in, bwd_ref))
    copies = [pltpu.make_async_copy(source, target, sems.at[n]) for n, (source, target) in enumerate(pairs)]
    for copy in copies:
        copy.start()
    rows, cols = fwd_ref.shape[1:]
    piece = fwd_out.shape[1]
    per_spin = rows // 4
    lane = cols // 4
    flat = lax.broadcasted_iota(jnp.int32, (piece, 1), 0) + z_ref[0] * piece
    spin = jnp.zeros_like(flat)
    for t in range(1, 4):
        spin += jnp.where(flat >= t * per_spin, 1, 0)
    source = 4 * (flat - spin * per_spin) + spin
    select = chosen(lax.broadcasted_iota(jnp.int32, (piece, rows), 1) == source).astype(BF16)
    column = lax.broadcasted_iota(jnp.int32, (1, cols), 1)
    spin = jnp.zeros_like(column)
    for t in range(1, 4):
        spin += jnp.where(column >= t * lane, 1, 0)
    source = 4 * (column - spin * lane) + spin
    perm = chosen(lax.broadcasted_iota(jnp.int32, (cols, cols), 0) == source).astype(BF16)
    copies[0].wait()
    for c in range(2):
        picked = mm(select, fwd_ref[c]).astype(BF16)
        fwd_out[c] = mm(picked, perm).astype(BF16)
    copies[1].wait()
    for c in range(2):
        bwd_out[c] = mm(select, bwd_ref[c]).astype(BF16)


def links_kernel(extent, link_ref, *outs):
    count = math.prod(extent)
    rows = 6 * count
    row = whole_numbers((rows, 1), 0)
    row_site, left = parts_of(row, 6)
    row_colour, row_part = parts_of(left, 2)
    row_where = coordinates(row_site, extent)
    link = link_ref[...]
    high = link.astype(BF16)
    rest = link - high.astype(F32)
    mid = rest.astype(BF16)
    low = (rest - mid.astype(F32)).astype(BF16)
    spread = chosen(row_site == whole_numbers((rows, count), 1)).astype(BF16)
    by_row = [mm(spread, part) for part in (high, mid, low)]
    by_row = [jnp.concatenate([part, part], axis=1) for part in by_row]

    def entry_of(entry):
        half = chosen(entry >= 54)
        direction, left = parts_of(entry - 54 * half, 18)
        part, left = parts_of(left, 9)
        into, out_of = parts_of(left, 3)
        return half, direction, part, into, out_of

    half, direction, _, into, _ = entry_of(whole_numbers((1, 108), 1))
    own_part = (half == row_part) & (into == row_colour)
    place_half, _, place_part, _, place_colour = entry_of(whole_numbers((108, 1), 0))
    for e, out in enumerate(outs):
        keep = chosen(own_part & (direction == e))
        picked = jnp.concatenate([part * keep for part in by_row], axis=0).astype(BF16)
        total, part, where, colour = source_columns(extent, e)
        sign = 1.0 - 2.0 * part * (1.0 - place_half)
        match = (place_colour == colour) & (jnp.abs(place_part - part) == place_half)
        placed = mm(picked, jnp.where(match, sign, 0.0).astype(BF16))
        same = None
        for d in range(3):
            hit = row_where[d] + (1.0 if d == e else 0.0) == where[d]
            same = hit if same is None else same & hit
        mask = chosen(same)
        for n in range(3):
            at = slice(n * rows, (n + 1) * rows)
            out[at, :] = (placed[at] * mask).astype(BF16)


def correlate_kernel(scale, vec_ref, face0, face1, face2, mat0, mat1, mat2, out_ref):
    gz_n, gx_n, split, depth, width = out_ref.shape
    each = 6 // split
    own_rows = depth // each
    vec = vec_ref[...]
    rows = vec.shape[0]
    row = lax.broadcasted_iota(jnp.int32, (rows, rows), 0)
    column = lax.broadcasted_iota(jnp.int32, (rows, rows), 1)
    odd = lax.rem(row, 2) == 1
    turn = jnp.where(odd & (column == row - 1), -1.0, chosen((column == row + 1) & ~odd)).astype(BF16)
    sources = [
        jnp.concatenate([vec[face0.shape[0] :], face0[...]], axis=0),
        jnp.concatenate([vec, face1[...]], axis=0),
        jnp.concatenate([vec, face2[...]], axis=0),
    ]
    for e, mat in enumerate((mat0, mat1, mat2)):
        terms = mm(mat[...], sources[e])
        moved = terms[:rows] + terms[rows : 2 * rows] + terms[2 * rows :]
        moved = moved.astype(BF16)
        turned = mm(turn, moved).astype(BF16)
        right = jnp.concatenate([moved, turned], axis=1)
        product = lax.dot_general(
            vec, right, (((0,), (0,)), ((), ())), preferred_element_type=F32
        )
        product = (product * scale).astype(BF16)
        for c in range(2):
            n = 2 * e + c
            half = product[:, c * width : (c + 1) * width]
            to = slice(n % each * own_rows, (n % each + 1) * own_rows)
            for g in range(gx_n):
                for z in range(gz_n):
                    at = (g * gz_n + z) * own_rows
                    out_ref[z, g, n // each, to] = half[at : at + own_rows]


def spin_groups(gz_n):
    keys = [(dy, dc) for dc in range(2) for dy in range(gz_n // 2)]
    if gz_n == 4:
        return [[key] for key in keys]
    return [[(dy, dc) for dc in range(2)] for dy in range(gz_n // 2)]


def rows_of(parts, c, count):
    rows = jnp.concatenate([part[:, c] for part in parts], axis=1)
    return rows.reshape(count, rows.shape[-1])


def right_kernel(gz_n, keys, left_ref, *refs):
    bwd_at = dict(zip(keys, refs))
    out_ref, b_ref = refs[len(keys) :]
    num_vecs = b_ref.shape[0] // 8
    op_count, _, row_count, width = out_ref.shape
    for t, group in enumerate(spin_groups(gz_n)):
        real, imag = [rows_of([bwd_at[key] for key in group], c, num_vecs) for c in range(2)]
        at = 2 * t * num_vecs
        b_ref[at : at + num_vecs, :width] = real
        b_ref[at : at + num_vecs, width:] = imag
        b_ref[at + num_vecs : at + 2 * num_vecs, :width] = -imag
        b_ref[at + num_vecs : at + 2 * num_vecs, width:] = real
    left = left_ref[...].reshape(op_count * row_count, 8 * num_vecs)
    block = min(width, 256)
    for c in range(2):
        for begin in range(0, width, block):
            at = c * width + begin
            result = mm(left, b_ref[:, at : at + block]).astype(BF16)
            out_ref[:, c, :, begin : begin + block] = result.reshape(op_count, row_count, block)


def left_kernel(inverse, plan, me_ref, dirs_ref, spin_ref, chain_ref, *refs):
    line, elem_keys, fwd_keys = plan
    elem_in, refs = refs[:2], refs[2:]
    fwd_in, refs = refs[: len(fwd_keys)], refs[len(fwd_keys) :]
    out_ref, elem_all, elem_ref, x_ref, p_ref = refs
    gx_n, gz_n, split, depth, num_vecs = elem_all.shape
    each = 6 // split
    own_rows = depth // each
    width = fwd_in[0].shape[3]
    op_count, row_count, _ = out_ref.shape
    vec_rows = row_count // 4
    gy_n = 4 * num_vecs // width
    lane = width // 4
    halves = gz_n // 4
    gx, gy, gz = me_ref[0], me_ref[1], me_ref[2]

    def back(at, step, count):
        return lax.rem(at - step + count, count)

    def gz_from(dy, dc):
        return back(lax.div(gz, 2), dy, gz_n // 2) * 2 + back(lax.rem(gz, 2), dc, 2)

    for dc, ref in enumerate(elem_in):
        for n, (dx, dy) in enumerate(elem_keys):
            for place, offset in enumerate(line):
                to = lax.bitwise_xor(gx, offset), gz_from(dy, dc), back(gy, dx, gy_n) if split > 1 else 0
                elem_all[to] = ref[n, place]
    column = lax.broadcasted_iota(jnp.int32, (1, num_vecs), 1)
    source = jnp.zeros_like(column)
    half_rows = vec_rows // halves
    for place, offset in enumerate(line):
        for half in range(halves):
            at = place * vec_rows + half * half_rows
            from_half = lax.bitwise_xor(lax.rem(gz, 2), half) if halves == 2 else half
            begin = lax.bitwise_xor(gx, offset) * vec_rows + from_half * half_rows
            inside = (column >= at) & (column < at + half_rows)
            source = jnp.where(inside, column + (begin - at), source)
    perm = chosen(lax.broadcasted_iota(jnp.int32, (num_vecs, num_vecs), 0) == source).astype(BF16)
    for n in range(6):
        rows = slice(n % each * own_rows, (n % each + 1) * own_rows)
        whole = elem_all[:, :, n // each, rows].reshape(num_vecs, num_vecs)
        elem_ref[n] = mm(whole, perm).astype(BF16)

    groups = spin_groups(gz_n)
    spins = [lax.div(gz_from(*group[0]), halves) for group in groups]

    first_row = pl.multiple_of(gx * vec_rows, vec_rows)

    def own(d, c):
        return elem_ref[2 * d + c, pl.ds(first_row, vec_rows), :]

    real_rows = [jnp.concatenate([own(d, 0), -own(d, 1)], axis=1) for d in range(3)]
    imag_rows = [jnp.concatenate([own(d, 1), own(d, 0)], axis=1) for d in range(3)]
    left = jnp.concatenate([part for d in range(3) for part in (real_rows[d], imag_rows[d])], axis=0)
    fwd_at = dict(zip(fwd_keys, fwd_in))
    for t, group in enumerate(groups):
        for dx in range(gy_n):
            parts = [fwd_at[(dx,) + key] for key in group]
            right = jnp.concatenate([rows_of(parts, c, num_vecs) for c in range(2)], axis=0)
            result = mm(left, right).astype(BF16)
            for d in range(3):
                for c in range(2):
                    at = (d * 2 + c) * vec_rows
                    x_ref[d, c, dx, t] = result[at : at + vec_rows]

    row = lax.broadcasted_iota(jnp.int32, (row_count, 1), 0)
    column = lax.broadcasted_iota(jnp.int32, (1, row_count), 1)
    row_spin = lax.rem(row, 4)
    diagonal = lax.div(row, 4) == lax.rem(column, vec_rows)
    column_spin = lax.div(column, vec_rows)
    blocks = [pl.multiple_of(back(gy, dx, gy_n) * lane, lane) for dx in range(gy_n)]

    def one_operator(op):
        a = chain_ref[2 * op]
        b = chain_ref[2 * op + 1]
        dir_a = dirs_ref[a]
        dir_b = dirs_ref[b]
        mix = None
        for t in range(4):
            weight = jnp.full((row_count, 1), spin_ref[a, 0, spins[t]])
            for s in range(1, 4):
                weight = jnp.where(row_spin == s, spin_ref[a, s, spins[t]], weight)
            mix = weight if mix is None else jnp.where(column_spin == t, weight, mix)
        mix = jnp.where(diagonal, mix, 0.0)
        high = mix.astype(BF16)
        low = (mix - high.astype(F32)).astype(BF16)
        mix = jnp.concatenate([high, low], axis=0)
        for c in range(2):
            for dx in range(gy_n):
                source = x_ref[dir_a, c, dx].reshape(row_count, width)
                both = mm(mix, source)
                result = (both[:row_count] + both[row_count:]).astype(BF16)
                for s in range(4):
                    to = c * num_vecs + dx * lane
                    p_ref[s, :, to : to + lane] = result[:, s * lane : (s + 1) * lane]

        def elem(c):
            return jnp.concatenate([elem_ref[2 * dir_b + c, pl.ds(at, lane), :] for at in blocks], axis=0)

        real_b, imag_b = elem(0), elem(1)
        right = jnp.concatenate(
            [
                jnp.concatenate([real_b, imag_b], axis=1),
                jnp.concatenate([-imag_b, real_b], axis=1),
            ],
            axis=0,
        )
        product = mm(p_ref[...].reshape(4 * row_count, 2 * num_vecs), right)
        parts = [product[s * row_count : (s + 1) * row_count] for s in range(4)]
        for t in range(4):
            total = parts[0] * (spin_ref[b, 0, spins[t]] * inverse)
            for s in range(1, 4):
                total += parts[s] * (spin_ref[b, s, spins[t]] * inverse)
            total = total.astype(BF16)
            out_ref[op, :, 2 * t * num_vecs : 2 * (t + 1) * num_vecs] = total

    for op in range(op_count):
        one_operator(op)


def passed_in_gz(value, dy, dc):
    count = lax.axis_size("gz")
    chips = count // 2
    pairs = [(n, ((n // 2 + dy) % chips) * 2 + (n + dc) % 2) for n in range(count)]
    return lax.ppermute(value, "gz", pairs)


def passed_in_plane(value, dx, dy):
    if not dx and not dy:
        return value
    gy_n, gz_n = lax.axis_size("gy"), lax.axis_size("gz")
    chips = gz_n // 2
    pairs = []
    for y in range(gy_n):
        for z in range(gz_n):
            to = (y + dx) % gy_n * gz_n + ((z // 2 + dy) % chips) * 2 + z % 2
            pairs.append((y * gz_n + z, to))
    return lax.ppermute(value, ("gy", "gz"), pairs)


def line_exchange(value, axis, distance, steps, offsets=(0,)):
    count = lax.axis_size(axis)
    gathered = value if len(offsets) > 1 else value[None]
    offsets = list(offsets)
    for _ in range(steps):
        pairs = [(n, n ^ distance) for n in range(count)]
        gathered = jnp.concatenate([gathered, lax.ppermute(gathered, axis, pairs)])
        offsets += [offset ^ distance for offset in offsets]
        distance //= 2
    return gathered, tuple(offsets)


def part_at(value, index, axis=0):
    return lax.dynamic_index_in_dim(value, index, axis, keepdims=False)


def added(*values):
    return sum(value.astype(F32) for value in values).astype(BF16)


def on_device(eigvecs, links, directions, spin_mats, forward_peram, backward_peram, chain_order):
    extent = eigvecs.shape[:3]
    num_vecs = eigvecs.shape[-1]
    gx_n, gy_n, gz_n = (lax.axis_size(name) for name in ("gx", "gy", "gz"))
    chips = gz_n // 2
    gx, gy, gz = (lax.axis_index(name).astype(jnp.int32) for name in ("gx", "gy", "gz"))
    me = jnp.stack([gx, gy, gz])
    chip, core = lax.div(gz, 2), lax.rem(gz, 2)

    rows, cols = forward_peram.shape[1:]
    piece = rows // gz_n
    site_rows = 6 * math.prod(extent)
    face_rows = [site_rows // n for n in extent]
    vec, *faces = pl.pallas_call(
        functools.partial(rows_kernel, extent),
        out_shape=[jax.ShapeDtypeStruct((n, num_vecs), BF16) for n in [site_rows] + face_rows],
        in_specs=[VMEM],
        out_specs=[VMEM] * 4,
        compiler_params=pltpu.CompilerParams(vmem_limit_bytes=24 * 2**20),
        name="rows",
    )(eigvecs.transpose(0, 1, 2, 4, 3, 5).reshape(-1, 2, num_vecs))
    faces = [passed_along(face, axis, -1) for face, axis in zip(faces, ("gx", "gy", "gz"))]

    piece_shape = jax.ShapeDtypeStruct((2, piece, cols), BF16)
    fwd_piece, bwd_piece = pl.pallas_call(
        pieces_kernel,
        out_shape=[piece_shape] * 2,
        in_specs=[SMEM] + [pl.BlockSpec(memory_space=pl.ANY)] * 2,
        out_specs=[VMEM] * 2,
        scratch_shapes=[
            pltpu.VMEM(forward_peram.shape, BF16),
            pltpu.VMEM(backward_peram.shape, BF16),
            pltpu.SemaphoreType.DMA((2,)),
        ],
        compiler_params=pltpu.CompilerParams(vmem_limit_bytes=60 * 2**20),
        cost_estimate=pl.CostEstimate(flops=10**8, bytes_accessed=10**7, transcendentals=0),
        name="pieces",
    )(me[2:], forward_peram, backward_peram)
    fwd_piece, links = lax.optimization_barrier((fwd_piece, links))
    fwd_half = lax.ppermute(fwd_piece, "gx", [(n, n ^ (gx_n // 2)) for n in range(gx_n)])

    link_mats = pl.pallas_call(
        functools.partial(links_kernel, extent),
        out_shape=[
            jax.ShapeDtypeStruct((3 * site_rows, site_rows - (0 if e else face_rows[0]) + face_rows[e]), BF16)
            for e in range(3)
        ],
        in_specs=[VMEM],
        out_specs=[VMEM] * 3,
        compiler_params=pltpu.CompilerParams(vmem_limit_bytes=24 * 2**20),
        name="link_matrices",
    )(links.reshape(-1, 54))

    volume = math.prod(extent) * gx_n * gy_n * gz_n
    own_rows = num_vecs // (gz_n * gx_n)
    split = gy_n if 6 % gy_n == 0 and own_rows % 16 == 0 else 1
    depth = 6 * own_rows // split
    partial = pl.pallas_call(
        functools.partial(correlate_kernel, 1.0 / math.sqrt(12.0 * volume)),
        out_shape=jax.ShapeDtypeStruct((gz_n, gx_n, split, depth, num_vecs), BF16),
        in_specs=[VMEM] * 7,
        out_specs=VMEM,
        compiler_params=pltpu.CompilerParams(vmem_limit_bytes=24 * 2**20),
        name="correlate",
    )(vec, *faces, *link_mats)

    partial, fwd_half = lax.optimization_barrier((partial, fwd_half))
    by_core = partial.reshape((chips, 2) + partial.shape[1:])
    summed = added(part_at(by_core, core, 1), passed_in_gz(part_at(by_core, 1 - core, 1), 0, 1))
    rounds = gx_n.bit_length() - 1
    fwd_line = jnp.stack([fwd_piece, fwd_half])
    fwd_line, line = line_exchange(fwd_line, "gx", gx_n // 4, rounds - 1, (0, gx_n // 2))
    plane = [(dx, dy) for dy in range(chips) for dx in range(gy_n)]

    def plane_part(dx, dy):
        part = part_at(summed, lax.rem(chip + dy, chips))
        return part_at(part, lax.rem(gy + dx, gy_n) if split > 1 else 0, 1)

    summed = added(*[passed_in_plane(plane_part(dx, dy), dx, dy) for dx, dy in plane])
    summed, fwd_line, bwd_piece = lax.optimization_barrier((summed, fwd_line, bwd_piece))
    bwd_line, _ = line_exchange(bwd_piece, "gx", gx_n // 2, rounds)

    four = gy_n == 2 and chips == 2
    fwd_parts = {(dx, dy, 0): passed_in_plane(fwd_line, dx, dy) for dx, dy in plane if not (four and dx and dy)}

    distance = gx_n // 2
    while distance:
        halves = summed.reshape((2, distance) + summed.shape[1:])
        bit = lax.rem(lax.div(gx, distance), 2)
        pairs = [(n, n ^ distance) for n in range(gx_n)]
        summed = added(part_at(halves, bit), lax.ppermute(part_at(halves, 1 - bit), "gx", pairs))
        distance //= 2
    elem_line, offsets = line_exchange(summed[0], "gx", gx_n // 2, rounds - 1)
    fwd_parts[0, 0, 1] = passed_in_gz(fwd_line, 0, 1)
    order = chain_order.reshape(-1)
    if four:
        keys = [(1, 0, 0), (0, 1, 0), (0, 0, 1)]
        tied = (elem_line, bwd_line, order, *[fwd_parts[key] for key in keys])
        elem_line, bwd_line, order, *parts = lax.optimization_barrier(tied)
        fwd_parts.update(zip(keys, parts))
        fwd_parts[1, 1, 0] = passed_in_plane(fwd_parts[0, 1, 0], 1, 0)
    bwd_parts = {(dy, 0): passed_in_gz(bwd_line, dy, 0) if dy else bwd_line for dy in range(chips)}
    elem_line, _ = line_exchange(elem_line, "gx", 1, 1, offsets)
    elem_keys = plane if split > 1 else [(0, dy) for dy in range(chips)]
    elem_own = jnp.stack([passed_in_plane(elem_line, dx, dy) for dx, dy in elem_keys])
    late = [(1, 1, 0)] if four else []
    elem_own, *parts = lax.optimization_barrier((elem_own, *[fwd_parts[key] for key in late], *bwd_parts.values()))
    fwd_parts.update(zip(late, parts))
    bwd_parts.update(zip(list(bwd_parts), parts[len(late) :]))
    elem_parts = [elem_own, passed_in_gz(elem_own, 0, 1)]
    for dx, dy in plane[1:]:
        fwd_parts[dx, dy, 1] = passed_in_gz(fwd_parts[dx, dy, 0], 0, 1)
    for dy in range(chips):
        bwd_parts[dy, 1] = passed_in_gz(bwd_parts[dy, 0], 0, 1)

    op_count = chain_order.shape[0]
    plan = (line, tuple(elem_keys), tuple(fwd_parts))
    left_shape = (op_count, rows, 8 * num_vecs)
    left = pl.pallas_call(
        functools.partial(left_kernel, 1.0 / math.sqrt(4 * num_vecs), plan),
        out_shape=jax.ShapeDtypeStruct(left_shape, BF16),
        in_specs=[SMEM] * 4 + [VMEM] * (len(elem_parts) + len(fwd_parts)),
        out_specs=VMEM,
        scratch_shapes=[
            pltpu.VMEM((gx_n, gz_n, split, depth, num_vecs), BF16),
            pltpu.VMEM((6, num_vecs, num_vecs), BF16),
            pltpu.VMEM((3, 2, gy_n, 4, rows // 4, cols), BF16),
            pltpu.VMEM((4, rows, 2 * num_vecs), BF16),
        ],
        compiler_params=pltpu.CompilerParams(vmem_limit_bytes=24 * 2**20),
        cost_estimate=pl.CostEstimate(flops=8 * 10**9, bytes_accessed=10**7, transcendentals=0),
        name="left",
    )(me, directions, spin_mats, order, *elem_parts, *fwd_parts.values())
    return pl.pallas_call(
        functools.partial(right_kernel, gz_n, tuple(bwd_parts)),
        out_shape=jax.ShapeDtypeStruct((op_count, 2, rows, cols), BF16),
        in_specs=[VMEM] * (1 + len(bwd_parts)),
        out_specs=VMEM,
        scratch_shapes=[pltpu.VMEM((8 * num_vecs, 2 * cols), BF16)],
        compiler_params=pltpu.CompilerParams(vmem_limit_bytes=24 * 2**20),
        name="right",
    )(left, *bwd_parts.values())


def solution(mesh):
    in_specs = (
        P("gx", "gy", "gz", None, None, None),
        P("gx", "gy", "gz", None, None, None, None),
        P(),
        P(),
        P(None, "gx", "gy"),
        P(None, "gx", "gy"),
        P("gz", None),
    )
    out_specs = P("gz", None, "gx", "gy")
    return jax.shard_map(
        on_device, mesh=mesh, in_specs=in_specs, out_specs=out_specs, check_vma=False
    )
```

```python
import functools
import math

import jax
import jax.numpy as jnp
from jax import lax
from jax.experimental import pallas as pl
from jax.experimental.pallas import tpu as pltpu
from jax.sharding import PartitionSpec as P

VMEM = pl.BlockSpec(memory_space=pltpu.VMEM)
SMEM = pl.BlockSpec(memory_space=pltpu.SMEM)
BF16 = jnp.bfloat16
F32 = jnp.float32


def passed_along(value, axis, steps):
    count = lax.axis_size(axis)
    pairs = [(source, (source + steps) % count) for source in range(count)]
    return lax.ppermute(value, axis, pairs)


def mm(left, right):
    return jnp.dot(left, right, preferred_element_type=F32)


def parts_of(value, divisor):
    quotient = jnp.floor((value + 0.5) * (1.0 / divisor))
    return quotient, value - quotient * divisor


def whole_numbers(shape, axis):
    return lax.broadcasted_iota(jnp.int32, shape, axis).astype(F32)


def chosen(condition):
    return jnp.where(condition, 1.0, 0.0)


def coordinates(index, extent):
    rest, third = parts_of(index, extent[2])
    first, second = parts_of(rest, extent[1])
    return [first, second, third]


def source_columns(extent, e):
    count = math.prod(extent)
    face = count // extent[e]
    inner = count - face if e == 0 else count
    total = 6 * (inner + face)
    column = whole_numbers((1, total), 1)
    beyond = chosen(column >= 6 * inner)
    site, left = parts_of(column - beyond * (6 * inner), 6)
    colour, part = parts_of(left, 2)
    within = coordinates(site, extent)
    if e == 0:
        within[0] = within[0] + 1
    flat = [n for d, n in enumerate(extent) if d != e]
    outer, last = parts_of(site, flat[1])
    edge = [outer, last]
    edge.insert(e, jnp.full_like(site, extent[e]))
    where = [w + beyond * (o - w) for w, o in zip(within, edge)]
    return total, part, where, colour


def rows_kernel(extent, eig_ref, vec_out, *face_outs):
    vec = eig_ref[...].astype(F32).reshape(vec_out.shape)
    vec_out[...] = vec.astype(BF16)
    strides = (6 * extent[1] * extent[2], 6 * extent[2], 6)
    for e, out in enumerate(face_outs):
        begins = [0]
        for d in range(e):
            begins = [at + n * strides[d] for at in begins for n in range(extent[d])]
        runs = [vec[at : at + strides[e]] for at in begins]
        out[...] = (jnp.concatenate(runs, axis=0) if e else runs[0]).astype(BF16)


def pieces_kernel(z_ref, fwd_in, bwd_in, fwd_out, bwd_out, fwd_ref, bwd_ref, sems):
    pairs = ((fwd_in, fwd_ref), (bwd_in, bwd_ref))
    copies = [pltpu.make_async_copy(source, target, sems.at[n]) for n, (source, target) in enumerate(pairs)]
    for copy in copies:
        copy.start()
    rows, cols = fwd_ref.shape[1:]
    piece = fwd_out.shape[1]
    per_spin = rows // 4
    lane = cols // 4
    flat = lax.broadcasted_iota(jnp.int32, (piece, 1), 0) + z_ref[0] * piece
    spin = jnp.zeros_like(flat)
    for t in range(1, 4):
        spin += jnp.where(flat >= t * per_spin, 1, 0)
    source = 4 * (flat - spin * per_spin) + spin
    select = chosen(lax.broadcasted_iota(jnp.int32, (piece, rows), 1) == source).astype(BF16)
    column = lax.broadcasted_iota(jnp.int32, (1, cols), 1)
    spin = jnp.zeros_like(column)
    for t in range(1, 4):
        spin += jnp.where(column >= t * lane, 1, 0)
    source = 4 * (column - spin * lane) + spin
    perm = chosen(lax.broadcasted_iota(jnp.int32, (cols, cols), 0) == source).astype(BF16)
    copies[0].wait()
    for c in range(2):
        picked = mm(select, fwd_ref[c]).astype(BF16)
        fwd_out[c] = mm(picked, perm).astype(BF16)
    copies[1].wait()
    for c in range(2):
        bwd_out[c] = mm(select, bwd_ref[c]).astype(BF16)


def links_kernel(extent, link_ref, *outs):
    count = math.prod(extent)
    rows = 6 * count
    row = whole_numbers((rows, 1), 0)
    row_site, left = parts_of(row, 6)
    row_colour, row_part = parts_of(left, 2)
    row_where = coordinates(row_site, extent)
    link = link_ref[...]
    high = link.astype(BF16)
    rest = link - high.astype(F32)
    mid = rest.astype(BF16)
    low = (rest - mid.astype(F32)).astype(BF16)
    spread = chosen(row_site == whole_numbers((rows, count), 1)).astype(BF16)
    by_row = [mm(spread, part) for part in (high, mid, low)]
    by_row = [jnp.concatenate([part, part], axis=1) for part in by_row]

    def entry_of(entry):
        half = chosen(entry >= 54)
        direction, left = parts_of(entry - 54 * half, 18)
        part, left = parts_of(left, 9)
        into, out_of = parts_of(left, 3)
        return half, direction, part, into, out_of

    half, direction, _, into, _ = entry_of(whole_numbers((1, 108), 1))
    own_part = (half == row_part) & (into == row_colour)
    place_half, _, place_part, _, place_colour = entry_of(whole_numbers((108, 1), 0))
    for e, out in enumerate(outs):
        keep = chosen(own_part & (direction == e))
        picked = jnp.concatenate([part * keep for part in by_row], axis=0).astype(BF16)
        total, part, where, colour = source_columns(extent, e)
        sign = 1.0 - 2.0 * part * (1.0 - place_half)
        match = (place_colour == colour) & (jnp.abs(place_part - part) == place_half)
        placed = mm(picked, jnp.where(match, sign, 0.0).astype(BF16))
        same = None
        for d in range(3):
            hit = row_where[d] + (1.0 if d == e else 0.0) == where[d]
            same = hit if same is None else same & hit
        mask = chosen(same)
        for n in range(3):
            at = slice(n * rows, (n + 1) * rows)
            out[at, :] = (placed[at] * mask).astype(BF16)


def correlate_kernel(scale, vec_ref, face0, face1, face2, mat0, mat1, mat2, out_ref):
    gz_n, gx_n, split, depth, width = out_ref.shape
    each = 6 // split
    own_rows = depth // each
    vec = vec_ref[...]
    rows = vec.shape[0]
    row = lax.broadcasted_iota(jnp.int32, (rows, rows), 0)
    column = lax.broadcasted_iota(jnp.int32, (rows, rows), 1)
    odd = lax.rem(row, 2) == 1
    turn = jnp.where(odd & (column == row - 1), -1.0, chosen((column == row + 1) & ~odd)).astype(BF16)
    sources = [
        jnp.concatenate([vec[face0.shape[0] :], face0[...]], axis=0),
        jnp.concatenate([vec, face1[...]], axis=0),
        jnp.concatenate([vec, face2[...]], axis=0),
    ]
    for e, mat in enumerate((mat0, mat1, mat2)):
        terms = mm(mat[...], sources[e])
        moved = terms[:rows] + terms[rows : 2 * rows] + terms[2 * rows :]
        moved = moved.astype(BF16)
        turned = mm(turn, moved).astype(BF16)
        right = jnp.concatenate([moved, turned], axis=1)
        product = lax.dot_general(
            vec, right, (((0,), (0,)), ((), ())), preferred_element_type=F32
        )
        product = (product * scale).astype(BF16)
        for c in range(2):
            n = 2 * e + c
            half = product[:, c * width : (c + 1) * width]
            to = slice(n % each * own_rows, (n % each + 1) * own_rows)
            for g in range(gx_n):
                for z in range(gz_n):
                    at = (g * gz_n + z) * own_rows
                    out_ref[z, g, n // each, to] = half[at : at + own_rows]


def spin_groups(gz_n):
    keys = [(dy, dc) for dc in range(2) for dy in range(gz_n // 2)]
    if gz_n == 4:
        return [[key] for key in keys]
    return [[(dy, dc) for dc in range(2)] for dy in range(gz_n // 2)]


def rows_of(parts, c, count):
    rows = jnp.concatenate([part[:, c] for part in parts], axis=1)
    return rows.reshape(count, rows.shape[-1])


def right_kernel(gz_n, keys, left_ref, *refs):
    bwd_at = dict(zip(keys, refs))
    out_ref, b_ref = refs[len(keys) :]
    num_vecs = b_ref.shape[0] // 8
    op_count, _, row_count, width = out_ref.shape
    for t, group in enumerate(spin_groups(gz_n)):
        real, imag = [rows_of([bwd_at[key] for key in group], c, num_vecs) for c in range(2)]
        at = 2 * t * num_vecs
        b_ref[at : at + num_vecs, :width] = real
        b_ref[at : at + num_vecs, width:] = imag
        b_ref[at + num_vecs : at + 2 * num_vecs, :width] = -imag
        b_ref[at + num_vecs : at + 2 * num_vecs, width:] = real
    left = left_ref[...].reshape(op_count * row_count, 8 * num_vecs)
    block = min(width, 512)
    for c in range(2):
        for begin in range(0, width, block):
            at = c * width + begin
            result = mm(left, b_ref[:, at : at + block]).astype(BF16)
            out_ref[:, c, :, begin : begin + block] = result.reshape(op_count, row_count, block)


def left_kernel(inverse, plan, me_ref, dirs_ref, spin_ref, chain_ref, *refs):
    line, elem_keys, fwd_keys = plan
    elem_in, refs = refs[:2], refs[2:]
    fwd_in, refs = refs[: len(fwd_keys)], refs[len(fwd_keys) :]
    out_ref, elem_all, elem_ref, x_ref, p_ref = refs
    gx_n, gz_n, split, depth, num_vecs = elem_all.shape
    each = 6 // split
    own_rows = depth // each
    width = fwd_in[0].shape[3]
    op_count, row_count, _ = out_ref.shape
    vec_rows = row_count // 4
    gy_n = 4 * num_vecs // width
    lane = width // 4
    halves = gz_n // 4
    gx, gy, gz = me_ref[0], me_ref[1], me_ref[2]

    def back(at, step, count):
        return lax.rem(at - step + count, count)

    def gz_from(dy, dc):
        return back(lax.div(gz, 2), dy, gz_n // 2) * 2 + back(lax.rem(gz, 2), dc, 2)

    for dc, ref in enumerate(elem_in):
        for n, (dx, dy) in enumerate(elem_keys):
            for place, offset in enumerate(line):
                to = lax.bitwise_xor(gx, offset), gz_from(dy, dc), back(gy, dx, gy_n) if split > 1 else 0
                elem_all[to] = ref[n, place]
    column = lax.broadcasted_iota(jnp.int32, (1, num_vecs), 1)
    source = jnp.zeros_like(column)
    half_rows = vec_rows // halves
    for place, offset in enumerate(line):
        for half in range(halves):
            at = place * vec_rows + half * half_rows
            from_half = lax.bitwise_xor(lax.rem(gz, 2), half) if halves == 2 else half
            begin = lax.bitwise_xor(gx, offset) * vec_rows + from_half * half_rows
            inside = (column >= at) & (column < at + half_rows)
            source = jnp.where(inside, column + (begin - at), source)
    perm = chosen(lax.broadcasted_iota(jnp.int32, (num_vecs, num_vecs), 0) == source).astype(BF16)
    for n in range(6):
        rows = slice(n % each * own_rows, (n % each + 1) * own_rows)
        whole = elem_all[:, :, n // each, rows].reshape(num_vecs, num_vecs)
        elem_ref[n] = mm(whole, perm).astype(BF16)

    groups = spin_groups(gz_n)
    spins = [lax.div(gz_from(*group[0]), halves) for group in groups]

    first_row = pl.multiple_of(gx * vec_rows, vec_rows)

    def own(d, c):
        return elem_ref[2 * d + c, pl.ds(first_row, vec_rows), :]

    real_rows = [jnp.concatenate([own(d, 0), -own(d, 1)], axis=1) for d in range(3)]
    imag_rows = [jnp.concatenate([own(d, 1), own(d, 0)], axis=1) for d in range(3)]
    left = jnp.concatenate([part for d in range(3) for part in (real_rows[d], imag_rows[d])], axis=0)
    fwd_at = dict(zip(fwd_keys, fwd_in))
    for t, group in enumerate(groups):
        for dx in range(gy_n):
            parts = [fwd_at[(dx,) + key] for key in group]
            right = jnp.concatenate([rows_of(parts, c, num_vecs) for c in range(2)], axis=0)
            result = mm(left, right).astype(BF16)
            for d in range(3):
                for c in range(2):
                    at = (d * 2 + c) * vec_rows
                    x_ref[d, c, dx, t] = result[at : at + vec_rows]

    row = lax.broadcasted_iota(jnp.int32, (row_count, 1), 0)
    column = lax.broadcasted_iota(jnp.int32, (1, row_count), 1)
    row_spin = lax.rem(row, 4)
    diagonal = lax.div(row, 4) == lax.rem(column, vec_rows)
    column_spin = lax.div(column, vec_rows)
    blocks = [pl.multiple_of(back(gy, dx, gy_n) * lane, lane) for dx in range(gy_n)]

    def one_operator(op):
        a = chain_ref[2 * op]
        b = chain_ref[2 * op + 1]
        dir_a = dirs_ref[a]
        dir_b = dirs_ref[b]
        mix = None
        for t in range(4):
            weight = jnp.full((row_count, 1), spin_ref[a, 0, spins[t]])
            for s in range(1, 4):
                weight = jnp.where(row_spin == s, spin_ref[a, s, spins[t]], weight)
            mix = weight if mix is None else jnp.where(column_spin == t, weight, mix)
        mix = jnp.where(diagonal, mix, 0.0)
        high = mix.astype(BF16)
        low = (mix - high.astype(F32)).astype(BF16)
        mix = jnp.concatenate([high, low], axis=0)
        for c in range(2):
            for dx in range(gy_n):
                source = x_ref[dir_a, c, dx].reshape(row_count, width)
                both = mm(mix, source)
                result = (both[:row_count] + both[row_count:]).astype(BF16)
                for s in range(4):
                    to = c * num_vecs + dx * lane
                    p_ref[s, :, to : to + lane] = result[:, s * lane : (s + 1) * lane]

        def elem(c):
            return jnp.concatenate([elem_ref[2 * dir_b + c, pl.ds(at, lane), :] for at in blocks], axis=0)

        real_b, imag_b = elem(0), elem(1)
        right = jnp.concatenate(
            [
                jnp.concatenate([real_b, imag_b], axis=1),
                jnp.concatenate([-imag_b, real_b], axis=1),
            ],
            axis=0,
        )
        product = mm(p_ref[...].reshape(4 * row_count, 2 * num_vecs), right)
        parts = [product[s * row_count : (s + 1) * row_count] for s in range(4)]
        for t in range(4):
            total = parts[0] * (spin_ref[b, 0, spins[t]] * inverse)
            for s in range(1, 4):
                total += parts[s] * (spin_ref[b, s, spins[t]] * inverse)
            total = total.astype(BF16)
            out_ref[op, :, 2 * t * num_vecs : 2 * (t + 1) * num_vecs] = total

    for op in range(op_count):
        one_operator(op)


def passed_in_gz(value, dy, dc):
    count = lax.axis_size("gz")
    chips = count // 2
    pairs = [(n, ((n // 2 + dy) % chips) * 2 + (n + dc) % 2) for n in range(count)]
    return lax.ppermute(value, "gz", pairs)


def passed_in_plane(value, dx, dy):
    if not dx and not dy:
        return value
    gy_n, gz_n = lax.axis_size("gy"), lax.axis_size("gz")
    chips = gz_n // 2
    pairs = []
    for y in range(gy_n):
        for z in range(gz_n):
            to = (y + dx) % gy_n * gz_n + ((z // 2 + dy) % chips) * 2 + z % 2
            pairs.append((y * gz_n + z, to))
    return lax.ppermute(value, ("gy", "gz"), pairs)


def line_exchange(value, axis, distance, steps, offsets=(0,)):
    count = lax.axis_size(axis)
    gathered = value if len(offsets) > 1 else value[None]
    offsets = list(offsets)
    for _ in range(steps):
        pairs = [(n, n ^ distance) for n in range(count)]
        gathered = jnp.concatenate([gathered, lax.ppermute(gathered, axis, pairs)])
        offsets += [offset ^ distance for offset in offsets]
        distance //= 2
    return gathered, tuple(offsets)


def part_at(value, index, axis=0):
    return lax.dynamic_index_in_dim(value, index, axis, keepdims=False)


def added(*values):
    return sum(value.astype(F32) for value in values).astype(BF16)


def on_device(eigvecs, links, directions, spin_mats, forward_peram, backward_peram, chain_order):
    extent = eigvecs.shape[:3]
    num_vecs = eigvecs.shape[-1]
    gx_n, gy_n, gz_n = (lax.axis_size(name) for name in ("gx", "gy", "gz"))
    chips = gz_n // 2
    gx, gy, gz = (lax.axis_index(name).astype(jnp.int32) for name in ("gx", "gy", "gz"))
    me = jnp.stack([gx, gy, gz])
    chip, core = lax.div(gz, 2), lax.rem(gz, 2)

    rows, cols = forward_peram.shape[1:]
    piece = rows // gz_n
    site_rows = 6 * math.prod(extent)
    face_rows = [site_rows // n for n in extent]
    vec, *faces = pl.pallas_call(
        functools.partial(rows_kernel, extent),
        out_shape=[jax.ShapeDtypeStruct((n, num_vecs), BF16) for n in [site_rows] + face_rows],
        in_specs=[VMEM],
        out_specs=[VMEM] * 4,
        compiler_params=pltpu.CompilerParams(vmem_limit_bytes=24 * 2**20),
        name="rows",
    )(eigvecs.transpose(0, 1, 2, 4, 3, 5).reshape(-1, 2, num_vecs))
    faces = [passed_along(face, axis, -1) for face, axis in zip(faces, ("gx", "gy", "gz"))]

    piece_shape = jax.ShapeDtypeStruct((2, piece, cols), BF16)
    fwd_piece, bwd_piece = pl.pallas_call(
        pieces_kernel,
        out_shape=[piece_shape] * 2,
        in_specs=[SMEM] + [pl.BlockSpec(memory_space=pl.ANY)] * 2,
        out_specs=[VMEM] * 2,
        scratch_shapes=[
            pltpu.VMEM(forward_peram.shape, BF16),
            pltpu.VMEM(backward_peram.shape, BF16),
            pltpu.SemaphoreType.DMA((2,)),
        ],
        compiler_params=pltpu.CompilerParams(vmem_limit_bytes=60 * 2**20),
        cost_estimate=pl.CostEstimate(flops=10**8, bytes_accessed=10**7, transcendentals=0),
        name="pieces",
    )(me[2:], forward_peram, backward_peram)
    fwd_piece, links = lax.optimization_barrier((fwd_piece, links))
    fwd_half = lax.ppermute(fwd_piece, "gx", [(n, n ^ (gx_n // 2)) for n in range(gx_n)])

    link_mats = pl.pallas_call(
        functools.partial(links_kernel, extent),
        out_shape=[
            jax.ShapeDtypeStruct((3 * site_rows, site_rows - (0 if e else face_rows[0]) + face_rows[e]), BF16)
            for e in range(3)
        ],
        in_specs=[VMEM],
        out_specs=[VMEM] * 3,
        compiler_params=pltpu.CompilerParams(vmem_limit_bytes=24 * 2**20),
        name="link_matrices",
    )(links.reshape(-1, 54))

    volume = math.prod(extent) * gx_n * gy_n * gz_n
    own_rows = num_vecs // (gz_n * gx_n)
    split = gy_n if 6 % gy_n == 0 and own_rows % 16 == 0 else 1
    depth = 6 * own_rows // split
    partial = pl.pallas_call(
        functools.partial(correlate_kernel, 1.0 / math.sqrt(12.0 * volume)),
        out_shape=jax.ShapeDtypeStruct((gz_n, gx_n, split, depth, num_vecs), BF16),
        in_specs=[VMEM] * 7,
        out_specs=VMEM,
        compiler_params=pltpu.CompilerParams(vmem_limit_bytes=24 * 2**20),
        name="correlate",
    )(vec, *faces, *link_mats)

    partial, fwd_half = lax.optimization_barrier((partial, fwd_half))
    by_core = partial.reshape((chips, 2) + partial.shape[1:])
    summed = added(part_at(by_core, core, 1), passed_in_gz(part_at(by_core, 1 - core, 1), 0, 1))
    rounds = gx_n.bit_length() - 1
    fwd_line = jnp.stack([fwd_piece, fwd_half])
    fwd_line, line = line_exchange(fwd_line, "gx", gx_n // 4, rounds - 1, (0, gx_n // 2))
    plane = [(dx, dy) for dy in range(chips) for dx in range(gy_n)]

    def plane_part(dx, dy):
        part = part_at(summed, lax.rem(chip + dy, chips))
        return part_at(part, lax.rem(gy + dx, gy_n) if split > 1 else 0, 1)

    summed = added(*[passed_in_plane(plane_part(dx, dy), dx, dy) for dx, dy in plane])
    summed, fwd_line, bwd_piece = lax.optimization_barrier((summed, fwd_line, bwd_piece))
    bwd_line, _ = line_exchange(bwd_piece, "gx", gx_n // 2, rounds)

    four = gy_n == 2 and chips == 2
    fwd_parts = {(dx, dy, 0): passed_in_plane(fwd_line, dx, dy) for dx, dy in plane if not (four and dx and dy)}

    distance = gx_n // 2
    while distance:
        halves = summed.reshape((2, distance) + summed.shape[1:])
        bit = lax.rem(lax.div(gx, distance), 2)
        pairs = [(n, n ^ distance) for n in range(gx_n)]
        summed = added(part_at(halves, bit), lax.ppermute(part_at(halves, 1 - bit), "gx", pairs))
        distance //= 2
    elem_line, offsets = line_exchange(summed[0], "gx", gx_n // 2, rounds - 1)
    fwd_parts[0, 0, 1] = passed_in_gz(fwd_line, 0, 1)
    order = chain_order.reshape(-1)
    if four:
        keys = [(1, 0, 0), (0, 1, 0), (0, 0, 1)]
        tied = (elem_line, bwd_line, order, *[fwd_parts[key] for key in keys])
        elem_line, bwd_line, order, *parts = lax.optimization_barrier(tied)
        fwd_parts.update(zip(keys, parts))
        fwd_parts[1, 1, 0] = passed_in_plane(fwd_parts[0, 1, 0], 1, 0)
    bwd_parts = {(dy, 0): passed_in_gz(bwd_line, dy, 0) if dy else bwd_line for dy in range(chips)}
    elem_line, _ = line_exchange(elem_line, "gx", 1, 1, offsets)
    elem_keys = plane if split > 1 else [(0, dy) for dy in range(chips)]
    elem_own = jnp.stack([passed_in_plane(elem_line, dx, dy) for dx, dy in elem_keys])
    late = [(1, 1, 0)] if four else []
    elem_own, *parts = lax.optimization_barrier((elem_own, *[fwd_parts[key] for key in late], *bwd_parts.values()))
    fwd_parts.update(zip(late, parts))
    bwd_parts.update(zip(list(bwd_parts), parts[len(late) :]))
    elem_parts = [elem_own, passed_in_gz(elem_own, 0, 1)]
    for dx, dy in plane[1:]:
        fwd_parts[dx, dy, 1] = passed_in_gz(fwd_parts[dx, dy, 0], 0, 1)
    for dy in range(chips):
        bwd_parts[dy, 1] = passed_in_gz(bwd_parts[dy, 0], 0, 1)

    op_count = chain_order.shape[0]
    plan = (line, tuple(elem_keys), tuple(fwd_parts))
    left_shape = (op_count, rows, 8 * num_vecs)
    left = pl.pallas_call(
        functools.partial(left_kernel, 1.0 / math.sqrt(4 * num_vecs), plan),
        out_shape=jax.ShapeDtypeStruct(left_shape, BF16),
        in_specs=[SMEM] * 4 + [VMEM] * (len(elem_parts) + len(fwd_parts)),
        out_specs=VMEM,
        scratch_shapes=[
            pltpu.VMEM((gx_n, gz_n, split, depth, num_vecs), BF16),
            pltpu.VMEM((6, num_vecs, num_vecs), BF16),
            pltpu.VMEM((3, 2, gy_n, 4, rows // 4, cols), BF16),
            pltpu.VMEM((4, rows, 2 * num_vecs), BF16),
        ],
        compiler_params=pltpu.CompilerParams(vmem_limit_bytes=24 * 2**20),
        cost_estimate=pl.CostEstimate(flops=8 * 10**9, bytes_accessed=10**7, transcendentals=0),
        name="left",
    )(me, directions, spin_mats, order, *elem_parts, *fwd_parts.values())
    return pl.pallas_call(
        functools.partial(right_kernel, gz_n, tuple(bwd_parts)),
        out_shape=jax.ShapeDtypeStruct((op_count, 2, rows, cols), BF16),
        in_specs=[VMEM] * (1 + len(bwd_parts)),
        out_specs=VMEM,
        scratch_shapes=[pltpu.VMEM((8 * num_vecs, 2 * cols), BF16)],
        compiler_params=pltpu.CompilerParams(vmem_limit_bytes=24 * 2**20),
        name="right",
    )(left, *bwd_parts.values())


def solution(mesh):
    in_specs = (
        P("gx", "gy", "gz", None, None, None),
        P("gx", "gy", "gz", None, None, None, None),
        P(),
        P(),
        P(None, "gx", "gy"),
        P(None, "gx", "gy"),
        P("gz", None),
    )
    out_specs = P("gz", None, "gx", "gy")
    return jax.shard_map(
        on_device, mesh=mesh, in_specs=in_specs, out_specs=out_specs, check_vma=False
    )
```
